32 devices in a mesh: dp: 8 (over y, x, core), mp: 4 (over z).
Axes of the slice: x: 2, y: 2, z: 4, core: 2. Of those that a mesh axis runs over, the one named last changes fastest.
Arguments:
- tokens: bfloat16 [16384, 768], P('dp'), may hold values from -6 to 6
- lengths: int32 [8, 16], P('dp'), may hold values from 1 to 1024, 2048 in all within a row
- first_gain: bfloat16 [768], P('dp'), may hold values from 0.5 to 1.5
- first_shift: bfloat16 [768], P('dp'), may hold values from -1.25 to 1.25
- qkv_weight: bfloat16 [3, 768, 768], P(None, 'dp', 'mp'), may hold values from -0.21875 to 0.21875
- qv_bias: bfloat16 [2, 4, 192], P(None, 'mp', 'dp'), may hold values from -1.25 to 1.25
- proj_weight: bfloat16 [768, 768], P('mp', 'dp'), may hold values from -0.875 to 0.875
- proj_bias: bfloat16 [768], P('dp'), may hold values from -1.25 to 1.25
- second_gain: bfloat16 [768], P('dp'), may hold values from 0.5 to 1.5
- second_shift: bfloat16 [768], P('dp'), may hold values from -1.25 to 1.25
- fc_weight: bfloat16 [768, 3072], P('dp', 'mp'), may hold values from -0.21875 to 0.21875
- fc_bias: bfloat16 [4, 768], P('mp', 'dp'), may hold values from -1.25 to 1.25
- out_weight: bfloat16 [3072, 768], P('mp', 'dp'), may hold values from -0.15625 to 0.15625
- out_bias: bfloat16 [768], P('dp'), may hold values from -1.25 to 1.25
- out_grad: bfloat16 [16384, 768], P('dp'), may hold values from -6 to 6
Outputs:
- output: bfloat16 [16384, 768], P('dp')
- grad_tokens: bfloat16 [16384, 768], P('dp')
- grad_first_gain: float32 [768], P('dp')
- grad_first_shift: float32 [768], P('dp')
- grad_qkv_weight: float32 [3, 768, 768], P(None, 'dp', 'mp')
- grad_qv_bias: float32 [2, 4, 192], P(None, 'mp', 'dp')
- grad_proj_weight: float32 [768, 768], P('mp', 'dp')
- grad_proj_bias: float32 [768], P('dp')
- grad_second_gain: float32 [768], P('dp')
- grad_second_shift: float32 [768], P('dp')
- grad_fc_weight: float32 [768, 3072], P('dp', 'mp')
- grad_fc_bias: float32 [4, 768], P('mp', 'dp')
- grad_out_weight: float32 [3072, 768], P('mp', 'dp')
- grad_out_bias: float32 [768], P('dp')
The draws below stay inside these ranges and needn't reach their ends.
Inputs may be any that keep to these rules, and one draw needn't show every extreme that they name: `lengths`: each row sums to 2048 and its largest entry is 1024.
All inputs are finite; a program needn't handle non-finite values.
Results may differ from the reference program's by a relative error of at most 0.018.
Values may be sent and summed in bfloat16 or wider, within the bound.
A program may use at most 128 MiB of HBM per device.

```python
import math
import jax
import jax.numpy as jnp
import numpy as np
from jax import lax

D = 768
HEADS = 12
HD = 64
FF = 3072
MAXLEN = 1024
TOK_DEV = 2048
NSEQ = 16
TOKENS = 16384
N_DP = 8
N_MP = 4


def shard_levels(stream_key, shape, cuts, smallest, top_value):
    loudness = 1.0
    for dim, shards_of in cuts:
        draws = jax.random.uniform(jax.random.fold_in(jax.random.fold_in(stream_key, 6), dim), (shards_of,), jnp.float32, smallest / len(cuts), top_value / len(cuts))
        loudness = loudness * jnp.repeat(jnp.exp(draws), shape[dim] // shards_of).reshape((-1,) + (1,) * (len(shape) - 1 - dim))
    return loudness


def split_up(amount, total, limit, skew):
    weights = [(1 << 20) // math.isqrt(standing ** skew) + 1 for standing in range(2, amount + 1)]
    spare, given = total - limit - (amount - 1), [1] * (amount - 1)
    while spare > 0:
        free = [i for i in range(amount - 1) if given[i] < limit]
        mass, remaining = sum([weights[i] for i in free]), spare
        for i in free:
            extra = min(limit - given[i], max(1, remaining * weights[i] // mass), spare)
            given[i] = given[i] + extra
            spare = spare - extra
    return np.array([limit] + given)


def ragged_sizes(key, amount, total, bound, slope):
    if amount == 2:
        one = jax.random.randint(key, (), max(1, total - bound), min(bound, total - 1) + 1)
        return jnp.stack([one, total - one])
    sizes = jnp.asarray(split_up(amount, total, bound, slope), jnp.int32)
    pairs = (amount - 1) // 2
    source_of, taker = sizes[1:1 + 2 * pairs:2], sizes[2:2 + 2 * pairs:2]
    room = jnp.minimum(source_of - 1, bound - taker)
    passed = jax.random.randint(jax.random.fold_in(key, 1), (pairs,), 0, 1 << 20) % (room + 1)
    sizes = sizes.at[1:1 + 2 * pairs:2].set(source_of - passed).at[2:2 + 2 * pairs:2].set(taker + passed)
    return sizes[jax.random.permutation(jax.random.fold_in(key, 2), amount)]


def scatter_about(stream_key, extent, scale, reach, pieces=(), held_as=jnp.bfloat16):
    level = shard_levels(stream_key, extent, pieces, -0.22, 0.18) if pieces else 1.0
    array = jax.random.normal(stream_key, extent, jnp.float32) * scale * level
    return jnp.minimum(jnp.maximum(array, -reach), reach).astype(held_as)


def setup_inputs(seed: int = 0) -> dict:
    seeds = jax.random.split(jax.random.key(seed), 16)
    return {
        "tokens": scatter_about(seeds[0], (TOKENS, D), 1.0, 6.0, ((0, 8),)),
        "lengths": jax.vmap(lambda own: ragged_sizes(own, NSEQ, TOK_DEV, MAXLEN, 2))(jax.random.split(seeds[1], N_DP)).reshape((N_DP, NSEQ)).astype(jnp.int32),
        "first_gain": jnp.clip(1.0 + 0.1 * jax.random.normal(seeds[2], (D,), jnp.float32), 0.5, 1.5).astype(jnp.bfloat16),
        "first_shift": scatter_about(seeds[3], (D,), 0.2, 1.25, ((0, 8),)),
        "qkv_weight": scatter_about(seeds[4], (3, D, D), D ** -0.5, 0.21875, ((1, 8), (2, 4))),
        "qv_bias": scatter_about(seeds[5], (2, N_MP, D // N_MP), 0.2, 1.25, ((1, 4), (2, 8))),
        "proj_weight": scatter_about(seeds[6], (D, D), (D // 16) ** -0.5, 0.875, ((0, 4), (1, 8))),
        "proj_bias": scatter_about(seeds[7], (D,), 0.2, 1.25, ((0, 8),)),
        "second_gain": jnp.clip(1.0 + 0.1 * jax.random.normal(seeds[8], (D,), jnp.float32), 0.5, 1.5).astype(jnp.bfloat16),
        "second_shift": scatter_about(seeds[9], (D,), 0.2, 1.25, ((0, 8),)),
        "fc_weight": scatter_about(seeds[10], (D, FF), D ** -0.5, 0.21875, ((0, 8), (1, 4))),
        "fc_bias": scatter_about(seeds[11], (N_MP, FF // N_MP), 0.2, 1.25, ((0, 4), (1, 8))),
        "out_weight": scatter_about(seeds[12], (FF, D), (FF // 2) ** -0.5, 0.15625, ((0, 4), (1, 8))),
        "out_bias": scatter_about(seeds[13], (D,), 0.2, 1.25, ((0, 8),)),
        "out_grad": scatter_about(seeds[14], (TOKENS, D), 1.0, 6.0, ((0, 8),)),
    }


@jax.custom_vjp
def low(v):
    return lax.optimization_barrier(v.astype(jnp.bfloat16)).astype(jnp.float32)

@jax.custom_vjp
def low_back(v):
    return v

def low_keep(v):
    return (low(v), None)

def low_pass(kept, grad):
    return (grad,)

def back_keep(v):
    return (v, None)

def back_low(kept, grad):
    return (low(grad),)
low.defvjp(low_keep, low_pass)
low_back.defvjp(back_keep, back_low)
EPS = 1e-05
SCALE = 0.125
NEG = -1e+30
GELU_C = 0.7978845608028654
HIGH = lax.Precision.HIGHEST

def matmul(left, right):
    return jnp.dot(left, right, precision=HIGH, preferred_element_type=jnp.float32)

def layer_norm(values, gain, shift):
    mean = lax.optimization_barrier(jnp.mean(values, axis=-1, keepdims=True))
    centred = values - mean
    spread = lax.optimization_barrier(jnp.mean(centred * centred, axis=-1, keepdims=True))
    return centred * lax.rsqrt(spread + EPS) * gain + shift

def gelu_tanh(values):
    return 0.5 * values * (1.0 + jnp.tanh(GELU_C * (values + 0.044715 * values * values * values)))

def segment_ids(lengths_row, count):
    ends = jnp.cumsum(lengths_row.astype(jnp.int32))
    places = jnp.arange(count, dtype=jnp.int32)
    return lax.optimization_barrier(jnp.sum((places[:, None] >= ends[None, :]).astype(jnp.int32), axis=1)).astype(jnp.int32)

def both_ways(v):
    return low_back(low(v))

def shard_attention(items):
    query, keys, values, seg = items
    places = jnp.arange(seg.shape[0], dtype=jnp.int32)
    allowed = (seg[:, None] == seg[None, :]) & (places[None, :] <= places[:, None])
    scores = low_back(jnp.einsum('qhd,khd->hqk', query, keys, precision=HIGH) * SCALE)
    masked = jnp.where(allowed[None], scores, NEG)
    biggest = lax.optimization_barrier(jnp.max(masked, axis=-1, keepdims=True))
    expo = jnp.exp(masked - biggest)
    probs = expo / lax.optimization_barrier(jnp.sum(expo, axis=-1, keepdims=True))
    return jnp.einsum('hqk,khd->qhd', low(probs), values, precision=HIGH)

def reference(tokens, lengths, first_gain, first_shift, qkv_weight, qv_bias, proj_weight, proj_bias, second_gain, second_shift, fc_weight, fc_bias, out_weight, out_bias, out_grad):
    seg = jax.vmap(lambda row: segment_ids(row, TOK_DEV))(lengths)

    def forward(xin, gain_one, shift_one, qkv_all, qv_all, proj_all, proj_bias_all, gain_two, shift_two, fc_all, fc_bias_all, out_all, out_bias_all):
        act_one = low(layer_norm(xin, gain_one, shift_one))
        biases = qv_all.reshape(2, D)
        query = both_ways(matmul(act_one, qkv_all[0]) + biases[0])
        keys = both_ways(matmul(act_one, qkv_all[1]))
        values = both_ways(matmul(act_one, qkv_all[2]) + biases[1])
        shaped = (N_DP, TOK_DEV, HEADS, HD)
        rows = lax.map(jax.checkpoint(shard_attention), (query.reshape(shaped), keys.reshape(shaped), values.reshape(shaped), seg))
        attn_rows = both_ways(rows.reshape(N_DP * TOK_DEV, D))
        hidden_one = xin + low_back(matmul(attn_rows, proj_all) + proj_bias_all)
        act_two = low(layer_norm(hidden_one, gain_two, shift_two))
        pre = low_back(matmul(act_two, fc_all) + fc_bias_all.reshape(FF))
        fired = low(gelu_tanh(pre))
        return hidden_one + low_back(matmul(fired, out_all) + out_bias_all)
    params = (first_gain, first_shift, qkv_weight, qv_bias, proj_weight, proj_bias, second_gain, second_shift, fc_weight, fc_bias, out_weight, out_bias)
    params = tuple((item.astype(jnp.float32) for item in params))
    result, pullback = jax.vjp(forward, tokens.astype(jnp.float32), *params)
    grads = pullback(out_grad.astype(jnp.float32))
    return (result.astype(jnp.bfloat16), grads[0].astype(jnp.bfloat16), grads[1], grads[2], grads[3], grads[4], grads[5], grads[6], grads[7], grads[8], grads[9], grads[10], grads[11], grads[12])
```

```python
import functools

import jax
import jax.numpy as jnp
from jax import lax
from jax.experimental import pallas as pl
from jax.experimental.pallas import tpu as pltpu
from jax.sharding import PartitionSpec as P

HD = 64
HPD = 3
WIDE = 256
MAXLEN = 1024
QB = 256
BAND = MAXLEN // QB


EPS = 1e-05
SCALE = 0.125
NEG = -1e30
GELU_C = 0.7978845608028654
NN = (((1,), (0,)), ((), ()))
NT = (((1,), (1,)), ((), ()))
TN = (((0,), (0,)), ((), ()))
f32 = jnp.float32
bf16 = jnp.bfloat16


def mm(left, right, dims=NN):
    return lax.dot_general(left, right, dims, preferred_element_type=f32)


def split_up(shard, dim, size):
    before, after = (shard.shape[:dim], shard.shape[dim + 1 :])
    return jnp.moveaxis(shard.reshape(*before, size, -1, *after), dim, 0)


def summed_on_arrival(shard, axis, dim):
    size = lax.axis_size(axis)
    pieces = lax.all_to_all(split_up(shard, dim, size), axis, 0, 0, tiled=True)
    return jnp.sum(pieces.astype(jnp.float32), axis=0)


def norm_parts(values):
    mean = jnp.mean(values, axis=-1, keepdims=True)
    centred = values - mean
    inverse = lax.rsqrt(jnp.mean(centred * centred, axis=-1, keepdims=True) + EPS)
    return (centred * inverse, inverse)


def norm_back(grad, gain, normed, inverse):
    scaled = grad * gain
    return inverse * (
        scaled
        - jnp.mean(scaled, axis=-1, keepdims=True)
        - normed * jnp.mean(scaled * normed, axis=-1, keepdims=True)
    )


def gelu_tanh(values):
    return 0.5 * values * (1.0 + jnp.tanh(GELU_C * (values + 0.044715 * values * values * values)))


def gelu_slope(values):
    inner = GELU_C * (values + 0.044715 * values * values * values)
    tangent = jnp.tanh(inner)
    return 0.5 * (1.0 + tangent) + 0.5 * values * (1.0 - tangent * tangent) * GELU_C * (
        1.0 + 3.0 * 0.044715 * values * values
    )


def segment_starts(lengths_row, count):
    ends = jnp.cumsum(lengths_row)
    places = jnp.arange(count, dtype=jnp.int32)
    return jnp.max(jnp.where(ends[None, :] <= places[:, None], ends[None, :], 0), axis=1)[None, :]


def rows_of(index, size=QB):
    return pl.ds(pl.multiple_of(index * size, size), size)


def tile_heads(x):
    return jnp.concatenate([x] * HPD, axis=1)


def allowed_keys(i, j, start_ref):
    start = start_ref[:, rows_of(i)]
    key = lax.broadcasted_iota(jnp.int32, (QB, QB), 0)
    query = lax.broadcasted_iota(jnp.int32, (QB, QB), 1)
    return (key >= start - j * QB) & (key <= query + (i - j) * QB)


def stack_heads(x):
    lane = lax.broadcasted_iota(jnp.int32, x.shape, 1)
    return jnp.concatenate(
        [
            jnp.where((lane >= HD * h) & (lane < HD * h + HD), x, jnp.zeros_like(x))
            for h in range(HPD)
        ],
        axis=0,
    )


def attend_block(i, q_ref, k_ref, vt_ref, start_ref, lse_ref, o_ref, qs, acc):
    rows = rows_of(i)
    qs[...] = stack_heads(q_ref[rows])
    acc[...] = jnp.zeros_like(acc)

    def step(jj, carry):
        biggest, total = carry
        j = i - jj
        keys = rows_of(j)
        s = mm(k_ref[keys], qs[...], NT)
        s = jnp.where(tile_heads(allowed_keys(i, j, start_ref)), s, NEG)
        new = jnp.maximum(biggest, jnp.max(s, axis=0, keepdims=True))
        p = jnp.exp(s - new)
        shrink = jnp.exp(biggest - new)
        total = total * shrink + jnp.sum(p, axis=0, keepdims=True)
        p = p.astype(bf16)
        for h in range(HPD):
            cols = slice(QB * h, QB * h + QB)
            acc[:, cols] = acc[:, cols] * shrink[:, cols] + mm(
                vt_ref[HD * h : HD * h + HD, keys], p[:, cols]
            )
        return new, total

    biggest, total = lax.fori_loop(
        0,
        jnp.minimum(i, BAND) + 1,
        step,
        (jnp.full((1, HPD * QB), NEG, f32), jnp.zeros((1, HPD * QB), f32)),
    )
    lse_ref[i] = biggest + jnp.log(total)
    inverse = 1.0 / total
    out = jnp.concatenate(
        [acc[:, QB * h : QB * h + QB] * inverse[:, QB * h : QB * h + QB] for h in range(HPD)]
        + [jnp.zeros((WIDE - HPD * HD, QB), f32)],
        axis=0,
    )
    o_ref[rows] = out.T.astype(bf16)


def attend_block_back(i, grad, q_ref, k_ref, v_ref, kt_ref, o_ref, start_ref, lse_ref, dk, dv, qs, gs, dqt):
    rows = rows_of(i)
    qs[...] = stack_heads(q_ref[rows])
    gs[...] = stack_heads(grad)
    both = (grad.astype(f32) * o_ref[rows].astype(f32)).T
    delta = jnp.concatenate(
        [jnp.sum(both[HD * h : HD * h + HD], axis=0, keepdims=True) for h in range(HPD)], axis=1
    )
    lse = lse_ref[i]
    dqt[...] = jnp.zeros_like(dqt)

    def step(jj, _):
        j = i - jj
        keys = rows_of(j)
        s = mm(k_ref[keys], qs[...], NT)
        s = jnp.where(tile_heads(allowed_keys(i, j, start_ref)), s, NEG)
        p = jnp.exp(s - lse)
        dp = mm(v_ref[keys], gs[...], NT)
        ds = (p * (dp - delta)).astype(bf16)
        p = p.astype(bf16)
        dv[keys] += mm(p, gs[...])
        dk[keys] += mm(ds, qs[...])
        for h in range(HPD):
            dqt[HD * h : HD * h + HD] += mm(
                kt_ref[HD * h : HD * h + HD, keys], ds[:, QB * h : QB * h + QB]
            )
        return 0

    lax.fori_loop(0, jnp.minimum(i, BAND) + 1, step, 0)


def forward_kernel(q_ref, k_ref, v_ref, start_ref, o_ref, lse_ref, vt, qs, acc):
    blocks = q_ref.shape[0] // QB

    def turn(i, _):
        vt[:, rows_of(i)] = v_ref[rows_of(i)].T
        return 0

    lax.fori_loop(0, blocks, turn, 0)

    def block(i, _):
        attend_block(i, q_ref, k_ref, vt, start_ref, lse_ref, o_ref, qs, acc)
        return 0

    lax.fori_loop(0, blocks, block, 0)


def backward_kernel(
    q_ref, k_ref, v_ref, o_ref, g_ref, start_ref, lse_ref, d_ref, kt, qs, gs, dqt, dk, dv
):
    blocks = q_ref.shape[0] // QB

    def turn(i, _):
        kt[:, rows_of(i)] = k_ref[rows_of(i)].T
        return 0

    lax.fori_loop(0, blocks, turn, 0)
    dk[...] = jnp.zeros_like(dk)
    dv[...] = jnp.zeros_like(dv)

    def block(turn_of, _):
        i = blocks - 1 - turn_of
        rows = rows_of(i)
        attend_block_back(
            i, g_ref[rows], q_ref, k_ref, v_ref, kt, o_ref, start_ref, lse_ref, dk, dv, qs, gs, dqt
        )
        d_ref[0, rows] = (dqt[...].T * SCALE).astype(bf16)
        d_ref[1, rows] = dk[rows].astype(bf16)
        d_ref[2, rows] = dv[rows].astype(bf16)
        return 0

    lax.fori_loop(0, blocks, block, 0)


VMEM = pl.BlockSpec(memory_space=pltpu.VMEM)
LIMIT = pltpu.CompilerParams(vmem_limit_bytes=40 * 2**20)


def attend_forward(query, keys, values, starts):
    count = query.shape[0]
    return pl.pallas_call(
        forward_kernel,
        out_shape=(
            jax.ShapeDtypeStruct((count, WIDE), bf16),
            jax.ShapeDtypeStruct((count // QB, 1, HPD * QB), f32),
        ),
        in_specs=[VMEM] * 4,
        out_specs=(VMEM, VMEM),
        scratch_shapes=[
            pltpu.VMEM((WIDE, count), bf16),
            pltpu.VMEM((HPD * QB, WIDE), bf16),
            pltpu.VMEM((HD, HPD * QB), f32),
        ],
        compiler_params=LIMIT,
    )(query, keys, values, starts)


def attend_backward(query, keys, values, rows, grad, starts, lse):
    count = query.shape[0]
    return pl.pallas_call(
        backward_kernel,
        out_shape=jax.ShapeDtypeStruct((3, count, WIDE), bf16),
        in_specs=[VMEM] * 7,
        out_specs=VMEM,
        scratch_shapes=[
            pltpu.VMEM((WIDE, count), bf16),
            pltpu.VMEM((HPD * QB, WIDE), bf16),
            pltpu.VMEM((HPD * QB, WIDE), bf16),
            pltpu.VMEM((WIDE, QB), f32),
            pltpu.VMEM((count, WIDE), f32),
            pltpu.VMEM((count, WIDE), f32),
        ],
        compiler_params=LIMIT,
    )(query, keys, values, rows, grad, starts, lse)


def per_device(
    tokens,
    lengths,
    first_gain,
    first_shift,
    qkv_weight,
    qv_bias,
    proj_weight,
    proj_bias,
    second_gain,
    second_shift,
    fc_weight,
    fc_bias,
    out_weight,
    out_bias,
    out_grad,
):
    count = tokens.shape[0]
    starts = segment_starts(lengths[0], count)
    gain_one, shift_one, qkv_all, qv_all, proj_all, proj_bias_all = (
        lax.all_gather(first_gain, "dp", axis=0, tiled=True),
        lax.all_gather(first_shift, "dp", axis=0, tiled=True),
        lax.all_gather(qkv_weight, "dp", axis=1, tiled=True),
        lax.all_gather(qv_bias, "dp", axis=2, tiled=True),
        lax.all_gather(proj_weight, "dp", axis=1, tiled=True),
        lax.all_gather(proj_bias, "dp", axis=0, tiled=True),
    )
    gain_one_f = gain_one.astype(jnp.float32)
    xin = tokens.astype(jnp.float32)
    normed_one, inverse_one = norm_parts(xin)
    act_one = (normed_one * gain_one_f + shift_one.astype(jnp.float32)).astype(jnp.bfloat16)
    projected = jnp.einsum("td,cde->cte", act_one, qkv_all, preferred_element_type=jnp.float32)
    width = qkv_all.shape[2]
    wide = ((0, 0), (0, WIDE - width))
    query = jnp.pad(
        (projected[0] + qv_all[0, 0].astype(f32)).astype(bf16) * jnp.asarray(SCALE, bf16), wide
    )
    keys = jnp.pad(projected[1].astype(bf16), wide)
    values = jnp.pad((projected[2] + qv_all[1, 0].astype(f32)).astype(bf16), wide)
    wide_rows, lse = attend_forward(query, keys, values, starts)
    flat_rows = wide_rows[:, :width]
    gain_two, shift_two, fc_all, fc_bias_all, out_all, out_bias_all = (
        lax.all_gather(second_gain, "dp", axis=0, tiled=True),
        lax.all_gather(second_shift, "dp", axis=0, tiled=True),
        lax.all_gather(fc_weight, "dp", axis=0, tiled=True),
        lax.all_gather(fc_bias, "dp", axis=1, tiled=True),
        lax.all_gather(out_weight, "dp", axis=1, tiled=True),
        lax.all_gather(out_bias, "dp", axis=0, tiled=True),
    )
    gain_two_f = gain_two.astype(jnp.float32)
    shift_two_f = shift_two.astype(jnp.float32)
    branch_one = lax.psum(
        jnp.dot(flat_rows, proj_all, preferred_element_type=jnp.float32).astype(jnp.bfloat16), "mp"
    ).astype(jnp.float32)
    hidden_one = xin + branch_one + proj_bias_all.astype(jnp.float32)
    normed_two, inverse_two = norm_parts(hidden_one)
    act_two = (normed_two * gain_two_f + shift_two_f).astype(jnp.bfloat16)
    pre = jnp.dot(act_two, fc_all, preferred_element_type=jnp.float32) + fc_bias_all[0].astype(
        jnp.float32
    )
    fired = gelu_tanh(pre).astype(jnp.bfloat16)
    branch_two = lax.psum(
        jnp.dot(fired, out_all, preferred_element_type=jnp.float32).astype(jnp.bfloat16), "mp"
    ).astype(jnp.float32)
    output = (hidden_one + branch_two + out_bias_all.astype(jnp.float32)).astype(jnp.bfloat16)
    grad_out = out_grad.astype(jnp.float32)
    out_bias_grad = jnp.sum(out_grad, axis=0, dtype=jnp.float32)
    out_weight_grad = jnp.einsum("tf,td->fd", fired, out_grad, preferred_element_type=jnp.float32)
    fired_grad = jnp.einsum("td,fd->tf", out_grad, out_all, preferred_element_type=jnp.float32)
    pre_grad = (fired_grad * gelu_slope(pre)).astype(jnp.bfloat16)
    fc_bias_grad = jnp.sum(pre_grad, axis=0, dtype=jnp.float32)
    fc_weight_grad = jnp.einsum("td,tf->df", act_two, pre_grad, preferred_element_type=jnp.float32)
    act_two_grad = lax.psum(
        jnp.einsum("tf,df->td", pre_grad, fc_all, preferred_element_type=jnp.float32).astype(
            jnp.bfloat16
        ),
        "mp",
    ).astype(jnp.float32)
    gain_two_grad = jnp.sum(act_two_grad * normed_two, axis=0)
    shift_two_grad = jnp.sum(act_two_grad, axis=0)
    hidden_grad = grad_out + norm_back(act_two_grad, gain_two_f, normed_two, inverse_two)
    branch_grad = hidden_grad.astype(jnp.bfloat16)
    proj_bias_grad = jnp.sum(branch_grad, axis=0, dtype=jnp.float32)
    proj_weight_grad = jnp.einsum(
        "te,td->ed", flat_rows, branch_grad, preferred_element_type=jnp.float32
    )
    rows_grad = jnp.einsum(
        "td,ed->te", branch_grad, proj_all, preferred_element_type=jnp.float32
    ).astype(jnp.bfloat16)
    stacked = attend_backward(
        query, keys, values, wide_rows, jnp.pad(rows_grad, wide), starts, lse
    )[:, :, :width]
    qkv_grad = jnp.einsum("td,cte->cde", act_one, stacked, preferred_element_type=jnp.float32)
    bias_sums = jnp.sum(stacked, axis=1, dtype=jnp.float32)
    qv_grad = jnp.stack([bias_sums[0], bias_sums[2]])[:, None, :]
    act_one_grad = lax.psum(
        jnp.einsum("cte,cde->td", stacked, qkv_all, preferred_element_type=jnp.float32).astype(
            jnp.bfloat16
        ),
        "mp",
    ).astype(jnp.float32)
    gain_one_grad = jnp.sum(act_one_grad * normed_one, axis=0)
    shift_one_grad = jnp.sum(act_one_grad, axis=0)
    input_grad = (
        hidden_grad + norm_back(act_one_grad, gain_one_f, normed_one, inverse_one)
    ).astype(jnp.bfloat16)
    mlp_grads = (
        lax.psum_scatter(gain_two_grad, "dp", scatter_dimension=0, tiled=True),
        lax.psum_scatter(shift_two_grad, "dp", scatter_dimension=0, tiled=True),
        lax.psum_scatter(fc_weight_grad, "dp", scatter_dimension=0, tiled=True),
        lax.psum_scatter(fc_bias_grad[None], "dp", scatter_dimension=1, tiled=True),
        lax.psum_scatter(out_weight_grad, "dp", scatter_dimension=1, tiled=True),
        lax.psum_scatter(out_bias_grad, "dp", scatter_dimension=0, tiled=True),
    )
    attn_grads = (
        summed_on_arrival(gain_one_grad.astype(jnp.bfloat16), "dp", 0),
        summed_on_arrival(shift_one_grad.astype(jnp.bfloat16), "dp", 0),
        summed_on_arrival(qkv_grad.astype(jnp.bfloat16), "dp", 1),
        summed_on_arrival(qv_grad.astype(jnp.bfloat16), "dp", 2),
        summed_on_arrival(proj_weight_grad.astype(jnp.bfloat16), "dp", 1),
        summed_on_arrival(proj_bias_grad.astype(jnp.bfloat16), "dp", 0),
    )
    return (
        output,
        input_grad,
        attn_grads[0],
        attn_grads[1],
        attn_grads[2],
        attn_grads[3],
        attn_grads[4],
        attn_grads[5],
        mlp_grads[0],
        mlp_grads[1],
        mlp_grads[2],
        mlp_grads[3],
        mlp_grads[4],
        mlp_grads[5],
    )


def solution(mesh):
    placed = (
        P("dp", None),
        P("dp", None),
        P("dp"),
        P("dp"),
        P(None, "dp", "mp"),
        P(None, "mp", "dp"),
        P("mp", "dp"),
        P("dp"),
        P("dp"),
        P("dp"),
        P("dp", "mp"),
        P("mp", "dp"),
        P("mp", "dp"),
        P("dp"),
        P("dp", None),
    )
    return jax.shard_map(
        per_device,
        mesh=mesh,
        in_specs=placed,
        out_specs=(
            P("dp", None),
            P("dp", None),
            P("dp"),
            P("dp"),
            P(None, "dp", "mp"),
            P(None, "mp", "dp"),
            P("mp", "dp"),
            P("dp"),
            P("dp"),
            P("dp"),
            P("dp", "mp"),
            P("mp", "dp"),
            P("mp", "dp"),
            P("dp"),
        ),
        check_vma=False,
    )
```

```python
import functools

import jax
import jax.numpy as jnp
from jax import lax
from jax.experimental import pallas as pl
from jax.experimental.pallas import tpu as pltpu
from jax.sharding import PartitionSpec as P

HD = 64
HPD = 3
WIDE = 256
MAXLEN = 1024
QB = 256
BAND = MAXLEN // QB


EPS = 1e-05
SCALE = 0.125
NEG = -1e30
GELU_C = 0.7978845608028654
NN = (((1,), (0,)), ((), ()))
NT = (((1,), (1,)), ((), ()))
TN = (((0,), (0,)), ((), ()))
f32 = jnp.float32
bf16 = jnp.bfloat16


def mm(left, right, dims=NN):
    return lax.dot_general(left, right, dims, preferred_element_type=f32)


def split_up(shard, dim, size):
    before, after = (shard.shape[:dim], shard.shape[dim + 1 :])
    return jnp.moveaxis(shard.reshape(*before, size, -1, *after), dim, 0)


def summed_on_arrival(shard, axis, dim):
    size = lax.axis_size(axis)
    pieces = lax.all_to_all(split_up(shard, dim, size), axis, 0, 0, tiled=True)
    return jnp.sum(pieces.astype(jnp.float32), axis=0)


def norm_parts(values):
    mean = jnp.mean(values, axis=-1, keepdims=True)
    centred = values - mean
    inverse = lax.rsqrt(jnp.mean(centred * centred, axis=-1, keepdims=True) + EPS)
    return (centred * inverse, inverse)


def norm_back(grad, gain, normed, inverse):
    scaled = grad * gain
    return inverse * (
        scaled
        - jnp.mean(scaled, axis=-1, keepdims=True)
        - normed * jnp.mean(scaled * normed, axis=-1, keepdims=True)
    )


def gelu_tanh(values):
    return 0.5 * values * (1.0 + jnp.tanh(GELU_C * (values + 0.044715 * values * values * values)))


def gelu_slope(values):
    inner = GELU_C * (values + 0.044715 * values * values * values)
    tangent = jnp.tanh(inner)
    return 0.5 * (1.0 + tangent) + 0.5 * values * (1.0 - tangent * tangent) * GELU_C * (
        1.0 + 3.0 * 0.044715 * values * values
    )


def segment_starts(lengths_row, count):
    ends = jnp.cumsum(lengths_row)
    places = jnp.arange(count, dtype=jnp.int32)
    return jnp.max(jnp.where(ends[None, :] <= places[:, None], ends[None, :], 0), axis=1)[None, :]


def rows_of(index, size=QB):
    return pl.ds(pl.multiple_of(index * size, size), size)


def tile_heads(x):
    return jnp.concatenate([x] * HPD, axis=1)


def allowed_keys(i, j, start_ref):
    start = start_ref[:, rows_of(i)]
    key = lax.broadcasted_iota(jnp.int32, (QB, QB), 0)
    query = lax.broadcasted_iota(jnp.int32, (QB, QB), 1)
    return (key >= start - j * QB) & (key <= query + (i - j) * QB)


def stack_heads(x):
    lane = lax.broadcasted_iota(jnp.int32, x.shape, 1)
    return jnp.concatenate(
        [
            jnp.where((lane >= HD * h) & (lane < HD * h + HD), x, jnp.zeros_like(x))
            for h in range(HPD)
        ],
        axis=0,
    )


def attend_block(i, q_ref, k_ref, vt_ref, start_ref, lse_ref, o_ref, qs, acc):
    rows = rows_of(i)
    qs[...] = stack_heads(q_ref[rows])
    acc[...] = jnp.zeros_like(acc)

    def step(jj, carry):
        biggest, total = carry
        j = i - jj
        keys = rows_of(j)
        s = mm(k_ref[keys], qs[...], NT)
        s = jnp.where(tile_heads(allowed_keys(i, j, start_ref)), s, NEG)
        new = jnp.maximum(biggest, jnp.max(s, axis=0, keepdims=True))
        p = jnp.exp(s - new)
        shrink = jnp.exp(biggest - new)
        total = total * shrink + jnp.sum(p, axis=0, keepdims=True)
        p = p.astype(bf16)
        for h in range(HPD):
            cols = slice(QB * h, QB * h + QB)
            acc[:, cols] = acc[:, cols] * shrink[:, cols] + mm(
                vt_ref[HD * h : HD * h + HD, keys], p[:, cols]
            )
        return new, total

    biggest, total = lax.fori_loop(
        0,
        jnp.minimum(i, BAND) + 1,
        step,
        (jnp.full((1, HPD * QB), NEG, f32), jnp.zeros((1, HPD * QB), f32)),
    )
    lse_ref[i] = biggest + jnp.log(total)
    inverse = 1.0 / total
    out = jnp.concatenate(
        [acc[:, QB * h : QB * h + QB] * inverse[:, QB * h : QB * h + QB] for h in range(HPD)]
        + [jnp.zeros((WIDE - HPD * HD, QB), f32)],
        axis=0,
    )
    o_ref[rows] = out.T.astype(bf16)


def attend_block_back(i, grad, q_ref, k_ref, v_ref, kt_ref, o_ref, start_ref, lse_ref, dk, dv, qs, gs, dqt):
    rows = rows_of(i)
    qs[...] = stack_heads(q_ref[rows])
    gs[...] = stack_heads(grad)
    both = (grad.astype(f32) * o_ref[rows].astype(f32)).T
    delta = jnp.concatenate(
        [jnp.sum(both[HD * h : HD * h + HD], axis=0, keepdims=True) for h in range(HPD)], axis=1
    )
    lse = lse_ref[i]
    dqt[...] = jnp.zeros_like(dqt)

    def step(jj, _):
        j = i - jj
        keys = rows_of(j)
        s = mm(k_ref[keys], qs[...], NT)
        s = jnp.where(tile_heads(allowed_keys(i, j, start_ref)), s, NEG)
        p = jnp.exp(s - lse)
        dp = mm(v_ref[keys], gs[...], NT)
        ds = (p * (dp - delta)).astype(bf16)
        p = p.astype(bf16)
        dv[keys] += mm(p, gs[...])
        dk[keys] += mm(ds, qs[...])
        for h in range(HPD):
            dqt[HD * h : HD * h + HD] += mm(
                kt_ref[HD * h : HD * h + HD, keys], ds[:, QB * h : QB * h + QB]
            )
        return 0

    lax.fori_loop(0, jnp.minimum(i, BAND) + 1, step, 0)


def forward_kernel(q_ref, k_ref, v_ref, start_ref, o_ref, lse_ref, vt, qs, acc):
    blocks = q_ref.shape[0] // QB

    def turn(i, _):
        vt[:, rows_of(i)] = v_ref[rows_of(i)].T
        return 0

    lax.fori_loop(0, blocks, turn, 0)

    def block(i, _):
        attend_block(i, q_ref, k_ref, vt, start_ref, lse_ref, o_ref, qs, acc)
        return 0

    lax.fori_loop(0, blocks, block, 0)


def backward_kernel(
    q_ref, k_ref, v_ref, o_ref, g_ref, start_ref, lse_ref, d_ref, kt, qs, gs, dqt, dk, dv
):
    blocks = q_ref.shape[0] // QB

    def turn(i, _):
        kt[:, rows_of(i)] = k_ref[rows_of(i)].T
        return 0

    lax.fori_loop(0, blocks, turn, 0)
    dk[...] = jnp.zeros_like(dk)
    dv[...] = jnp.zeros_like(dv)

    def block(turn_of, _):
        i = blocks - 1 - turn_of
        rows = rows_of(i)
        attend_block_back(
            i, g_ref[rows], q_ref, k_ref, v_ref, kt, o_ref, start_ref, lse_ref, dk, dv, qs, gs, dqt
        )
        d_ref[0, rows] = (dqt[...].T * SCALE).astype(bf16)
        d_ref[1, rows] = dk[rows].astype(bf16)
        d_ref[2, rows] = dv[rows].astype(bf16)
        return 0

    lax.fori_loop(0, blocks, block, 0)


VMEM = pl.BlockSpec(memory_space=pltpu.VMEM)
LIMIT = pltpu.CompilerParams(vmem_limit_bytes=40 * 2**20)


def attend_forward(query, keys, values, starts):
    count = query.shape[0]
    return pl.pallas_call(
        forward_kernel,
        out_shape=(
            jax.ShapeDtypeStruct((count, WIDE), bf16),
            jax.ShapeDtypeStruct((count // QB, 1, HPD * QB), f32),
        ),
        in_specs=[VMEM] * 4,
        out_specs=(VMEM, VMEM),
        scratch_shapes=[
            pltpu.VMEM((WIDE, count), bf16),
            pltpu.VMEM((HPD * QB, WIDE), bf16),
            pltpu.VMEM((HD, HPD * QB), f32),
        ],
        compiler_params=LIMIT,
    )(query, keys, values, starts)


def attend_backward(query, keys, values, rows, grad, starts, lse):
    count = query.shape[0]
    return pl.pallas_call(
        backward_kernel,
        out_shape=jax.ShapeDtypeStruct((3, count, WIDE), bf16),
        in_specs=[VMEM] * 7,
        out_specs=VMEM,
        scratch_shapes=[
            pltpu.VMEM((WIDE, count), bf16),
            pltpu.VMEM((HPD * QB, WIDE), bf16),
            pltpu.VMEM((HPD * QB, WIDE), bf16),
            pltpu.VMEM((WIDE, QB), f32),
            pltpu.VMEM((count, WIDE), f32),
            pltpu.VMEM((count, WIDE), f32),
        ],
        compiler_params=LIMIT,
    )(query, keys, values, rows, grad, starts, lse)


def per_device(
    tokens,
    lengths,
    first_gain,
    first_shift,
    qkv_weight,
    qv_bias,
    proj_weight,
    proj_bias,
    second_gain,
    second_shift,
    fc_weight,
    fc_bias,
    out_weight,
    out_bias,
    out_grad,
):
    count = tokens.shape[0]
    starts = segment_starts(lengths[0], count)
    gain_one, shift_one, qkv_all, qv_all, proj_all, proj_bias_all = (
        lax.all_gather(first_gain, "dp", axis=0, tiled=True),
        lax.all_gather(first_shift, "dp", axis=0, tiled=True),
        lax.all_gather(qkv_weight, "dp", axis=1, tiled=True),
        lax.all_gather(qv_bias, "dp", axis=2, tiled=True),
        lax.all_gather(proj_weight, "dp", axis=1, tiled=True),
        lax.all_gather(proj_bias, "dp", axis=0, tiled=True),
    )
    gain_one_f = gain_one.astype(jnp.float32)
    xin = tokens.astype(jnp.float32)
    normed_one, inverse_one = norm_parts(xin)
    act_one = (normed_one * gain_one_f + shift_one.astype(jnp.float32)).astype(jnp.bfloat16)
    projected = jnp.einsum("td,cde->cte", act_one, qkv_all, preferred_element_type=jnp.float32)
    width = qkv_all.shape[2]
    wide = ((0, 0), (0, WIDE - width))
    query = jnp.pad(
        (projected[0] + qv_all[0, 0].astype(f32)).astype(bf16) * jnp.asarray(SCALE, bf16), wide
    )
    keys = jnp.pad(projected[1].astype(bf16), wide)
    values = jnp.pad((projected[2] + qv_all[1, 0].astype(f32)).astype(bf16), wide)
    wide_rows, lse = attend_forward(query, keys, values, starts)
    flat_rows = wide_rows[:, :width]
    gain_two, shift_two, fc_all, fc_bias_all, out_all, out_bias_all = (
        lax.all_gather(second_gain, "dp", axis=0, tiled=True),
        lax.all_gather(second_shift, "dp", axis=0, tiled=True),
        lax.all_gather(fc_weight, "dp", axis=0, tiled=True),
        lax.all_gather(fc_bias, "dp", axis=1, tiled=True),
        lax.all_gather(out_weight, "dp", axis=1, tiled=True),
        lax.all_gather(out_bias, "dp", axis=0, tiled=True),
    )
    gain_two_f = gain_two.astype(jnp.float32)
    shift_two_f = shift_two.astype(jnp.float32)
    branch_one = lax.psum(
        jnp.dot(flat_rows, proj_all, preferred_element_type=jnp.float32).astype(jnp.bfloat16), "mp"
    ).astype(jnp.float32)
    hidden_one = xin + branch_one + proj_bias_all.astype(jnp.float32)
    normed_two, inverse_two = norm_parts(hidden_one)
    act_two = (normed_two * gain_two_f + shift_two_f).astype(jnp.bfloat16)
    pre = jnp.dot(act_two, fc_all, preferred_element_type=jnp.float32) + fc_bias_all[0].astype(
        jnp.float32
    )
    fired = gelu_tanh(pre).astype(jnp.bfloat16)
    branch_two = lax.psum(
        jnp.dot(fired, out_all, preferred_element_type=jnp.float32).astype(jnp.bfloat16), "mp"
    ).astype(jnp.float32)
    output = (hidden_one + branch_two + out_bias_all.astype(jnp.float32)).astype(jnp.bfloat16)
    grad_out = out_grad.astype(jnp.float32)
    out_bias_grad = jnp.sum(out_grad, axis=0, dtype=jnp.float32)
    out_weight_grad = jnp.einsum("tf,td->fd", fired, out_grad, preferred_element_type=jnp.float32)
    fired_grad = jnp.einsum("td,fd->tf", out_grad, out_all, preferred_element_type=jnp.float32)
    pre_grad = (fired_grad * gelu_slope(pre)).astype(jnp.bfloat16)
    fc_bias_grad = jnp.sum(pre_grad, axis=0, dtype=jnp.float32)
    fc_weight_grad = jnp.einsum("td,tf->df", act_two, pre_grad, preferred_element_type=jnp.float32)
    act_two_grad = lax.psum(
        jnp.einsum("tf,df->td", pre_grad, fc_all, preferred_element_type=jnp.float32).astype(
            jnp.bfloat16
        ),
        "mp",
    ).astype(jnp.float32)
    gain_two_grad = jnp.sum(act_two_grad * normed_two, axis=0)
    shift_two_grad = jnp.sum(act_two_grad, axis=0)
    hidden_grad = grad_out + norm_back(act_two_grad, gain_two_f, normed_two, inverse_two)
    branch_grad = hidden_grad.astype(jnp.bfloat16)
    proj_bias_grad = jnp.sum(branch_grad, axis=0, dtype=jnp.float32)
    proj_weight_grad = jnp.einsum(
        "te,td->ed", flat_rows, branch_grad, preferred_element_type=jnp.float32
    )
    rows_grad = jnp.einsum(
        "td,ed->te", branch_grad, proj_all, preferred_element_type=jnp.float32
    ).astype(jnp.bfloat16)
    stacked = attend_backward(
        query, keys, values, wide_rows, jnp.pad(rows_grad, wide), starts, lse
    )[:, :, :width]
    qkv_grad = jnp.einsum("td,cte->cde", act_one, stacked, preferred_element_type=jnp.float32)
    bias_sums = jnp.sum(stacked, axis=1, dtype=jnp.float32)
    qv_grad = jnp.stack([bias_sums[0], bias_sums[2]])[:, None, :]
    act_one_grad = lax.psum(
        jnp.einsum("cte,cde->td", stacked, qkv_all, preferred_element_type=jnp.float32).astype(
            jnp.bfloat16
        ),
        "mp",
    ).astype(jnp.float32)
    gain_one_grad = jnp.sum(act_one_grad * normed_one, axis=0)
    shift_one_grad = jnp.sum(act_one_grad, axis=0)
    input_grad = (
        hidden_grad + norm_back(act_one_grad, gain_one_f, normed_one, inverse_one)
    ).astype(jnp.bfloat16)
    mlp_grads = (
        lax.psum_scatter(gain_two_grad, "dp", scatter_dimension=0, tiled=True),
        lax.psum_scatter(shift_two_grad, "dp", scatter_dimension=0, tiled=True),
        lax.psum_scatter(fc_weight_grad, "dp", scatter_dimension=0, tiled=True),
        lax.psum_scatter(fc_bias_grad[None], "dp", scatter_dimension=1, tiled=True),
        lax.psum_scatter(out_weight_grad, "dp", scatter_dimension=1, tiled=True),
        lax.psum_scatter(out_bias_grad, "dp", scatter_dimension=0, tiled=True),
    )
    attn_grads = (
        summed_on_arrival(gain_one_grad.astype(jnp.bfloat16), "dp", 0),
        summed_on_arrival(shift_one_grad.astype(jnp.bfloat16), "dp", 0),
        summed_on_arrival(qkv_grad.astype(jnp.bfloat16), "dp", 1),
        summed_on_arrival(qv_grad.astype(jnp.bfloat16), "dp", 2),
        summed_on_arrival(proj_weight_grad.astype(jnp.bfloat16), "dp", 1),
        summed_on_arrival(proj_bias_grad.astype(jnp.bfloat16), "dp", 0),
    )
    return (
        output,
        input_grad,
        attn_grads[0],
        attn_grads[1],
        attn_grads[2],
        attn_grads[3],
        attn_grads[4],
        attn_grads[5],
        mlp_grads[0],
        mlp_grads[1],
        mlp_grads[2],
        mlp_grads[3],
        mlp_grads[4],
        mlp_grads[5],
    )


MESH = pl.DeviceIdType.MESH
TB = 512
RB = 128


def norm(values):
    mean = jnp.mean(values, axis=-1, keepdims=True)
    centred = values - mean
    inverse = lax.rsqrt(jnp.mean(centred * centred, axis=-1, keepdims=True) + EPS)
    return centred * inverse, inverse


def remote(src, dst, send, recv, device):
    return pltpu.make_async_remote_copy(
        src_ref=src, dst_ref=dst, send_sem=send, recv_sem=recv, device_id=device, device_id_type=MESH
    )


def whole_kernel(
    tokens,
    grads,
    starts,
    fc_own,
    out_own,
    qkv_own,
    par_own,
    output,
    grad_tokens,
    dw_out,
    dwp_out,
    pg_out,
    w_fc,
    w_out,
    w_qkv,
    pars,
    par,
    fcb,
    qr,
    kr,
    vr,
    turned,
    orow,
    rows_all,
    lse,
    qs,
    gs,
    acc,
    dqt,
    dk,
    dv,
    gbuf,
    normed,
    inv,
    act,
    oacc,
    gacc,
    fired,
    preg,
    rowg,
    stacked,
    hid,
    dw,
    dwp,
    pgrad,
    pgbuf,
    part,
    edge,
    far,
    q_s,
    q_r,
    p_s,
    p_r,
    z_s,
    z_r,
    w_s,
    w_r,
    a_s,
    a_r,
    ar_s,
    ar_r,
    d_s,
    d_r,
    g_s,
    g_r,
    loc,
    free,
):
    d = lax.axis_index("dp")
    m = lax.axis_index("mp")
    y, x, k = d // 4, (d // 2) % 2, d % 2
    count = tokens.shape[0]
    blocks, subs = count // TB, count // QB

    def place(yy, xx, kk):
        return (yy * 4 + xx * 2 + kk, m)

    flat_fc = w_fc.reshape(4, 768, 1024)
    flat_out = w_out.reshape(4, 768, 768)
    flat_qkv = w_qkv.reshape(768, 3 * WIDE)
    x_dev, y_dev, diag, twin = (
        place(y, 1 - x, k),
        place(1 - y, x, k),
        place(1 - y, 1 - x, k),
        place(y, x, 1 - k),
    )
    plane = [(lax.rem(d + o, 8), m) for o in range(8)]
    line = [(d, lax.rem(m + o, 4)) for o in range(4)]
    came = [lax.rem(m + 4 - o, 4) for o in range(4)]

    barrier = pltpu.get_barrier_semaphore()
    for device in plane[1:] + line[1:]:
        pl.semaphore_signal(barrier, inc=1, device_id=device, device_id_type=MESH)
    pl.semaphore_wait(barrier, 10)

    q_send = [
        remote(qkv_own, w_qkv.at[y, x, k], q_s.at[i], q_r.at[i], device)
        for i, device in enumerate((x_dev, y_dev, diag, twin))
    ]
    q_from = [(y, 1 - x, k), (1 - y, x, k), (1 - y, 1 - x, k)]
    q_pass = [
        remote(w_qkv.at[c], w_qkv.at[c], q_s.at[4 + i], q_r.at[4 + i], twin)
        for i, c in enumerate(q_from)
    ]
    for copy in q_send:
        copy.start()
    p_send = [remote(par_own, pars.at[o], p_s.at[o], p_r.at[o], plane[o]) for o in range(1, 8)]
    for copy in p_send:
        copy.start()
    own = (fc_own, out_own)
    held = (w_fc, w_out)
    z_send = [
        [
            remote(own[c], held[c].at[m, y, x, k], z_s.at[c, o], z_r.at[c, o], line[o])
            for o in range(1, 4)
        ]
        for c in range(2)
    ]
    for o in range(3):
        for c in range(2):
            z_send[c][o].start()
    w_fc[m, y, x, k] = fc_own[...]
    w_out[m, y, x, k] = out_own[...]
    w_qkv[y, x, k] = qkv_own[...]
    pars[0] = par_own[...]

    def hop(o, c, stage):
        s = came[o]
        if stage == 0:
            part_of = held[c].at[s, y, x, k]
            device = (x_dev, y_dev)[c]
        elif stage == 1:
            part_of = (held[0].at[s, y, :, k], held[1].at[s, :, x, k])[c]
            device = (y_dev, x_dev)[c]
        else:
            part_of = held[c].at[s, :, :, k]
            device = twin
        return remote(part_of, part_of, w_s.at[c, stage, o], w_r.at[c, stage, o], device)

    def advance(o, stage):
        for c in range(2):
            if stage > 0:
                hop(o, c, stage - 1).wait_recv()
            elif o > 0:
                z_send[c][o - 1].wait_recv()
            hop(o, c, stage).start()

    advance(0, 0)
    g_in = [
        pltpu.make_async_copy(
            grads.at[pl.ds((blocks - 1 - t) * TB, TB)], gbuf.at[t % 2], loc.at[t % 2]
        )
        for t in range(blocks)
    ]
    g_in[0].start()

    for copy in p_send:
        copy.wait_recv()
    total = pars[0].astype(f32)
    for o in range(1, 8):
        total = total + pars[o].astype(f32)
    par[...] = total
    dk[...] = jnp.zeros_like(dk)
    dv[...] = jnp.zeros_like(dv)
    dw[...] = jnp.zeros_like(dw)
    dwp[...] = jnp.zeros_like(dwp)
    pgrad[...] = jnp.zeros_like(pgrad)
    for i in range(3):
        q_send[i].wait_recv()
        q_pass[i].start()
    q_send[3].wait_recv()
    for copy in q_pass:
        copy.wait_recv()

    def first_act(rows):
        unit, inverse = norm(tokens[rows].astype(f32))
        return (unit * par[0:1] + par[1:2]).astype(bf16)

    def project(b, _):
        rows = rows_of(b)
        r = mm(first_act(rows), flat_qkv[...]) + par[7:8]
        qr[rows] = r[:, :WIDE].astype(bf16) * jnp.asarray(SCALE, bf16)
        kr[rows] = r[:, WIDE : 2 * WIDE].astype(bf16)
        v = r[:, 2 * WIDE :].astype(bf16)
        vr[rows] = v
        turned[:, rows] = v.T
        return 0

    lax.fori_loop(0, subs, project, 0)

    def a_send(b, o):
        return remote(
            rows_all.at[m, b], rows_all.at[m, b], a_s.at[b, o], a_r.at[b, o], line[o]
        )

    def attend(t, _):
        b = blocks - 1 - t
        for half in (1, 0):
            attend_block(2 * b + half, qr, kr, turned, starts, lse, orow, qs, acc)
        top, low = rows_of(2 * b), rows_of(2 * b + 1)
        rows_all[m, b, :QB] = orow[top, :128]
        rows_all[m, b, QB : 2 * QB] = orow[low, :128]
        rows_all[m, b, 2 * QB :] = (
            orow[top, 128:].astype(f32) + pltpu.roll(orow[low, 128:].astype(f32), 64, 1)
        ).astype(bf16)
        for o in range(1, 4):
            a_send(b, o).start()

        @pl.when(t == 0)
        def _():
            advance(0, 1)
            advance(1, 0)

        @pl.when(t == 1)
        def _():
            advance(0, 2)
            advance(1, 1)

        @pl.when(t == 2)
        def _():
            advance(2, 0)
            advance(1, 2)

        return 0

    lax.fori_loop(0, blocks, attend, 0)

    def turn(i, _):
        turned[:, rows_of(i)] = kr[rows_of(i)].T
        return 0

    lax.fori_loop(0, subs, turn, 0)
    advance(2, 1)
    advance(3, 0)
    advance(2, 2)
    advance(3, 1)
    advance(3, 2)
    for o in range(4):
        for c in range(2):
            hop(o, c, 2).wait_recv()

    def bias_row(s, _):
        wide = flat_fc[s, :, 896:1024].astype(f32)
        fcb[s] = wide.T[64:65]
        return 0

    lax.fori_loop(0, 4, bias_row, 0)

    end = (m == 0) | (m == 3)
    inner = jnp.logical_not(end)
    inward = (d, jnp.where(m < 2, 1, 2))
    across = (d, 3 - m)
    outward = (d, jnp.where(m < 2, 0, 3))

    def hop_a(i):
        return remote(part.at[i], edge.at[i], ar_s.at[0, i], ar_r.at[0, i], inward)

    def hop_b(i):
        return remote(part.at[i], far.at[i], ar_s.at[1, i], ar_r.at[1, i], across)

    def hop_c(i):
        return remote(edge.at[i], far.at[i], ar_s.at[2, i], ar_r.at[2, i], outward)

    def stage_two(i):
        @pl.when(inner)
        def _():
            hop_a(i).wait_recv()
            part[i] = (part[i].astype(f32) + edge[i].astype(f32)).astype(bf16)
            hop_b(i).start()

    def stage_three(i):
        @pl.when(inner)
        def _():
            hop_b(i).wait_recv()
            edge[i] = (part[i].astype(f32) + far[i].astype(f32)).astype(bf16)
            hop_c(i).start()

    def gt_out(i):
        return pltpu.make_async_copy(
            hid.at[rows_of(i)], grad_tokens.at[rows_of(i)], g_s.at[8 + i]
        )

    def stage_four(i):
        @pl.when(end)
        def _():
            hop_c(i).wait_recv()
            edge[i] = far[i]

        def finish(r, _):
            some = rows_of(r, RB)
            there = pl.ds(pl.multiple_of(i * QB + r * RB, RB), RB)
            grad = edge[i, some].astype(f32)
            unit, inverse = norm(tokens[there].astype(f32))
            pgrad[0:1] += jnp.sum(grad * unit, axis=0, keepdims=True)
            pgrad[1:2] += jnp.sum(grad, axis=0, keepdims=True)
            back = norm_back(grad, par[0:1], unit, inverse)
            hid[there] = (hid[there].astype(f32) + back).astype(bf16)
            return 0

        lax.fori_loop(0, QB // RB, finish, 0)
        gt_out(i).start()

    def out_copy(b, slot):
        return pltpu.make_async_copy(gbuf.at[slot], output.at[rows_of(b, TB)], loc.at[2])

    def block(t, _):
        b = blocks - 1 - t
        rows = rows_of(b, TB)
        slot = lax.rem(t, 2)
        pltpu.make_async_copy(grads.at[rows], gbuf.at[slot], loc.at[slot]).wait()

        @pl.when(t >= 1)
        def _():
            out_copy(b + 1, 1 - slot).wait()

        @pl.when(t < blocks - 1)
        def _():
            pltpu.make_async_copy(
                grads.at[rows_of(b - 1, TB)], gbuf.at[1 - slot], loc.at[1 - slot]
            ).start()

        for o in range(1, 4):
            a_send(b, o).wait_recv()

        def head(s, _):
            third = rows_all[s, b, 2 * QB :].astype(f32)
            third = jnp.concatenate([third, pltpu.roll(third, 64, 1)], axis=0)
            lane = lax.broadcasted_iota(jnp.int32, third.shape, 1)
            third = jnp.where(lane < 64, third, 0.0).astype(bf16)
            left = jnp.concatenate([rows_all[s, b, : 2 * QB], third], axis=1)
            oacc[...] += mm(left, flat_fc[s, :, 768:1024], NT)
            return 0

        oacc[...] = tokens[rows].astype(f32) + par[4:5]
        lax.fori_loop(0, 4, head, 0)

        def second(r, _):
            some = rows_of(r, RB)
            hidden = oacc[some]
            unit, inverse = norm(hidden)
            normed[some] = unit
            inv[some] = inverse
            act[some] = (unit * par[2:3] + par[3:4]).astype(bf16)
            oacc[some] = hidden + par[5:6]
            gacc[some] = jnp.zeros_like(hidden)
            return 0

        lax.fori_loop(0, TB // RB, second, 0)

        def slab(s, _):
            def units(r, _):
                some = rows_of(r)
                pre = mm(act[some], flat_fc[s, :, 0:768]) + fcb[s]
                back = mm(gbuf[slot, some], flat_out[s])
                square = pre * pre
                tangent = jnp.tanh(pre * (GELU_C + (GELU_C * 0.044715) * square))
                half = 0.5 * pre
                fired[some] = (half + half * tangent).astype(bf16)
                slope = (0.5 + 0.5 * tangent) + half * (1.0 - tangent * tangent) * (
                    GELU_C + (3.0 * GELU_C * 0.044715) * square
                )
                preg[some] = (back * slope).astype(bf16)
                return 0

            lax.fori_loop(0, TB // QB, units, 0)
            oacc[...] += mm(fired[...], flat_out[s], NT)
            gacc[...] += mm(preg[...], flat_fc[s, :, 0:768], NT)

            @pl.when(s == m)
            def _():
                def outer(r, _):
                    some = rows_of(r)
                    dw[0, some] += mm(act[:, some], preg[...], TN)
                    dw[1, some] += mm(gbuf[slot, :, some], fired[...], TN)
                    return 0

                lax.fori_loop(0, 3, outer, 0)
                pgrad[6:7] += jnp.sum(preg[...].astype(f32), axis=0, keepdims=True)

            @pl.when((s == 1) & (t >= 2))
            def _():
                stage_three(2 * b + 5)
                stage_three(2 * b + 4)

            return 0

        lax.fori_loop(0, 4, slab, 0)

        def rejoin(r, _):
            some = rows_of(r, RB)
            there = pl.ds(pl.multiple_of(b * TB + r * RB, RB), RB)
            grad = gbuf[slot, some].astype(f32)
            through, unit = gacc[some], normed[some]
            pgrad[5:6] += jnp.sum(grad, axis=0, keepdims=True)
            pgrad[2:3] += jnp.sum(through * unit, axis=0, keepdims=True)
            pgrad[3:4] += jnp.sum(through, axis=0, keepdims=True)
            branch = (grad + norm_back(through, par[2:3], unit, inv[some])).astype(bf16)
            hid[there] = branch
            pgrad[4:5] += jnp.sum(branch.astype(f32), axis=0, keepdims=True)
            gbuf[slot, some] = oacc[some].astype(bf16)
            return 0

        lax.fori_loop(0, TB // RB, rejoin, 0)
        out_copy(b, slot).start()
        dwp[...] += mm(hid[rows], orow[rows], TN)
        rowg[...] = mm(hid[rows], flat_fc[m, :, 768:1024]).astype(bf16)

        @pl.when(t >= 1)
        def _():
            stage_two(2 * b + 3)
            stage_two(2 * b + 2)

        for half in (1, 0):
            i = 2 * b + half
            some = slice(half * QB, half * QB + QB)
            attend_block_back(
                i, rowg[some], qr, kr, vr, turned, orow, starts, lse, dk, dv, qs, gs, dqt
            )
            stacked[some, :WIDE] = (dqt[...].T * SCALE).astype(bf16)
            stacked[some, WIDE : 2 * WIDE] = dk[rows_of(i)].astype(bf16)
            stacked[some, 2 * WIDE :] = dv[rows_of(i)].astype(bf16)
            part[i] = mm(stacked[some], flat_qkv[...], NT).astype(bf16)

            @pl.when(end)
            def _():
                hop_a(i).start()

        pgrad[7:8] += jnp.sum(stacked[...].astype(f32), axis=0, keepdims=True)
        def again(r, _):
            act[rows_of(r, RB)] = first_act(pl.ds(pl.multiple_of(b * TB + r * RB, RB), RB))
            return 0

        lax.fori_loop(0, TB // RB, again, 0)

        def outer(r, _):
            some = rows_of(r)
            dw[2, some] += mm(act[:, some], stacked[...], TN)
            return 0

        lax.fori_loop(0, 3, outer, 0)

        @pl.when(t >= 2)
        def _():
            stage_four(2 * b + 5)
            stage_four(2 * b + 4)

        return 0

    lax.fori_loop(0, blocks, block, 0)

    for c in range(2):
        for o in range(3):
            z_send[c][o].wait_send()
        for o in range(4):
            for stage in range(3):
                hop(o, c, stage).wait_send()
    for device in (x_dev, y_dev, diag, twin):
        pl.semaphore_signal(free, inc=1, device_id=device, device_id_type=MESH)
    sib = w_fc.at[:, :, :, 0, :, 0:768]

    def rbuf(i):
        return w_fc.at[:, i // 2, i % 2, 1, :, 0:768]

    def pieces(yy, xx, kk):
        return w_out.at[:, yy, xx, kk]

    def take(c, dest):
        if c < 3:
            return dw[c, pl.ds(pl.multiple_of(dest * 96, 96), 96)]
        return dwp[pl.ds(pl.multiple_of(dest * 96, 96), 96)]

    spans = (768, 768, 768, 256)
    for yy in range(2):
        for xx in range(2):
            for c in range(4):
                w_out[c, yy, xx, 1 - k, :, : spans[c]] = take(c, yy * 4 + xx * 2 + 1 - k).astype(bf16)
    twin_copy = remote(w_out.at[:, :, :, 1 - k], sib, d_s.at[0], d_r.at[0], twin)
    pl.semaphore_wait(free, 4)
    twin_copy.start()
    stage_two(1)
    stage_three(3)
    stage_three(2)
    twin_copy.wait_recv()
    wants = [(y, 1 - x, x_dev), (1 - y, x, y_dev), (1 - y, 1 - x, diag)]
    owner_copies = []
    for i, (yy, xx, device) in enumerate(wants):
        for c in range(4):
            w_out[c, yy, xx, k, :, : spans[c]] = (
                take(c, yy * 4 + xx * 2 + k) + w_fc[c, yy, xx, 0, :, : spans[c]].astype(f32)
            ).astype(bf16)
        copy = remote(pieces(yy, xx, k), rbuf(i), d_s.at[1 + i], d_r.at[1 + i], device)
        copy.start()
        owner_copies.append(copy)
    stage_two(0)
    stage_three(1)
    stage_four(3)
    stage_four(2)
    stage_three(0)
    for copy in owner_copies:
        copy.wait_recv()
    for c in range(4):
        value = take(c, d) + w_fc[c, y, x, 0, :, : spans[c]].astype(f32)
        for i in range(3):
            value = value + w_fc[c, i // 2, i % 2, 1, :, : spans[c]].astype(f32)
        if c < 3:
            dw[c, pl.ds(pl.multiple_of(d * 96, 96), 96)] = value
        else:
            dwp[pl.ds(pl.multiple_of(d * 96, 96), 96)] = value
    results = [
        pltpu.make_async_copy(
            dw.at[:, pl.ds(pl.multiple_of(d * 96, 96), 96)], dw_out, loc.at[3]
        ),
        pltpu.make_async_copy(dwp.at[pl.ds(pl.multiple_of(d * 96, 96), 96)], dwp_out, loc.at[4]),
    ]
    for copy in results:
        copy.start()
    stage_four(1)
    stage_four(0)

    g_send = [
        remote(pgrad, pgbuf.at[o], g_s.at[o], g_r.at[o], plane[o]) for o in range(1, 8)
    ]
    for copy in g_send:
        copy.start()
    total = pgrad[...]
    for o, copy in enumerate(g_send):
        copy.wait_recv()
    for o in range(1, 8):
        total = total + pgbuf[o]
    pg_out[...] = total

    for copy in results:
        copy.wait()
    for copy in g_send + q_send + q_pass + p_send + owner_copies + [twin_copy]:
        copy.wait_send()
    out_copy(0, (blocks - 1) % 2).wait()

    def leave(i, _):
        gt_out(i).wait()

        @pl.when(end)
        def _():
            hop_a(i).wait_send()

        @pl.when(inner)
        def _():
            hop_b(i).wait_send()
            hop_c(i).wait_send()

        return 0

    lax.fori_loop(0, subs, leave, 0)
    for b in range(blocks):
        for o in range(1, 4):
            a_send(b, o).wait_send()


def whole_block(tokens, out_grad, starts, fc_own, out_own, qkv_own, par_own):
    count = tokens.shape[0]
    blocks, subs = count // TB, count // QB
    any_space = pl.BlockSpec(memory_space=pl.ANY)
    dma = pltpu.SemaphoreType.DMA
    return pl.pallas_call(
        whole_kernel,
        out_shape=(
            jax.ShapeDtypeStruct((count, 768), bf16),
            jax.ShapeDtypeStruct((count, 768), bf16),
            jax.ShapeDtypeStruct((3, 96, 768), f32),
            jax.ShapeDtypeStruct((96, WIDE), f32),
            jax.ShapeDtypeStruct((8, 768), f32),
        ),
        in_specs=[VMEM, any_space] + [VMEM] * 5,
        out_specs=(any_space, any_space, any_space, any_space, VMEM),
        scratch_shapes=[
            pltpu.VMEM((4, 2, 2, 2, 96, 1024), bf16),
            pltpu.VMEM((4, 2, 2, 2, 96, 768), bf16),
            pltpu.VMEM((2, 2, 2, 96, 768), bf16),
            pltpu.VMEM((8, 16, 768), bf16),
            pltpu.VMEM((16, 768), f32),
            pltpu.VMEM((4, 1, 768), f32),
            pltpu.VMEM((count, WIDE), bf16),
            pltpu.VMEM((count, WIDE), bf16),
            pltpu.VMEM((count, WIDE), bf16),
            pltpu.VMEM((WIDE, count), bf16),
            pltpu.VMEM((count, WIDE), bf16),
            pltpu.VMEM((4, blocks, 3 * QB, 128), bf16),
            pltpu.VMEM((subs, 1, HPD * QB), f32),
            pltpu.VMEM((HPD * QB, WIDE), bf16),
            pltpu.VMEM((HPD * QB, WIDE), bf16),
            pltpu.VMEM((HD, HPD * QB), f32),
            pltpu.VMEM((WIDE, QB), f32),
            pltpu.VMEM((count, WIDE), f32),
            pltpu.VMEM((count, WIDE), f32),
            pltpu.VMEM((2, TB, 768), bf16),
            pltpu.VMEM((TB, 768), f32),
            pltpu.VMEM((TB, 1), f32),
            pltpu.VMEM((TB, 768), bf16),
            pltpu.VMEM((TB, 768), f32),
            pltpu.VMEM((TB, 768), f32),
            pltpu.VMEM((TB, 768), bf16),
            pltpu.VMEM((TB, 768), bf16),
            pltpu.VMEM((TB, WIDE), bf16),
            pltpu.VMEM((TB, 768), bf16),
            pltpu.VMEM((count, 768), bf16),
            pltpu.VMEM((3, 768, 768), f32),
            pltpu.VMEM((768, 256), f32),
            pltpu.VMEM((8, 768), f32),
            pltpu.VMEM((8, 8, 768), f32),
            pltpu.VMEM((subs, QB, 768), bf16),
            pltpu.VMEM((subs, QB, 768), bf16),
            pltpu.VMEM((subs, QB, 768), bf16),
            dma((7,)),
            dma((7,)),
            dma((8,)),
            dma((8,)),
            dma((2, 4)),
            dma((2, 4)),
            dma((2, 3, 4)),
            dma((2, 3, 4)),
            dma((blocks, 4)),
            dma((blocks, 4)),
            dma((3, subs)),
            dma((3, subs)),
            dma((4,)),
            dma((4,)),
            dma((8 + subs,)),
            dma((8,)),
            dma((5,)),
            pltpu.SemaphoreType.REGULAR,
        ],
        compiler_params=pltpu.CompilerParams(
            collective_id=0, has_side_effects=True, vmem_limit_bytes=63 * 2**20
        ),
    )(tokens, out_grad, starts, fc_own, out_own, qkv_own, par_own)


def per_device_whole(
    tokens,
    lengths,
    first_gain,
    first_shift,
    qkv_weight,
    qv_bias,
    proj_weight,
    proj_bias,
    second_gain,
    second_shift,
    fc_weight,
    fc_bias,
    out_weight,
    out_bias,
    out_grad,
):
    d = lax.axis_index("dp")
    starts = segment_starts(lengths[0], tokens.shape[0])
    fc_own = jnp.concatenate(
        [fc_weight, proj_weight.T, fc_bias.T, jnp.zeros((96, 63), bf16)], axis=1
    )
    out_own = out_weight.T
    qkv_own = jnp.pad(qkv_weight, ((0, 0), (0, 0), (0, WIDE - 192)))
    qkv_own = jnp.moveaxis(qkv_own, 0, 1).reshape(96, 3 * WIDE)
    vectors = jnp.stack(
        [first_gain, first_shift, second_gain, second_shift, proj_bias, out_bias, fc_bias[0]]
    )
    par_own = jnp.zeros((16, 768), bf16)
    par_own = lax.dynamic_update_slice(par_own, vectors, (0, 96 * d))
    par_own = lax.dynamic_update_slice(par_own, qv_bias[0], (7, 24 * d))
    par_own = lax.dynamic_update_slice(par_own, qv_bias[1], (7, 2 * WIDE + 24 * d))
    output, grad_tokens, dw, dwp, pg = whole_block(
        tokens, out_grad, starts, fc_own, out_own, qkv_own, par_own
    )
    vec = lax.dynamic_slice(pg, (0, 96 * d), (7, 96))
    qv = jnp.concatenate(
        [
            lax.dynamic_slice(pg, (7, 24 * d), (1, 24)),
            lax.dynamic_slice(pg, (7, 2 * WIDE + 24 * d), (1, 24)),
        ]
    )[:, None, :]
    qkv_grad = jnp.moveaxis(dw[2].reshape(96, 3, WIDE)[:, :, :192], 1, 0)
    return (
        output,
        grad_tokens,
        vec[0],
        vec[1],
        qkv_grad,
        qv,
        dwp[:, :192].T,
        vec[4],
        vec[2],
        vec[3],
        dw[0],
        vec[6][None],
        dw[1].T,
        vec[5],
    )


def solution(mesh):
    placed = (
        P("dp", None),
        P("dp", None),
        P("dp"),
        P("dp"),
        P(None, "dp", "mp"),
        P(None, "mp", "dp"),
        P("mp", "dp"),
        P("dp"),
        P("dp"),
        P("dp"),
        P("dp", "mp"),
        P("mp", "dp"),
        P("mp", "dp"),
        P("dp"),
        P("dp", None),
    )
    return jax.shard_map(
        per_device_whole if dict(mesh.shape) == {"dp": 8, "mp": 4} else per_device,
        mesh=mesh,
        in_specs=placed,
        out_specs=(
            P("dp", None),
            P("dp", None),
            P("dp"),
            P("dp"),
            P(None, "dp", "mp"),
            P(None, "mp", "dp"),
            P("mp", "dp"),
            P("dp"),
            P("dp"),
            P("dp"),
            P("dp", "mp"),
            P("mp", "dp"),
            P("mp", "dp"),
            P("dp"),
        ),
        check_vma=False,
    )
```

```python
import functools

import jax
import jax.numpy as jnp
from jax import lax
from jax.experimental import pallas as pl
from jax.experimental.pallas import tpu as pltpu
from jax.sharding import PartitionSpec as P

HD = 64
HPD = 3
WIDE = 256
MAXLEN = 1024
QB = 256
BAND = MAXLEN // QB


EPS = 1e-05
SCALE = 0.125
NEG = -1e30
GELU_C = 0.7978845608028654
NN = (((1,), (0,)), ((), ()))
NT = (((1,), (1,)), ((), ()))
TN = (((0,), (0,)), ((), ()))
f32 = jnp.float32
bf16 = jnp.bfloat16


def mm(left, right, dims=NN):
    return lax.dot_general(left, right, dims, preferred_element_type=f32)


def split_up(shard, dim, size):
    before, after = (shard.shape[:dim], shard.shape[dim + 1 :])
    return jnp.moveaxis(shard.reshape(*before, size, -1, *after), dim, 0)


def summed_on_arrival(shard, axis, dim):
    size = lax.axis_size(axis)
    pieces = lax.all_to_all(split_up(shard, dim, size), axis, 0, 0, tiled=True)
    return jnp.sum(pieces.astype(jnp.float32), axis=0)


def norm_parts(values):
    mean = jnp.mean(values, axis=-1, keepdims=True)
    centred = values - mean
    inverse = lax.rsqrt(jnp.mean(centred * centred, axis=-1, keepdims=True) + EPS)
    return (centred * inverse, inverse)


def norm_back(grad, gain, normed, inverse):
    scaled = grad * gain
    return inverse * (
        scaled
        - jnp.mean(scaled, axis=-1, keepdims=True)
        - normed * jnp.mean(scaled * normed, axis=-1, keepdims=True)
    )


def gelu_tanh(values):
    return 0.5 * values * (1.0 + jnp.tanh(GELU_C * (values + 0.044715 * values * values * values)))


def gelu_slope(values):
    inner = GELU_C * (values + 0.044715 * values * values * values)
    tangent = jnp.tanh(inner)
    return 0.5 * (1.0 + tangent) + 0.5 * values * (1.0 - tangent * tangent) * GELU_C * (
        1.0 + 3.0 * 0.044715 * values * values
    )


def segment_starts(lengths_row, count):
    ends = jnp.cumsum(lengths_row)
    places = jnp.arange(count, dtype=jnp.int32)
    return jnp.max(jnp.where(ends[None, :] <= places[:, None], ends[None, :], 0), axis=1)[None, :]


def rows_of(index, size=QB):
    return pl.ds(pl.multiple_of(index * size, size), size)


def tile_heads(x):
    return jnp.concatenate([x] * HPD, axis=1)


def allowed_keys(i, j, start_ref):
    start = start_ref[:, rows_of(i)]
    key = lax.broadcasted_iota(jnp.int32, (QB, QB), 0)
    query = lax.broadcasted_iota(jnp.int32, (QB, QB), 1)
    return (key >= start - j * QB) & (key <= query + (i - j) * QB)


def stack_heads(x):
    lane = lax.broadcasted_iota(jnp.int32, x.shape, 1)
    return jnp.concatenate(
        [
            jnp.where((lane >= HD * h) & (lane < HD * h + HD), x, jnp.zeros_like(x))
            for h in range(HPD)
        ],
        axis=0,
    )


def attend_block(i, q_ref, k_ref, vt_ref, start_ref, lse_ref, o_ref, qs, acc):
    rows = rows_of(i)
    qs[...] = stack_heads(q_ref[rows])
    acc[...] = jnp.zeros_like(acc)

    def step(jj, carry):
        biggest, total = carry
        j = i - jj
        keys = rows_of(j)
        s = mm(k_ref[keys], qs[...], NT)
        s = jnp.where(tile_heads(allowed_keys(i, j, start_ref)), s, NEG)
        new = jnp.maximum(biggest, jnp.max(s, axis=0, keepdims=True))
        p = jnp.exp(s - new)
        shrink = jnp.exp(biggest - new)
        total = total * shrink + jnp.sum(p, axis=0, keepdims=True)
        p = p.astype(bf16)
        for h in range(HPD):
            cols = slice(QB * h, QB * h + QB)
            acc[:, cols] = acc[:, cols] * shrink[:, cols] + mm(
                vt_ref[HD * h : HD * h + HD, keys], p[:, cols]
            )
        return new, total

    biggest, total = lax.fori_loop(
        0,
        jnp.minimum(i, BAND) + 1,
        step,
        (jnp.full((1, HPD * QB), NEG, f32), jnp.zeros((1, HPD * QB), f32)),
    )
    lse_ref[i] = biggest + jnp.log(total)
    inverse = 1.0 / total
    out = jnp.concatenate(
        [acc[:, QB * h : QB * h + QB] * inverse[:, QB * h : QB * h + QB] for h in range(HPD)]
        + [jnp.zeros((WIDE - HPD * HD, QB), f32)],
        axis=0,
    )
    o_ref[rows] = out.T.astype(bf16)


def attend_block_back(i, grad, q_ref, k_ref, v_ref, kt_ref, o_ref, start_ref, lse_ref, dk, dv, qs, gs, dqt):
    rows = rows_of(i)
    qs[...] = stack_heads(q_ref[rows])
    gs[...] = stack_heads(grad)
    both = (grad.astype(f32) * o_ref[rows].astype(f32)).T
    delta = jnp.concatenate(
        [jnp.sum(both[HD * h : HD * h + HD], axis=0, keepdims=True) for h in range(HPD)], axis=1
    )
    lse = lse_ref[i]
    dqt[...] = jnp.zeros_like(dqt)

    def step(jj, _):
        j = i - jj
        keys = rows_of(j)
        s = mm(k_ref[keys], qs[...], NT)
        s = jnp.where(tile_heads(allowed_keys(i, j, start_ref)), s, NEG)
        p = jnp.exp(s - lse)
        dp = mm(v_ref[keys], gs[...], NT)
        ds = (p * (dp - delta)).astype(bf16)
        p = p.astype(bf16)
        dv[keys] += mm(p, gs[...])
        dk[keys] += mm(ds, qs[...])
        for h in range(HPD):
            dqt[HD * h : HD * h + HD] += mm(
                kt_ref[HD * h : HD * h + HD, keys], ds[:, QB * h : QB * h + QB]
            )
        return 0

    lax.fori_loop(0, jnp.minimum(i, BAND) + 1, step, 0)


def forward_kernel(q_ref, k_ref, v_ref, start_ref, o_ref, lse_ref, vt, qs, acc):
    blocks = q_ref.shape[0] // QB

    def turn(i, _):
        vt[:, rows_of(i)] = v_ref[rows_of(i)].T
        return 0

    lax.fori_loop(0, blocks, turn, 0)

    def block(i, _):
        attend_block(i, q_ref, k_ref, vt, start_ref, lse_ref, o_ref, qs, acc)
        return 0

    lax.fori_loop(0, blocks, block, 0)


def backward_kernel(
    q_ref, k_ref, v_ref, o_ref, g_ref, start_ref, lse_ref, d_ref, kt, qs, gs, dqt, dk, dv
):
    blocks = q_ref.shape[0] // QB

    def turn(i, _):
        kt[:, rows_of(i)] = k_ref[rows_of(i)].T
        return 0

    lax.fori_loop(0, blocks, turn, 0)
    dk[...] = jnp.zeros_like(dk)
    dv[...] = jnp.zeros_like(dv)

    def block(turn_of, _):
        i = blocks - 1 - turn_of
        rows = rows_of(i)
        attend_block_back(
            i, g_ref[rows], q_ref, k_ref, v_ref, kt, o_ref, start_ref, lse_ref, dk, dv, qs, gs, dqt
        )
        d_ref[0, rows] = (dqt[...].T * SCALE).astype(bf16)
        d_ref[1, rows] = dk[rows].astype(bf16)
        d_ref[2, rows] = dv[rows].astype(bf16)
        return 0

    lax.fori_loop(0, blocks, block, 0)


VMEM = pl.BlockSpec(memory_space=pltpu.VMEM)
LIMIT = pltpu.CompilerParams(vmem_limit_bytes=40 * 2**20)


def attend_forward(query, keys, values, starts):
    count = query.shape[0]
    return pl.pallas_call(
        forward_kernel,
        out_shape=(
            jax.ShapeDtypeStruct((count, WIDE), bf16),
            jax.ShapeDtypeStruct((count // QB, 1, HPD * QB), f32),
        ),
        in_specs=[VMEM] * 4,
        out_specs=(VMEM, VMEM),
        scratch_shapes=[
            pltpu.VMEM((WIDE, count), bf16),
            pltpu.VMEM((HPD * QB, WIDE), bf16),
            pltpu.VMEM((HD, HPD * QB), f32),
        ],
        compiler_params=LIMIT,
    )(query, keys, values, starts)


def attend_backward(query, keys, values, rows, grad, starts, lse):
    count = query.shape[0]
    return pl.pallas_call(
        backward_kernel,
        out_shape=jax.ShapeDtypeStruct((3, count, WIDE), bf16),
        in_specs=[VMEM] * 7,
        out_specs=VMEM,
        scratch_shapes=[
            pltpu.VMEM((WIDE, count), bf16),
            pltpu.VMEM((HPD * QB, WIDE), bf16),
            pltpu.VMEM((HPD * QB, WIDE), bf16),
            pltpu.VMEM((WIDE, QB), f32),
            pltpu.VMEM((count, WIDE), f32),
            pltpu.VMEM((count, WIDE), f32),
        ],
        compiler_params=LIMIT,
    )(query, keys, values, rows, grad, starts, lse)


def per_device(
    tokens,
    lengths,
    first_gain,
    first_shift,
    qkv_weight,
    qv_bias,
    proj_weight,
    proj_bias,
    second_gain,
    second_shift,
    fc_weight,
    fc_bias,
    out_weight,
    out_bias,
    out_grad,
):
    count = tokens.shape[0]
    starts = segment_starts(lengths[0], count)
    gain_one, shift_one, qkv_all, qv_all, proj_all, proj_bias_all = (
        lax.all_gather(first_gain, "dp", axis=0, tiled=True),
        lax.all_gather(first_shift, "dp", axis=0, tiled=True),
        lax.all_gather(qkv_weight, "dp", axis=1, tiled=True),
        lax.all_gather(qv_bias, "dp", axis=2, tiled=True),
        lax.all_gather(proj_weight, "dp", axis=1, tiled=True),
        lax.all_gather(proj_bias, "dp", axis=0, tiled=True),
    )
    gain_one_f = gain_one.astype(jnp.float32)
    xin = tokens.astype(jnp.float32)
    normed_one, inverse_one = norm_parts(xin)
    act_one = (normed_one * gain_one_f + shift_one.astype(jnp.float32)).astype(jnp.bfloat16)
    projected = jnp.einsum("td,cde->cte", act_one, qkv_all, preferred_element_type=jnp.float32)
    width = qkv_all.shape[2]
    wide = ((0, 0), (0, WIDE - width))
    query = jnp.pad(
        (projected[0] + qv_all[0, 0].astype(f32)).astype(bf16) * jnp.asarray(SCALE, bf16), wide
    )
    keys = jnp.pad(projected[1].astype(bf16), wide)
    values = jnp.pad((projected[2] + qv_all[1, 0].astype(f32)).astype(bf16), wide)
    wide_rows, lse = attend_forward(query, keys, values, starts)
    flat_rows = wide_rows[:, :width]
    gain_two, shift_two, fc_all, fc_bias_all, out_all, out_bias_all = (
        lax.all_gather(second_gain, "dp", axis=0, tiled=True),
        lax.all_gather(second_shift, "dp", axis=0, tiled=True),
        lax.all_gather(fc_weight, "dp", axis=0, tiled=True),
        lax.all_gather(fc_bias, "dp", axis=1, tiled=True),
        lax.all_gather(out_weight, "dp", axis=1, tiled=True),
        lax.all_gather(out_bias, "dp", axis=0, tiled=True),
    )
    gain_two_f = gain_two.astype(jnp.float32)
    shift_two_f = shift_two.astype(jnp.float32)
    branch_one = lax.psum(
        jnp.dot(flat_rows, proj_all, preferred_element_type=jnp.float32).astype(jnp.bfloat16), "mp"
    ).astype(jnp.float32)
    hidden_one = xin + branch_one + proj_bias_all.astype(jnp.float32)
    normed_two, inverse_two = norm_parts(hidden_one)
    act_two = (normed_two * gain_two_f + shift_two_f).astype(jnp.bfloat16)
    pre = jnp.dot(act_two, fc_all, preferred_element_type=jnp.float32) + fc_bias_all[0].astype(
        jnp.float32
    )
    fired = gelu_tanh(pre).astype(jnp.bfloat16)
    branch_two = lax.psum(
        jnp.dot(fired, out_all, preferred_element_type=jnp.float32).astype(jnp.bfloat16), "mp"
    ).astype(jnp.float32)
    output = (hidden_one + branch_two + out_bias_all.astype(jnp.float32)).astype(jnp.bfloat16)
    grad_out = out_grad.astype(jnp.float32)
    out_bias_grad = jnp.sum(out_grad, axis=0, dtype=jnp.float32)
    out_weight_grad = jnp.einsum("tf,td->fd", fired, out_grad, preferred_element_type=jnp.float32)
    fired_grad = jnp.einsum("td,fd->tf", out_grad, out_all, preferred_element_type=jnp.float32)
    pre_grad = (fired_grad * gelu_slope(pre)).astype(jnp.bfloat16)
    fc_bias_grad = jnp.sum(pre_grad, axis=0, dtype=jnp.float32)
    fc_weight_grad = jnp.einsum("td,tf->df", act_two, pre_grad, preferred_element_type=jnp.float32)
    act_two_grad = lax.psum(
        jnp.einsum("tf,df->td", pre_grad, fc_all, preferred_element_type=jnp.float32).astype(
            jnp.bfloat16
        ),
        "mp",
    ).astype(jnp.float32)
    gain_two_grad = jnp.sum(act_two_grad * normed_two, axis=0)
    shift_two_grad = jnp.sum(act_two_grad, axis=0)
    hidden_grad = grad_out + norm_back(act_two_grad, gain_two_f, normed_two, inverse_two)
    branch_grad = hidden_grad.astype(jnp.bfloat16)
    proj_bias_grad = jnp.sum(branch_grad, axis=0, dtype=jnp.float32)
    proj_weight_grad = jnp.einsum(
        "te,td->ed", flat_rows, branch_grad, preferred_element_type=jnp.float32
    )
    rows_grad = jnp.einsum(
        "td,ed->te", branch_grad, proj_all, preferred_element_type=jnp.float32
    ).astype(jnp.bfloat16)
    stacked = attend_backward(
        query, keys, values, wide_rows, jnp.pad(rows_grad, wide), starts, lse
    )[:, :, :width]
    qkv_grad = jnp.einsum("td,cte->cde", act_one, stacked, preferred_element_type=jnp.float32)
    bias_sums = jnp.sum(stacked, axis=1, dtype=jnp.float32)
    qv_grad = jnp.stack([bias_sums[0], bias_sums[2]])[:, None, :]
    act_one_grad = lax.psum(
        jnp.einsum("cte,cde->td", stacked, qkv_all, preferred_element_type=jnp.float32).astype(
            jnp.bfloat16
        ),
        "mp",
    ).astype(jnp.float32)
    gain_one_grad = jnp.sum(act_one_grad * normed_one, axis=0)
    shift_one_grad = jnp.sum(act_one_grad, axis=0)
    input_grad = (
        hidden_grad + norm_back(act_one_grad, gain_one_f, normed_one, inverse_one)
    ).astype(jnp.bfloat16)
    mlp_grads = (
        lax.psum_scatter(gain_two_grad, "dp", scatter_dimension=0, tiled=True),
        lax.psum_scatter(shift_two_grad, "dp", scatter_dimension=0, tiled=True),
        lax.psum_scatter(fc_weight_grad, "dp", scatter_dimension=0, tiled=True),
        lax.psum_scatter(fc_bias_grad[None], "dp", scatter_dimension=1, tiled=True),
        lax.psum_scatter(out_weight_grad, "dp", scatter_dimension=1, tiled=True),
        lax.psum_scatter(out_bias_grad, "dp", scatter_dimension=0, tiled=True),
    )
    attn_grads = (
        summed_on_arrival(gain_one_grad.astype(jnp.bfloat16), "dp", 0),
        summed_on_arrival(shift_one_grad.astype(jnp.bfloat16), "dp", 0),
        summed_on_arrival(qkv_grad.astype(jnp.bfloat16), "dp", 1),
        summed_on_arrival(qv_grad.astype(jnp.bfloat16), "dp", 2),
        summed_on_arrival(proj_weight_grad.astype(jnp.bfloat16), "dp", 1),
        summed_on_arrival(proj_bias_grad.astype(jnp.bfloat16), "dp", 0),
    )
    return (
        output,
        input_grad,
        attn_grads[0],
        attn_grads[1],
        attn_grads[2],
        attn_grads[3],
        attn_grads[4],
        attn_grads[5],
        mlp_grads[0],
        mlp_grads[1],
        mlp_grads[2],
        mlp_grads[3],
        mlp_grads[4],
        mlp_grads[5],
    )


MESH = pl.DeviceIdType.MESH
TB = 512
RB = 128


def norm(values):
    mean = jnp.mean(values, axis=-1, keepdims=True)
    centred = values - mean
    inverse = lax.rsqrt(jnp.mean(centred * centred, axis=-1, keepdims=True) + EPS)
    return centred * inverse, inverse


def remote(src, dst, send, recv, device):
    return pltpu.make_async_remote_copy(
        src_ref=src, dst_ref=dst, send_sem=send, recv_sem=recv, device_id=device, device_id_type=MESH
    )


def whole_kernel(
    tokens,
    grads,
    starts,
    fc_own,
    out_own,
    pr_own,
    qkv_own,
    par_own,
    output,
    grad_tokens,
    dw_out,
    dwp_out,
    pg_out,
    w_fc,
    w_out,
    w_pr,
    w_qkv,
    pars,
    par,
    fcb,
    qr,
    kr,
    vr,
    turned,
    orow,
    rows_all,
    lse,
    qs,
    gs,
    acc,
    dqt,
    dk,
    dv,
    gbuf,
    normed,
    inv,
    act,
    oacc,
    gacc,
    fired,
    preg,
    rowg,
    stacked,
    hid,
    dw,
    dwp,
    pgrad,
    pgbuf,
    zgbuf,
    part,
    edge,
    far,
    q_s,
    q_r,
    p_s,
    p_r,
    z_s,
    z_r,
    w_s,
    w_r,
    af_s,
    a_s,
    a_r,
    ar_s,
    ar_r,
    d_s,
    d_r,
    zg_s,
    zg_r,
    g_s,
    g_r,
    loc,
    free,
):
    d = lax.axis_index("dp")
    m = lax.axis_index("mp")
    y, x, k = d // 4, (d // 2) % 2, d % 2
    count = tokens.shape[0]
    blocks, subs = count // TB, count // QB

    def place(yy, xx, kk):
        return (yy * 4 + xx * 2 + kk, m)

    flat_fc = w_fc.reshape(4, 768, 768)
    flat_pr = w_pr.reshape(4, 768, 256)
    flat_out = w_out.reshape(4, 768, 768)
    flat_qkv = w_qkv.reshape(768, 3 * WIDE)
    x_dev, y_dev, diag, twin = (
        place(y, 1 - x, k),
        place(1 - y, x, k),
        place(1 - y, 1 - x, k),
        place(y, x, 1 - k),
    )
    plane = [(lax.rem(d + o, 8), m) for o in range(8)]
    line = [(d, lax.rem(m + o, 4)) for o in range(4)]
    above, below = (d, jnp.minimum(m + 1, 3)), (d, jnp.maximum(m - 1, 0))
    end = (m == 0) | (m == 3)
    inner = jnp.logical_not(end)
    order = [m] + [jnp.where(m <= o - 1, o, o - 1) for o in range(1, 4)]

    barrier = pltpu.get_barrier_semaphore()
    for device in plane[1:] + line[1:]:
        pl.semaphore_signal(barrier, inc=1, device_id=device, device_id_type=MESH)
    pl.semaphore_wait(barrier, 10)

    q_send = [
        remote(qkv_own, w_qkv.at[y, x, k], q_s.at[i], q_r.at[i], device)
        for i, device in enumerate((x_dev, y_dev, diag, twin))
    ]
    q_from = [(y, 1 - x, k), (1 - y, x, k), (1 - y, 1 - x, k)]
    q_pass = [
        remote(w_qkv.at[c], w_qkv.at[c], q_s.at[4 + i], q_r.at[4 + i], twin)
        for i, c in enumerate(q_from)
    ]
    for copy in q_send:
        copy.start()
    p_send = [remote(par_own, pars.at[o], p_s.at[o], p_r.at[o], plane[o]) for o in range(1, 8)]
    for copy in p_send:
        copy.start()
    w_fc[m, y, x, k] = fc_own[...]
    w_out[m, y, x, k] = out_own[...]
    w_pr[m, y, x, k] = pr_own[...]
    w_qkv[y, x, k] = qkv_own[...]
    pars[0] = par_own[...]
    held = (w_fc, w_out, w_pr)

    def along(piece, send, recv, s):
        up = remote(piece, piece, send.at[0], recv, above)
        down = remote(piece, piece, send.at[1], recv, below)
        return ((s <= m) & (m < 3), up), ((s >= m) & (m > 0), down)

    def pass_on(piece, send, recv, s):
        for where, copy in along(piece, send, recv, s):
            pl.when(where)(copy.start)

    def passed_on(piece, send, recv, s):
        for where, copy in along(piece, send, recv, s):
            pl.when(where)(copy.wait_send)

    def z_args(c, s):
        return held[c].at[s, y, x, k], z_s.at[c, s], z_r.at[c, s], s

    def z_step(cs, far_by):
        for s, there in ((m - far_by, m >= far_by), (m + far_by, m + far_by <= 3)):

            @pl.when(there)
            def _():
                for c in cs:
                    piece, send, recv, _ = z_args(c, s)
                    remote(piece, piece, send.at[0], recv, above).wait_recv()
                    pass_on(*z_args(c, s))
                if 0 in cs:
                    spread(s, cs)

    for c in (2, 0, 1):
        pass_on(*z_args(c, m))

    def hop(s, c, stage):
        if stage == 0:
            part_of = held[c].at[s, y, x, k]
            device = y_dev if c == 1 else x_dev
        elif stage == 1:
            part_of = held[c].at[s, :, x, k] if c == 1 else held[c].at[s, y, :, k]
            device = x_dev if c == 1 else y_dev
        else:
            part_of = held[c].at[s, :, :, k]
            device = twin
        return remote(part_of, part_of, w_s.at[c, stage, s], w_r.at[c, stage, s], device)

    def spread(s, cs=(0, 1)):
        for c in cs:
            hop(s, c, 0).start()

    def advance(o, stage, cs=(0, 1)):
        for c in cs:
            hop(order[o], c, stage - 1).wait_recv()
            hop(order[o], c, stage).start()

    pltpu.make_async_copy(
        grads.at[rows_of(blocks - 1, TB)], gbuf.at[0], loc.at[0]
    ).start()

    for copy in p_send:
        copy.wait_recv()
    total = pars[0].astype(f32)
    for o in range(1, 8):
        total = total + pars[o].astype(f32)
    par[...] = total
    dk[...] = jnp.zeros_like(dk)
    dv[...] = jnp.zeros_like(dv)
    dw[...] = jnp.zeros_like(dw)
    dwp[...] = jnp.zeros_like(dwp)
    pgrad[...] = jnp.zeros_like(pgrad)
    z_step((2,), 1)
    z_step((2,), 2)
    z_step((2,), 3)
    for i in range(3):
        q_send[i].wait_recv()
        q_pass[i].start()
    spread(m)
    for s in range(4):
        spread(s, (2,))
    z_step((0, 1), 1)
    q_send[3].wait_recv()
    for copy in q_pass:
        copy.wait_recv()

    def first_act(rows):
        unit, inverse = norm(tokens[rows].astype(f32))
        return (unit * par[0:1] + par[1:2]).astype(bf16)

    def project(b, _):
        rows = rows_of(b)
        r = mm(first_act(rows), flat_qkv[...]) + par[7:8]
        qr[rows] = r[:, :WIDE].astype(bf16) * jnp.asarray(SCALE, bf16)
        kr[rows] = r[:, WIDE : 2 * WIDE].astype(bf16)
        v = r[:, 2 * WIDE :].astype(bf16)
        vr[rows] = v
        turned[:, rows] = v.T

        @pl.when(b == 0)
        def _():
            advance(0, 1)

        @pl.when(b == 2)
        def _():
            for o in range(4):
                advance(o, 1, (2,))

        @pl.when(b == 4)
        def _():
            z_step((0, 1), 2)

        @pl.when(b == 6)
        def _():
            for o in range(4):
                advance(o, 2, (2,))

        return 0

    lax.fori_loop(0, subs, project, 0)

    def a_args(b, s):
        return rows_all.at[s, b], a_s.at[b, s], a_r.at[b, s], s

    def a_wait(b, s):
        piece, send, recv, _ = a_args(b, s)
        remote(piece, piece, send.at[0], recv, above).wait_recv()

    def a_step(b, far_by):
        for s, there in ((m - far_by, m >= far_by), (m + far_by, m + far_by <= 3)):

            @pl.when(there & inner)
            def _():
                a_wait(b, s)
                pass_on(*a_args(b, s))

    def direct(b, o):
        return remote(rows_all.at[m, b], rows_all.at[m, b], af_s.at[o], a_r.at[b, m], line[o])

    def attend(t, _):
        b = blocks - 1 - t
        attend_block(2 * b + 1, qr, kr, turned, starts, lse, orow, qs, acc)

        @pl.when(t == 0)
        def _():
            advance(0, 2)

        @pl.when(t == 1)
        def _():
            advance(1, 1)

        @pl.when(t == 2)
        def _():
            advance(3, 1)

        attend_block(2 * b, qr, kr, turned, starts, lse, orow, qs, acc)
        top, low = rows_of(2 * b), rows_of(2 * b + 1)
        rows_all[m, b, :QB] = orow[top, :128]
        rows_all[m, b, QB : 2 * QB] = orow[low, :128]
        rows_all[m, b, 2 * QB :] = (
            orow[top, 128:].astype(f32) + pltpu.roll(orow[low, 128:].astype(f32), 64, 1)
        ).astype(bf16)

        @pl.when(t == 0)
        def _():
            z_step((0, 1), 3)
            for o in range(1, 4):
                direct(blocks - 1, o).start()

        @pl.when(t > 0)
        def _():
            pass_on(*a_args(b, m))

        @pl.when(t == 1)
        def _():
            advance(2, 1)

        return 0

    lax.fori_loop(0, blocks, attend, 0)
    advance(1, 2)

    def turn(i, _):
        turned[:, rows_of(i)] = kr[rows_of(i)].T
        return 0

    lax.fori_loop(0, subs, turn, 0)
    for s in range(4):
        hop(s, 2, 2).wait_recv()

    def bias_row(s, _):
        fcb[s] = flat_pr[s, :, 128:256].astype(f32).T[64:65]
        return 0

    lax.fori_loop(0, 4, bias_row, 0)

    inward = (d, jnp.where(m < 2, 1, 2))
    across = (d, 3 - m)
    outward = (d, jnp.where(m < 2, 0, 3))

    def hop_a(i):
        return remote(part.at[i], edge.at[i], ar_s.at[0, i], ar_r.at[0, i], inward)

    def hop_b(i):
        return remote(part.at[i], far.at[i], ar_s.at[1, i], ar_r.at[1, i], across)

    def hop_c(i):
        return remote(edge.at[i], far.at[i], ar_s.at[2, i], ar_r.at[2, i], outward)

    def stage_two(i):
        @pl.when(inner)
        def _():
            hop_a(i).wait_recv()
            part[i] = (part[i].astype(f32) + edge[i].astype(f32)).astype(bf16)
            hop_b(i).start()

    def stage_three(i):
        @pl.when(inner)
        def _():
            hop_b(i).wait_recv()
            edge[i] = (part[i].astype(f32) + far[i].astype(f32)).astype(bf16)
            hop_c(i).start()

    def gt_out(i):
        return pltpu.make_async_copy(
            hid.at[rows_of(i, RB)], grad_tokens.at[rows_of(i, RB)], g_s.at[8 + i]
        )

    def stage_four(i):
        @pl.when(end)
        def _():
            hop_c(i).wait_recv()
            edge[i] = far[i]

        there = rows_of(i, RB)
        grad = edge[i].astype(f32)
        unit, inverse = norm(tokens[there].astype(f32))
        back = norm_back(grad, par[0:1], unit, inverse)
        hid[there] = (hid[there].astype(f32) + back).astype(bf16)
        gt_out(i).start()

    def out_copy(b, slot):
        return pltpu.make_async_copy(gbuf.at[slot], output.at[rows_of(b, TB)], loc.at[2])

    def out_half(i):
        return pltpu.make_async_copy(
            gbuf.at[(blocks - 1) % 2, rows_of(i)], output.at[rows_of(i)], loc.at[5 + i]
        )

    groups = ((0, 1), (2,), (3,))
    spans = (768, 768, 768, 256)
    wants = [(y, 1 - x, x_dev), (1 - y, x, y_dev), (1 - y, 1 - x, diag)]

    def take(c, dest):
        some = pl.ds(pl.multiple_of(dest * 96, 96), 96)
        return dw[c, some] if c < 3 else dwp[some]

    def span_of(ref, g, *rest):
        if g == 0:
            return ref.at[(slice(0, 2),) + rest]
        return ref.at[(g + 1,) + rest + ((slice(None), slice(0, 256)) if g == 2 else ())]

    def twin_sum(g):
        every = (slice(None), slice(None))
        return remote(
            span_of(w_out, g, *every, 1 - k), span_of(w_fc, g, *every, 0), d_s.at[g], d_r.at[g], twin
        )

    def to_owner(g, i):
        yy, xx, device = wants[i]
        n = 3 + 3 * i + g
        return remote(
            span_of(w_out, g, yy, xx, k),
            span_of(w_fc, g, i // 2, i % 2, 1),
            d_s.at[n],
            d_r.at[n],
            device,
        )

    def give_twin(g):
        for yy in range(2):
            for xx in range(2):
                for c in groups[g]:
                    w_out[c, yy, xx, 1 - k, :, : spans[c]] = take(
                        c, yy * 4 + xx * 2 + 1 - k
                    ).astype(bf16)

    def give_owners(g):
        twin_sum(g).wait_recv()
        for i, (yy, xx, _) in enumerate(wants):
            for c in groups[g]:
                w_out[c, yy, xx, k, :, : spans[c]] = (
                    take(c, yy * 4 + xx * 2 + k) + w_fc[c, yy, xx, 0, :, : spans[c]].astype(f32)
                ).astype(bf16)
            to_owner(g, i).start()

    def result(c):
        some = pl.ds(pl.multiple_of(d * 96, 96), 96)
        return (
            pltpu.make_async_copy(dw.at[c, some], dw_out.at[c], loc.at[7 + c])
            if c < 3
            else pltpu.make_async_copy(dwp.at[some], dwp_out, loc.at[10])
        )

    def own_sum(g):
        for i in range(3):
            to_owner(g, i).wait_recv()
        some = pl.ds(pl.multiple_of(d * 96, 96), 96)
        for c in groups[g]:
            value = take(c, d) + w_fc[c, y, x, 0, :, : spans[c]].astype(f32)
            for i in range(3):
                value = value + w_fc[c, i // 2, i % 2, 1, :, : spans[c]].astype(f32)
            if c < 3:
                dw[c, some] = value
            else:
                dwp[some] = value
            result(c).start()

    def make_block(size):
        big = size == TB
        all_rows = slice(0, size)

        def block(t, _):
            b = blocks - 1 - t if big else 0
            i_last = 2 * b + 1 if big else 1 - t
            row = b * TB if big else (1 - t) * QB
            off = 0 if big else (1 - t) * QB
            rows = pl.ds(pl.multiple_of(row, QB), size)
            slot = lax.rem(t, 2) if big else (blocks - 1) % 2
            g_rows = pl.ds(pl.multiple_of(off, QB), size)

            def part_of(r, step):
                return pl.ds(pl.multiple_of(off + r * step, step), step)

            @pl.when((t >= 0) if big else (t == 0))
            def _():
                pltpu.make_async_copy(
                    grads.at[rows_of(b, TB)], gbuf.at[slot], loc.at[slot]
                ).wait()

            if big:

                @pl.when(t >= 1)
                def _():
                    out_copy(b + 1, 1 - slot).wait()

                pltpu.make_async_copy(
                    grads.at[rows_of(b - 1, TB)], gbuf.at[1 - slot], loc.at[1 - slot]
                ).start()

            for s in range(4):

                @pl.when((end | (b == blocks - 1)) & (m != s) & ((t >= 0) if big else (t == 0)))
                def _():
                    a_wait(b, s)

            def head(s, _):
                third = rows_all[s, b, 2 * QB :].astype(f32)
                turned_third = pltpu.roll(third, 64, 1)
                if big:
                    third = jnp.concatenate([third, turned_third], axis=0)
                else:
                    third = jnp.where(t == 0, turned_third, third)
                lane = lax.broadcasted_iota(jnp.int32, third.shape, 1)
                third = jnp.where(lane < 64, third, 0.0).astype(bf16)
                left = jnp.concatenate([rows_all[s, b, g_rows], third], axis=1)
                oacc[all_rows] += mm(left, flat_pr[s], NT)
                return 0

            oacc[all_rows] = tokens[rows].astype(f32) + par[4:5]
            lax.fori_loop(0, 4, head, 0)

            def second(r, _):
                some = rows_of(r, RB)
                hidden = oacc[some]
                unit, inverse = norm(hidden)
                normed[some] = unit
                inv[some] = inverse
                act[some] = (unit * par[2:3] + par[3:4]).astype(bf16)
                oacc[some] = hidden + par[5:6]
                gacc[some] = jnp.zeros_like(hidden)
                return 0

            lax.fori_loop(0, size // RB, second, 0)

            def slab(s, _):
                if big:

                    @pl.when(t == 0)
                    def _():
                        for c in range(2):
                            hop(s, c, 2).wait_recv()

                def units(r, _):
                    some = rows_of(r)
                    pre = mm(act[some], flat_fc[s]) + fcb[s]
                    back = mm(gbuf[slot, part_of(r, QB)], flat_out[s])
                    square = pre * pre
                    tangent = jnp.tanh(pre * (GELU_C + (GELU_C * 0.044715) * square))
                    half = 0.5 * pre
                    fired[some] = (half + half * tangent).astype(bf16)
                    slope = (0.5 + 0.5 * tangent) + half * (1.0 - tangent * tangent) * (
                        GELU_C + (3.0 * GELU_C * 0.044715) * square
                    )
                    preg[some] = (back * slope).astype(bf16)
                    return 0

                lax.fori_loop(0, size // QB, units, 0)
                oacc[all_rows] += mm(fired[all_rows], flat_out[s], NT)
                gacc[all_rows] += mm(preg[all_rows], flat_fc[s], NT)

                @pl.when(s == m)
                def _():
                    def outer(r, _):
                        some = rows_of(r)
                        dw[0, some] += mm(act[all_rows, some], preg[all_rows], TN)
                        dw[1, some] += mm(gbuf[slot, g_rows, some], fired[all_rows], TN)
                        return 0

                    lax.fori_loop(0, 3, outer, 0)
                    pgrad[6:7] += jnp.sum(preg[all_rows].astype(f32), axis=0, keepdims=True)

                def at(when, do, *what):
                    @pl.when(when)
                    def _():
                        for item in what:
                            do(item)

                if big:

                    @pl.when((t == 0) & (s == 0))
                    def _():
                        advance(2, 2)

                    @pl.when((t == 0) & (s == jnp.where(m == 3, 1, 2)))
                    def _():
                        advance(3, 2)

                    @pl.when((t == 0) & (s == 2))
                    def _():
                        a_step(2, 1)
                        a_step(1, 1)

                    j = 4 * b + 4
                    at((t >= 1) & (s == 0), stage_two, j + 3, j + 2)
                    at((t >= 1) & (s == 2), stage_two, j + 1, j)
                    at((t >= 1) & (s == 3), stage_three, j + 3, j + 2)
                    at((t >= 2) & (s == 1), stage_four, j + 7, j + 6, j + 5, j + 4)
                else:
                    at((t == 0) & (s == 1), stage_two, 7, 6)
                    at((t == 0) & (s == 3), stage_two, 5)
                    at((t == 0) & (s == 2), stage_four, 11, 10, 9, 8)
                    at((t == 1) & (s == 1), stage_three, 5)
                    at((t == 1) & (s == 3), stage_three, 4)
                return 0

            lax.fori_loop(0, 4, slab, 0)
            if big:

                @pl.when(t == 0)
                def _():
                    a_step(2, 2)
                    a_step(0, 1)

            else:

                @pl.when(t == 1)
                def _():
                    for c in range(3):
                        for s in range(4):
                            passed_on(*z_args(c, s))
                            for stage in range(3):
                                hop(s, c, stage).wait_send()
                    for device in (x_dev, y_dev, diag, twin):
                        pl.semaphore_signal(free, inc=1, device_id=device, device_id_type=MESH)
                    give_twin(0)
                    pl.semaphore_wait(free, 4)
                    twin_sum(0).start()

            def rejoin(r, _):
                some = rows_of(r, RB)
                there = pl.ds(pl.multiple_of(row + r * RB, RB), RB)
                grad = gbuf[slot, part_of(r, RB)].astype(f32)
                through, unit = gacc[some], normed[some]
                pgrad[5:6] += jnp.sum(grad, axis=0, keepdims=True)
                pgrad[2:3] += jnp.sum(through * unit, axis=0, keepdims=True)
                pgrad[3:4] += jnp.sum(through, axis=0, keepdims=True)
                branch = (grad + norm_back(through, par[2:3], unit, inv[some])).astype(bf16)
                hid[there] = branch
                pgrad[4:5] += jnp.sum(branch.astype(f32), axis=0, keepdims=True)
                gbuf[slot, part_of(r, RB)] = oacc[some].astype(bf16)
                return 0

            lax.fori_loop(0, size // RB, rejoin, 0)
            if big:
                out_copy(b, slot).start()
            else:
                out_half(1 - t).start()
            dwp[...] += mm(hid[rows], orow[rows], TN)
            if not big:

                @pl.when(t == 1)
                def _():
                    give_twin(2)
                    twin_sum(2).start()
                    give_owners(0)

            rowg[all_rows] = mm(hid[rows], flat_pr[m]).astype(bf16)

            for n in range(size // QB):
                i = i_last - n
                some = slice(size - QB * (n + 1), size - QB * n)
                attend_block_back(
                    i, rowg[some], qr, kr, vr, turned, orow, starts, lse, dk, dv, qs, gs, dqt
                )
                stacked[some, :WIDE] = (dqt[...].T * SCALE).astype(bf16)
                stacked[some, WIDE : 2 * WIDE] = dk[rows_of(i)].astype(bf16)
                stacked[some, 2 * WIDE :] = dv[rows_of(i)].astype(bf16)
                whole = mm(stacked[some], flat_qkv[...], NT).astype(bf16)
                part[2 * i] = whole[:RB]
                part[2 * i + 1] = whole[RB:]

                @pl.when(end)
                def _():
                    hop_a(2 * i + 1).start()
                    hop_a(2 * i).start()

                if big and n == 0:

                    @pl.when(t >= 1)
                    def _():
                        stage_three(4 * b + 5)
                        stage_three(4 * b + 4)

                if not big:

                    @pl.when(t == 0)
                    def _():
                        stage_two(4)
                        stage_three(7)
                        stage_three(6)

                    @pl.when(t == 1)
                    def _():
                        stage_two(3)
                        stage_two(2)

            pgrad[7:8] += jnp.sum(stacked[all_rows].astype(f32), axis=0, keepdims=True)

            def again(r, _):
                unit, _ = norm(tokens[pl.ds(pl.multiple_of(row + r * RB, RB), RB)].astype(f32))
                act[rows_of(r, RB)] = (unit * par[0:1] + par[1:2]).astype(bf16)
                grad = part[row // RB + r].astype(f32)
                pgrad[0:1] += jnp.sum(grad * unit, axis=0, keepdims=True)
                pgrad[1:2] += jnp.sum(grad, axis=0, keepdims=True)
                return 0

            lax.fori_loop(0, size // RB, again, 0)

            def outer(r, _):
                some = rows_of(r)
                dw[2, some] += mm(act[all_rows, some], stacked[all_rows], TN)
                return 0

            lax.fori_loop(0, 3, outer, 0)
            if big:

                @pl.when(t == 0)
                def _():
                    a_step(1, 2)

                @pl.when(t == 1)
                def _():
                    a_step(0, 2)

            return 0

        return block

    lax.fori_loop(0, blocks - 1, make_block(TB), 0)
    lax.fori_loop(0, 2, make_block(QB), 0)

    zg_send = [
        remote(zgbuf.at[m], zgbuf.at[m], zg_s.at[o], zg_r.at[m], line[o]) for o in range(1, 4)
    ]
    zgbuf[m] = pgrad[...]
    for copy in zg_send:
        copy.start()
    give_twin(1)
    twin_sum(1).start()
    stage_three(3)
    stage_three(2)
    for s in range(4):

        @pl.when(m != s)
        def _():
            remote(zgbuf.at[s], zgbuf.at[s], zg_s.at[1], zg_r.at[s], line[1]).wait_recv()

    pgrad[0:2] = zgbuf[0, 0:2] + zgbuf[1, 0:2] + zgbuf[2, 0:2] + zgbuf[3, 0:2]
    g_send = [
        remote(pgrad, pgbuf.at[o], g_s.at[o], g_r.at[o], plane[o]) for o in range(1, 8)
    ]
    for copy in g_send:
        copy.start()
    give_owners(2)
    give_owners(1)
    for i in (7, 6, 5, 4):
        stage_four(i)
    stage_two(1)
    stage_two(0)
    total = pgrad[...]
    for copy in g_send:
        copy.wait_recv()
    for o in range(1, 8):
        total = total + pgbuf[o]
    pg_out[...] = total
    stage_three(1)
    stage_three(0)
    stage_four(3)
    stage_four(2)
    own_sum(0)
    own_sum(2)
    own_sum(1)
    stage_four(1)
    stage_four(0)

    for c in range(4):
        result(c).wait()
    for copy in g_send + zg_send + q_send + q_pass + p_send:
        copy.wait_send()
    for g in range(3):
        twin_sum(g).wait_send()
        for i in range(3):
            to_owner(g, i).wait_send()
    out_copy(1, (blocks - 2) % 2).wait()
    out_half(1).wait()
    out_half(0).wait()

    def leave(i, _):
        gt_out(i).wait()

        @pl.when(end)
        def _():
            hop_a(i).wait_send()

        @pl.when(inner)
        def _():
            hop_b(i).wait_send()
            hop_c(i).wait_send()

        return 0

    lax.fori_loop(0, count // RB, leave, 0)
    for o in range(1, 4):
        direct(blocks - 1, o).wait_send()
    for b in range(blocks - 1):
        for s in range(4):
            passed_on(*a_args(b, s))


def whole_block(tokens, out_grad, starts, fc_own, out_own, pr_own, qkv_own, par_own):
    count = tokens.shape[0]
    blocks, subs = count // TB, count // QB
    any_space = pl.BlockSpec(memory_space=pl.ANY)
    dma = pltpu.SemaphoreType.DMA
    return pl.pallas_call(
        whole_kernel,
        out_shape=(
            jax.ShapeDtypeStruct((count, 768), bf16),
            jax.ShapeDtypeStruct((count, 768), bf16),
            jax.ShapeDtypeStruct((3, 96, 768), f32),
            jax.ShapeDtypeStruct((96, WIDE), f32),
            jax.ShapeDtypeStruct((8, 768), f32),
        ),
        in_specs=[VMEM, any_space] + [VMEM] * 6,
        out_specs=(any_space, any_space, any_space, any_space, VMEM),
        scratch_shapes=[
            pltpu.VMEM((4, 2, 2, 2, 96, 768), bf16),
            pltpu.VMEM((4, 2, 2, 2, 96, 768), bf16),
            pltpu.VMEM((4, 2, 2, 2, 96, 256), bf16),
            pltpu.VMEM((2, 2, 2, 96, 768), bf16),
            pltpu.VMEM((8, 16, 768), bf16),
            pltpu.VMEM((16, 768), f32),
            pltpu.VMEM((4, 1, 768), f32),
            pltpu.VMEM((count, WIDE), bf16),
            pltpu.VMEM((count, WIDE), bf16),
            pltpu.VMEM((count, WIDE), bf16),
            pltpu.VMEM((WIDE, count), bf16),
            pltpu.VMEM((count, WIDE), bf16),
            pltpu.VMEM((4, blocks, 3 * QB, 128), bf16),
            pltpu.VMEM((subs, 1, HPD * QB), f32),
            pltpu.VMEM((HPD * QB, WIDE), bf16),
            pltpu.VMEM((HPD * QB, WIDE), bf16),
            pltpu.VMEM((HD, HPD * QB), f32),
            pltpu.VMEM((WIDE, QB), f32),
            pltpu.VMEM((count, WIDE), f32),
            pltpu.VMEM((count, WIDE), f32),
            pltpu.VMEM((2, TB, 768), bf16),
            pltpu.VMEM((TB, 768), f32),
            pltpu.VMEM((TB, 1), f32),
            pltpu.VMEM((TB, 768), bf16),
            pltpu.VMEM((TB, 768), f32),
            pltpu.VMEM((TB, 768), f32),
            pltpu.VMEM((TB, 768), bf16),
            pltpu.VMEM((TB, 768), bf16),
            pltpu.VMEM((TB, WIDE), bf16),
            pltpu.VMEM((TB, 768), bf16),
            pltpu.VMEM((count, 768), bf16),
            pltpu.VMEM((3, 768, 768), f32),
            pltpu.VMEM((768, 256), f32),
            pltpu.VMEM((8, 768), f32),
            pltpu.VMEM((8, 8, 768), f32),
            pltpu.VMEM((4, 8, 768), f32),
            pltpu.VMEM((count // RB, RB, 768), bf16),
            pltpu.VMEM((count // RB, RB, 768), bf16),
            pltpu.VMEM((count // RB, RB, 768), bf16),
            dma((7,)),
            dma((7,)),
            dma((8,)),
            dma((8,)),
            dma((3, 4, 2)),
            dma((3, 4)),
            dma((3, 3, 4)),
            dma((3, 3, 4)),
            dma((4,)),
            dma((blocks, 4, 2)),
            dma((blocks, 4)),
            dma((3, count // RB)),
            dma((3, count // RB)),
            dma((12,)),
            dma((12,)),
            dma((4,)),
            dma((4,)),
            dma((8 + count // RB,)),
            dma((8,)),
            dma((11,)),
            pltpu.SemaphoreType.REGULAR,
        ],
        compiler_params=pltpu.CompilerParams(
            collective_id=0, has_side_effects=True, vmem_limit_bytes=63 * 2**20
        ),
    )(tokens, out_grad, starts, fc_own, out_own, pr_own, qkv_own, par_own)


def per_device_whole(
    tokens,
    lengths,
    first_gain,
    first_shift,
    qkv_weight,
    qv_bias,
    proj_weight,
    proj_bias,
    second_gain,
    second_shift,
    fc_weight,
    fc_bias,
    out_weight,
    out_bias,
    out_grad,
):
    d = lax.axis_index("dp")
    starts = segment_starts(lengths[0], tokens.shape[0])
    pr_own = jnp.concatenate([proj_weight.T, fc_bias.T, jnp.zeros((96, 63), bf16)], axis=1)
    out_own = out_weight.T
    qkv_own = jnp.pad(qkv_weight, ((0, 0), (0, 0), (0, WIDE - 192)))
    qkv_own = jnp.moveaxis(qkv_own, 0, 1).reshape(96, 3 * WIDE)
    vectors = jnp.stack(
        [first_gain, first_shift, second_gain, second_shift, proj_bias, out_bias, fc_bias[0]]
    )
    par_own = jnp.zeros((16, 768), bf16)
    par_own = lax.dynamic_update_slice(par_own, vectors, (0, 96 * d))
    par_own = lax.dynamic_update_slice(par_own, qv_bias[0], (7, 24 * d))
    par_own = lax.dynamic_update_slice(par_own, qv_bias[1], (7, 2 * WIDE + 24 * d))
    output, grad_tokens, dw, dwp, pg = whole_block(
        tokens, out_grad, starts, fc_weight, out_own, pr_own, qkv_own, par_own
    )
    vec = lax.dynamic_slice(pg, (0, 96 * d), (7, 96))
    qv = jnp.concatenate(
        [
            lax.dynamic_slice(pg, (7, 24 * d), (1, 24)),
            lax.dynamic_slice(pg, (7, 2 * WIDE + 24 * d), (1, 24)),
        ]
    )[:, None, :]
    qkv_grad = jnp.moveaxis(dw[2].reshape(96, 3, WIDE)[:, :, :192], 1, 0)
    return (
        output,
        grad_tokens,
        vec[0],
        vec[1],
        qkv_grad,
        qv,
        dwp[:, :192].T,
        vec[4],
        vec[2],
        vec[3],
        dw[0],
        vec[6][None],
        dw[1].T,
        vec[5],
    )


def solution(mesh):
    placed = (
        P("dp", None),
        P("dp", None),
        P("dp"),
        P("dp"),
        P(None, "dp", "mp"),
        P(None, "mp", "dp"),
        P("mp", "dp"),
        P("dp"),
        P("dp"),
        P("dp"),
        P("dp", "mp"),
        P("mp", "dp"),
        P("mp", "dp"),
        P("dp"),
        P("dp", None),
    )
    return jax.shard_map(
        per_device_whole if dict(mesh.shape) == {"dp": 8, "mp": 4} else per_device,
        mesh=mesh,
        in_specs=placed,
        out_specs=(
            P("dp", None),
            P("dp", None),
            P("dp"),
            P("dp"),
            P(None, "dp", "mp"),
            P(None, "mp", "dp"),
            P("mp", "dp"),
            P("dp"),
            P("dp"),
            P("dp"),
            P("dp", "mp"),
            P("mp", "dp"),
            P("mp", "dp"),
            P("dp"),
        ),
        check_vma=False,
    )
```

```python
import functools

import jax
import jax.numpy as jnp
from jax import lax
from jax.experimental import pallas as pl
from jax.experimental.pallas import tpu as pltpu
from jax.sharding import PartitionSpec as P

HD = 64
HPD = 3
WIDE = 256
MAXLEN = 1024
QB = 256
BAND = MAXLEN // QB


EPS = 1e-05
SCALE = 0.125
NEG = -1e30
GELU_C = 0.7978845608028654
NN = (((1,), (0,)), ((), ()))
NT = (((1,), (1,)), ((), ()))
TN = (((0,), (0,)), ((), ()))
f32 = jnp.float32
bf16 = jnp.bfloat16


def mm(left, right, dims=NN):
    return lax.dot_general(left, right, dims, preferred_element_type=f32)


def split_up(shard, dim, size):
    before, after = (shard.shape[:dim], shard.shape[dim + 1 :])
    return jnp.moveaxis(shard.reshape(*before, size, -1, *after), dim, 0)


def summed_on_arrival(shard, axis, dim):
    size = lax.axis_size(axis)
    pieces = lax.all_to_all(split_up(shard, dim, size), axis, 0, 0, tiled=True)
    return jnp.sum(pieces.astype(jnp.float32), axis=0)


def norm_parts(values):
    mean = jnp.mean(values, axis=-1, keepdims=True)
    centred = values - mean
    inverse = lax.rsqrt(jnp.mean(centred * centred, axis=-1, keepdims=True) + EPS)
    return (centred * inverse, inverse)


def norm_back(grad, gain, normed, inverse):
    scaled = grad * gain
    return inverse * (
        scaled
        - jnp.mean(scaled, axis=-1, keepdims=True)
        - normed * jnp.mean(scaled * normed, axis=-1, keepdims=True)
    )


def gelu_tanh(values):
    return 0.5 * values * (1.0 + jnp.tanh(GELU_C * (values + 0.044715 * values * values * values)))


def gelu_slope(values):
    inner = GELU_C * (values + 0.044715 * values * values * values)
    tangent = jnp.tanh(inner)
    return 0.5 * (1.0 + tangent) + 0.5 * values * (1.0 - tangent * tangent) * GELU_C * (
        1.0 + 3.0 * 0.044715 * values * values
    )


def segment_starts(lengths_row, count):
    ends = jnp.cumsum(lengths_row)
    places = jnp.arange(count, dtype=jnp.int32)
    return jnp.max(jnp.where(ends[None, :] <= places[:, None], ends[None, :], 0), axis=1)[None, :]


def rows_of(index, size=QB):
    return pl.ds(pl.multiple_of(index * size, size), size)


def tile_heads(x):
    return jnp.concatenate([x] * HPD, axis=1)


def allowed_keys(i, j, start_ref):
    start = start_ref[:, rows_of(i)]
    key = lax.broadcasted_iota(jnp.int32, (QB, QB), 0)
    query = lax.broadcasted_iota(jnp.int32, (QB, QB), 1)
    return (key >= start - j * QB) & (key <= query + (i - j) * QB)


def stack_heads(x):
    lane = lax.broadcasted_iota(jnp.int32, x.shape, 1)
    return jnp.concatenate(
        [
            jnp.where((lane >= HD * h) & (lane < HD * h + HD), x, jnp.zeros_like(x))
            for h in range(HPD)
        ],
        axis=0,
    )


def attend_block(i, q_ref, k_ref, vt_ref, start_ref, lse_ref, o_ref, qs, acc):
    rows = rows_of(i)
    qs[...] = stack_heads(q_ref[rows])
    acc[...] = jnp.zeros_like(acc)

    def step(jj, carry):
        biggest, total = carry
        j = i - jj
        keys = rows_of(j)
        s = mm(k_ref[keys], qs[...], NT)
        s = jnp.where(tile_heads(allowed_keys(i, j, start_ref)), s, NEG)
        new = jnp.maximum(biggest, jnp.max(s, axis=0, keepdims=True))
        p = jnp.exp(s - new)
        shrink = jnp.exp(biggest - new)
        total = total * shrink + jnp.sum(p, axis=0, keepdims=True)
        p = p.astype(bf16)
        for h in range(HPD):
            cols = slice(QB * h, QB * h + QB)
            acc[:, cols] = acc[:, cols] * shrink[:, cols] + mm(
                vt_ref[HD * h : HD * h + HD, keys], p[:, cols]
            )
        return new, total

    biggest, total = lax.fori_loop(
        0,
        jnp.minimum(i, BAND) + 1,
        step,
        (jnp.full((1, HPD * QB), NEG, f32), jnp.zeros((1, HPD * QB), f32)),
    )
    lse_ref[i] = biggest + jnp.log(total)
    inverse = 1.0 / total
    out = jnp.concatenate(
        [acc[:, QB * h : QB * h + QB] * inverse[:, QB * h : QB * h + QB] for h in range(HPD)]
        + [jnp.zeros((WIDE - HPD * HD, QB), f32)],
        axis=0,
    )
    o_ref[rows] = out.T.astype(bf16)


def attend_block_back(i, grad, q_ref, k_ref, v_ref, kt_ref, o_ref, start_ref, lse_ref, dk, dv, qs, gs, dqt):
    rows = rows_of(i)
    qs[...] = stack_heads(q_ref[rows])
    gs[...] = stack_heads(grad)
    both = (grad.astype(f32) * o_ref[rows].astype(f32)).T
    delta = jnp.concatenate(
        [jnp.sum(both[HD * h : HD * h + HD], axis=0, keepdims=True) for h in range(HPD)], axis=1
    )
    lse = lse_ref[i]
    dqt[...] = jnp.zeros_like(dqt)

    def step(jj, _):
        j = i - jj
        keys = rows_of(j)
        s = mm(k_ref[keys], qs[...], NT)
        s = jnp.where(tile_heads(allowed_keys(i, j, start_ref)), s, NEG)
        p = jnp.exp(s - lse)
        dp = mm(v_ref[keys], gs[...], NT)
        ds = (p * (dp - delta)).astype(bf16)
        p = p.astype(bf16)
        dv[keys] += mm(p, gs[...])
        dk[keys] += mm(ds, qs[...])
        for h in range(HPD):
            dqt[HD * h : HD * h + HD] += mm(
                kt_ref[HD * h : HD * h + HD, keys], ds[:, QB * h : QB * h + QB]
            )
        return 0

    lax.fori_loop(0, jnp.minimum(i, BAND) + 1, step, 0)


def forward_kernel(q_ref, k_ref, v_ref, start_ref, o_ref, lse_ref, vt, qs, acc):
    blocks = q_ref.shape[0] // QB

    def turn(i, _):
        vt[:, rows_of(i)] = v_ref[rows_of(i)].T
        return 0

    lax.fori_loop(0, blocks, turn, 0)

    def block(i, _):
        attend_block(i, q_ref, k_ref, vt, start_ref, lse_ref, o_ref, qs, acc)
        return 0

    lax.fori_loop(0, blocks, block, 0)


def backward_kernel(
    q_ref, k_ref, v_ref, o_ref, g_ref, start_ref, lse_ref, d_ref, kt, qs, gs, dqt, dk, dv
):
    blocks = q_ref.shape[0] // QB

    def turn(i, _):
        kt[:, rows_of(i)] = k_ref[rows_of(i)].T
        return 0

    lax.fori_loop(0, blocks, turn, 0)
    dk[...] = jnp.zeros_like(dk)
    dv[...] = jnp.zeros_like(dv)

    def block(turn_of, _):
        i = blocks - 1 - turn_of
        rows = rows_of(i)
        attend_block_back(
            i, g_ref[rows], q_ref, k_ref, v_ref, kt, o_ref, start_ref, lse_ref, dk, dv, qs, gs, dqt
        )
        d_ref[0, rows] = (dqt[...].T * SCALE).astype(bf16)
        d_ref[1, rows] = dk[rows].astype(bf16)
        d_ref[2, rows] = dv[rows].astype(bf16)
        return 0

    lax.fori_loop(0, blocks, block, 0)


VMEM = pl.BlockSpec(memory_space=pltpu.VMEM)
LIMIT = pltpu.CompilerParams(vmem_limit_bytes=40 * 2**20)


def attend_forward(query, keys, values, starts):
    count = query.shape[0]
    return pl.pallas_call(
        forward_kernel,
        out_shape=(
            jax.ShapeDtypeStruct((count, WIDE), bf16),
            jax.ShapeDtypeStruct((count // QB, 1, HPD * QB), f32),
        ),
        in_specs=[VMEM] * 4,
        out_specs=(VMEM, VMEM),
        scratch_shapes=[
            pltpu.VMEM((WIDE, count), bf16),
            pltpu.VMEM((HPD * QB, WIDE), bf16),
            pltpu.VMEM((HD, HPD * QB), f32),
        ],
        compiler_params=LIMIT,
    )(query, keys, values, starts)


def attend_backward(query, keys, values, rows, grad, starts, lse):
    count = query.shape[0]
    return pl.pallas_call(
        backward_kernel,
        out_shape=jax.ShapeDtypeStruct((3, count, WIDE), bf16),
        in_specs=[VMEM] * 7,
        out_specs=VMEM,
        scratch_shapes=[
            pltpu.VMEM((WIDE, count), bf16),
            pltpu.VMEM((HPD * QB, WIDE), bf16),
            pltpu.VMEM((HPD * QB, WIDE), bf16),
            pltpu.VMEM((WIDE, QB), f32),
            pltpu.VMEM((count, WIDE), f32),
            pltpu.VMEM((count, WIDE), f32),
        ],
        compiler_params=LIMIT,
    )(query, keys, values, rows, grad, starts, lse)


def per_device(
    tokens,
    lengths,
    first_gain,
    first_shift,
    qkv_weight,
    qv_bias,
    proj_weight,
    proj_bias,
    second_gain,
    second_shift,
    fc_weight,
    fc_bias,
    out_weight,
    out_bias,
    out_grad,
):
    count = tokens.shape[0]
    starts = segment_starts(lengths[0], count)
    gain_one, shift_one, qkv_all, qv_all, proj_all, proj_bias_all = (
        lax.all_gather(first_gain, "dp", axis=0, tiled=True),
        lax.all_gather(first_shift, "dp", axis=0, tiled=True),
        lax.all_gather(qkv_weight, "dp", axis=1, tiled=True),
        lax.all_gather(qv_bias, "dp", axis=2, tiled=True),
        lax.all_gather(proj_weight, "dp", axis=1, tiled=True),
        lax.all_gather(proj_bias, "dp", axis=0, tiled=True),
    )
    gain_one_f = gain_one.astype(jnp.float32)
    xin = tokens.astype(jnp.float32)
    normed_one, inverse_one = norm_parts(xin)
    act_one = (normed_one * gain_one_f + shift_one.astype(jnp.float32)).astype(jnp.bfloat16)
    projected = jnp.einsum("td,cde->cte", act_one, qkv_all, preferred_element_type=jnp.float32)
    width = qkv_all.shape[2]
    wide = ((0, 0), (0, WIDE - width))
    query = jnp.pad(
        (projected[0] + qv_all[0, 0].astype(f32)).astype(bf16) * jnp.asarray(SCALE, bf16), wide
    )
    keys = jnp.pad(projected[1].astype(bf16), wide)
    values = jnp.pad((projected[2] + qv_all[1, 0].astype(f32)).astype(bf16), wide)
    wide_rows, lse = attend_forward(query, keys, values, starts)
    flat_rows = wide_rows[:, :width]
    gain_two, shift_two, fc_all, fc_bias_all, out_all, out_bias_all = (
        lax.all_gather(second_gain, "dp", axis=0, tiled=True),
        lax.all_gather(second_shift, "dp", axis=0, tiled=True),
        lax.all_gather(fc_weight, "dp", axis=0, tiled=True),
        lax.all_gather(fc_bias, "dp", axis=1, tiled=True),
        lax.all_gather(out_weight, "dp", axis=1, tiled=True),
        lax.all_gather(out_bias, "dp", axis=0, tiled=True),
    )
    gain_two_f = gain_two.astype(jnp.float32)
    shift_two_f = shift_two.astype(jnp.float32)
    branch_one = lax.psum(
        jnp.dot(flat_rows, proj_all, preferred_element_type=jnp.float32).astype(jnp.bfloat16), "mp"
    ).astype(jnp.float32)
    hidden_one = xin + branch_one + proj_bias_all.astype(jnp.float32)
    normed_two, inverse_two = norm_parts(hidden_one)
    act_two = (normed_two * gain_two_f + shift_two_f).astype(jnp.bfloat16)
    pre = jnp.dot(act_two, fc_all, preferred_element_type=jnp.float32) + fc_bias_all[0].astype(
        jnp.float32
    )
    fired = gelu_tanh(pre).astype(jnp.bfloat16)
    branch_two = lax.psum(
        jnp.dot(fired, out_all, preferred_element_type=jnp.float32).astype(jnp.bfloat16), "mp"
    ).astype(jnp.float32)
    output = (hidden_one + branch_two + out_bias_all.astype(jnp.float32)).astype(jnp.bfloat16)
    grad_out = out_grad.astype(jnp.float32)
    out_bias_grad = jnp.sum(out_grad, axis=0, dtype=jnp.float32)
    out_weight_grad = jnp.einsum("tf,td->fd", fired, out_grad, preferred_element_type=jnp.float32)
    fired_grad = jnp.einsum("td,fd->tf", out_grad, out_all, preferred_element_type=jnp.float32)
    pre_grad = (fired_grad * gelu_slope(pre)).astype(jnp.bfloat16)
    fc_bias_grad = jnp.sum(pre_grad, axis=0, dtype=jnp.float32)
    fc_weight_grad = jnp.einsum("td,tf->df", act_two, pre_grad, preferred_element_type=jnp.float32)
    act_two_grad = lax.psum(
        jnp.einsum("tf,df->td", pre_grad, fc_all, preferred_element_type=jnp.float32).astype(
            jnp.bfloat16
        ),
        "mp",
    ).astype(jnp.float32)
    gain_two_grad = jnp.sum(act_two_grad * normed_two, axis=0)
    shift_two_grad = jnp.sum(act_two_grad, axis=0)
    hidden_grad = grad_out + norm_back(act_two_grad, gain_two_f, normed_two, inverse_two)
    branch_grad = hidden_grad.astype(jnp.bfloat16)
    proj_bias_grad = jnp.sum(branch_grad, axis=0, dtype=jnp.float32)
    proj_weight_grad = jnp.einsum(
        "te,td->ed", flat_rows, branch_grad, preferred_element_type=jnp.float32
    )
    rows_grad = jnp.einsum(
        "td,ed->te", branch_grad, proj_all, preferred_element_type=jnp.float32
    ).astype(jnp.bfloat16)
    stacked = attend_backward(
        query, keys, values, wide_rows, jnp.pad(rows_grad, wide), starts, lse
    )[:, :, :width]
    qkv_grad = jnp.einsum("td,cte->cde", act_one, stacked, preferred_element_type=jnp.float32)
    bias_sums = jnp.sum(stacked, axis=1, dtype=jnp.float32)
    qv_grad = jnp.stack([bias_sums[0], bias_sums[2]])[:, None, :]
    act_one_grad = lax.psum(
        jnp.einsum("cte,cde->td", stacked, qkv_all, preferred_element_type=jnp.float32).astype(
            jnp.bfloat16
        ),
        "mp",
    ).astype(jnp.float32)
    gain_one_grad = jnp.sum(act_one_grad * normed_one, axis=0)
    shift_one_grad = jnp.sum(act_one_grad, axis=0)
    input_grad = (
        hidden_grad + norm_back(act_one_grad, gain_one_f, normed_one, inverse_one)
    ).astype(jnp.bfloat16)
    mlp_grads = (
        lax.psum_scatter(gain_two_grad, "dp", scatter_dimension=0, tiled=True),
        lax.psum_scatter(shift_two_grad, "dp", scatter_dimension=0, tiled=True),
        lax.psum_scatter(fc_weight_grad, "dp", scatter_dimension=0, tiled=True),
        lax.psum_scatter(fc_bias_grad[None], "dp", scatter_dimension=1, tiled=True),
        lax.psum_scatter(out_weight_grad, "dp", scatter_dimension=1, tiled=True),
        lax.psum_scatter(out_bias_grad, "dp", scatter_dimension=0, tiled=True),
    )
    attn_grads = (
        summed_on_arrival(gain_one_grad.astype(jnp.bfloat16), "dp", 0),
        summed_on_arrival(shift_one_grad.astype(jnp.bfloat16), "dp", 0),
        summed_on_arrival(qkv_grad.astype(jnp.bfloat16), "dp", 1),
        summed_on_arrival(qv_grad.astype(jnp.bfloat16), "dp", 2),
        summed_on_arrival(proj_weight_grad.astype(jnp.bfloat16), "dp", 1),
        summed_on_arrival(proj_bias_grad.astype(jnp.bfloat16), "dp", 0),
    )
    return (
        output,
        input_grad,
        attn_grads[0],
        attn_grads[1],
        attn_grads[2],
        attn_grads[3],
        attn_grads[4],
        attn_grads[5],
        mlp_grads[0],
        mlp_grads[1],
        mlp_grads[2],
        mlp_grads[3],
        mlp_grads[4],
        mlp_grads[5],
    )


MESH = pl.DeviceIdType.MESH
TB = 512
RB = 128


def norm(values):
    mean = jnp.mean(values, axis=-1, keepdims=True)
    centred = values - mean
    inverse = lax.rsqrt(jnp.mean(centred * centred, axis=-1, keepdims=True) + EPS)
    return centred * inverse, inverse


def remote(src, dst, send, recv, device):
    return pltpu.make_async_remote_copy(
        src_ref=src, dst_ref=dst, send_sem=send, recv_sem=recv, device_id=device, device_id_type=MESH
    )


def whole_kernel(
    tokens,
    grads,
    lengths,
    fc_own,
    out_own,
    pr_own,
    fb_own,
    qkv_own,
    gain_one,
    shift_one,
    gain_two,
    shift_two,
    proj_bias,
    out_bias,
    qv_own,
    output,
    grad_tokens,
    fc_grad,
    out_grad,
    qkv_grad,
    pr_grad,
    pg_out,
    w_fc,
    w_out,
    w_pr,
    starts,
    par_own,
    w_qkv,
    pars,
    par,
    fcb,
    qr,
    kr,
    vr,
    turned,
    orow,
    rows_all,
    lse,
    qs,
    gs,
    acc,
    dqt,
    dk,
    dv,
    gbuf,
    normed,
    inv,
    act,
    oacc,
    gacc,
    fired,
    preg,
    rowg,
    stacked,
    hid,
    dw,
    dwp,
    pgrad,
    pgbuf,
    zgbuf,
    part,
    edge,
    far,
    q_s,
    q_r,
    p_s,
    p_r,
    z_s,
    z_r,
    w_s,
    w_r,
    af_s,
    a_s,
    a_r,
    ar_s,
    ar_r,
    d_s,
    d_r,
    zg_s,
    zg_r,
    g_s,
    g_r,
    loc,
    free,
):
    d = lax.axis_index("dp")
    m = lax.axis_index("mp")
    y, x, k = d // 4, (d // 2) % 2, d % 2
    count = tokens.shape[0]
    blocks, subs = count // TB, count // QB

    def place(yy, xx, kk):
        return (yy * 4 + xx * 2 + kk, m)

    flat_fc = w_fc.reshape(4, 768, 768)
    flat_pr = w_pr.reshape(4, 768, 256)
    flat_out = w_out.reshape(4, 768, 768)
    flat_qkv = w_qkv.reshape(768, 3 * WIDE)
    x_dev, y_dev, diag, twin = (
        place(y, 1 - x, k),
        place(1 - y, x, k),
        place(1 - y, 1 - x, k),
        place(y, x, 1 - k),
    )
    plane = [(lax.rem(d + o, 8), m) for o in range(8)]
    line = [(d, lax.rem(m + o, 4)) for o in range(4)]
    above, below = (d, jnp.minimum(m + 1, 3)), (d, jnp.maximum(m - 1, 0))
    end = (m == 0) | (m == 3)
    inner = jnp.logical_not(end)
    order = [m] + [jnp.where(m <= o - 1, o, o - 1) for o in range(1, 4)]

    for c in range(3):
        w_qkv[y, x, k, :, WIDE * c : WIDE * c + WIDE] = jnp.concatenate(
            [qkv_own[c], jnp.zeros((96, WIDE - HPD * HD), bf16)], axis=1
        )
    par[...] = jnp.zeros_like(par)
    vectors = (gain_one, shift_one, gain_two, shift_two, proj_bias, out_bias, fb_own)
    for n, vector in enumerate(vectors):
        par[n : n + 1, 0:96] = vector[...].astype(f32)
    par[8:9, 0:24] = qv_own[0:1].astype(f32)
    par[8:9, 2 * WIDE : 2 * WIDE + 24] = qv_own[1:2].astype(f32)
    lined = pltpu.roll(par[0:8], 96 * d, 1)
    heads = pltpu.roll(par[8:16], 24 * d, 1)
    row = lax.broadcasted_iota(jnp.int32, (8, 768), 0)
    lined = jnp.where(row == 7, jnp.broadcast_to(heads[0:1], (8, 768)), lined)
    par_own[...] = jnp.concatenate([lined, jnp.zeros((8, 768), f32)], axis=0).astype(bf16)
    barrier = pltpu.get_barrier_semaphore()
    for device in plane[1:] + line[1:]:
        pl.semaphore_signal(barrier, inc=1, device_id=device, device_id_type=MESH)
    pl.semaphore_wait(barrier, 10)

    q_send = [
        remote(w_qkv.at[y, x, k], w_qkv.at[y, x, k], q_s.at[i], q_r.at[i], device)
        for i, device in enumerate((x_dev, y_dev, diag, twin))
    ]
    q_from = [(y, 1 - x, k), (1 - y, x, k), (1 - y, 1 - x, k)]
    q_pass = [
        remote(w_qkv.at[c], w_qkv.at[c], q_s.at[4 + i], q_r.at[4 + i], twin)
        for i, c in enumerate(q_from)
    ]
    for copy in q_send:
        copy.start()
    p_send = [remote(par_own, pars.at[o], p_s.at[o], p_r.at[o], plane[o]) for o in range(1, 8)]
    for copy in p_send:
        copy.start()
    w_fc[m, y, x, k] = fc_own[...]
    w_out[m, y, x, k] = out_own[...]
    tall = jnp.concatenate(
        [pr_own[...].astype(f32), fb_own[...].astype(f32), jnp.zeros((63, 96), f32)], axis=0
    )
    w_pr[m, y, x, k] = tall.T.astype(bf16)
    pars[0] = par_own[...]
    held = (w_fc, w_out, w_pr)

    def along(piece, send, recv, s):
        up = remote(piece, piece, send.at[0], recv, above)
        down = remote(piece, piece, send.at[1], recv, below)
        return ((s <= m) & (m < 3), up), ((s >= m) & (m > 0), down)

    def pass_on(piece, send, recv, s):
        for where, copy in along(piece, send, recv, s):
            pl.when(where)(copy.start)

    def passed_on(piece, send, recv, s):
        for where, copy in along(piece, send, recv, s):
            pl.when(where)(copy.wait_send)

    def z_args(c, s):
        return held[c].at[s, y, x, k], z_s.at[c, s], z_r.at[c, s], s

    def z_step(cs, far_by):
        for s, there in ((m - far_by, m >= far_by), (m + far_by, m + far_by <= 3)):

            @pl.when(there)
            def _():
                for c in cs:
                    piece, send, recv, _ = z_args(c, s)
                    remote(piece, piece, send.at[0], recv, above).wait_recv()
                    pass_on(*z_args(c, s))
                if 0 in cs:
                    spread(s, cs)

    for c in (2, 0, 1):
        pass_on(*z_args(c, m))

    def hop(s, c, stage):
        if stage == 0:
            part_of = held[c].at[s, y, x, k]
            device = y_dev if c == 1 else x_dev
        elif stage == 1:
            part_of = held[c].at[s, :, x, k] if c == 1 else held[c].at[s, y, :, k]
            device = x_dev if c == 1 else y_dev
        else:
            part_of = held[c].at[s, :, :, k]
            device = twin
        return remote(part_of, part_of, w_s.at[c, stage, s], w_r.at[c, stage, s], device)

    def spread(s, cs=(0, 1)):
        for c in cs:
            hop(s, c, 0).start()

    def advance(o, stage, cs=(0, 1)):
        for c in cs:
            hop(order[o], c, stage - 1).wait_recv()
            hop(order[o], c, stage).start()

    pltpu.make_async_copy(
        grads.at[rows_of(blocks - 1, TB)], gbuf.at[0], loc.at[0]
    ).start()

    for copy in p_send:
        copy.wait_recv()
    total = pars[0].astype(f32)
    for o in range(1, 8):
        total = total + pars[o].astype(f32)
    par[...] = total
    spot = lax.broadcasted_iota(jnp.int32, (1, count), 1)
    start = jnp.zeros((1, count), jnp.int32)
    finish = lengths[0, 0]
    for n in range(lengths.shape[1]):
        start = jnp.where(spot >= finish, finish, start)
        if n + 1 < lengths.shape[1]:
            finish = finish + lengths[0, n + 1]
    starts[...] = start
    dk[...] = jnp.zeros_like(dk)
    dv[...] = jnp.zeros_like(dv)
    dw[...] = jnp.zeros_like(dw)
    dwp[...] = jnp.zeros_like(dwp)
    pgrad[...] = jnp.zeros_like(pgrad)
    z_step((2,), 1)
    z_step((2,), 2)
    z_step((2,), 3)
    for i in range(3):
        q_send[i].wait_recv()
        q_pass[i].start()
    spread(m)
    for s in range(4):
        spread(s, (2,))
    z_step((0, 1), 1)
    q_send[3].wait_recv()
    for copy in q_pass:
        copy.wait_recv()

    def first_act(rows):
        unit, inverse = norm(tokens[rows].astype(f32))
        return (unit * par[0:1] + par[1:2]).astype(bf16)

    def project(b, _):
        rows = rows_of(b)
        r = mm(first_act(rows), flat_qkv[...]) + par[7:8]
        qr[rows] = r[:, :WIDE].astype(bf16) * jnp.asarray(SCALE, bf16)
        kr[rows] = r[:, WIDE : 2 * WIDE].astype(bf16)
        v = r[:, 2 * WIDE :].astype(bf16)
        vr[rows] = v
        turned[:, rows] = v.T

        @pl.when(b == 0)
        def _():
            advance(0, 1)

        @pl.when(b == 2)
        def _():
            for o in range(4):
                advance(o, 1, (2,))

        @pl.when(b == 4)
        def _():
            z_step((0, 1), 2)

        @pl.when(b == 6)
        def _():
            for o in range(4):
                advance(o, 2, (2,))

        return 0

    lax.fori_loop(0, subs, project, 0)

    def a_args(b, s):
        return rows_all.at[s, b], a_s.at[b, s], a_r.at[b, s], s

    def a_wait(b, s):
        piece, send, recv, _ = a_args(b, s)
        remote(piece, piece, send.at[0], recv, above).wait_recv()

    def a_step(b, far_by):
        for s, there in ((m - far_by, m >= far_by), (m + far_by, m + far_by <= 3)):

            @pl.when(there & inner)
            def _():
                a_wait(b, s)
                pass_on(*a_args(b, s))

    def direct(b, o):
        return remote(rows_all.at[m, b], rows_all.at[m, b], af_s.at[o], a_r.at[b, m], line[o])

    def attend(t, _):
        b = blocks - 1 - t
        attend_block(2 * b + 1, qr, kr, turned, starts, lse, orow, qs, acc)

        @pl.when(t == 0)
        def _():
            advance(0, 2)

        @pl.when(t == 1)
        def _():
            advance(1, 1)

        @pl.when(t == 2)
        def _():
            advance(3, 1)

        attend_block(2 * b, qr, kr, turned, starts, lse, orow, qs, acc)
        top, low = rows_of(2 * b), rows_of(2 * b + 1)
        rows_all[m, b, :QB] = orow[top, :128]
        rows_all[m, b, QB : 2 * QB] = orow[low, :128]
        rows_all[m, b, 2 * QB :] = (
            orow[top, 128:].astype(f32) + pltpu.roll(orow[low, 128:].astype(f32), 64, 1)
        ).astype(bf16)

        @pl.when(t == 0)
        def _():
            z_step((0, 1), 3)
            for o in range(1, 4):
                direct(blocks - 1, o).start()

        @pl.when(t > 0)
        def _():
            pass_on(*a_args(b, m))

        @pl.when(t == 1)
        def _():
            advance(2, 1)

        return 0

    lax.fori_loop(0, blocks, attend, 0)
    advance(1, 2)

    def turn(i, _):
        turned[:, rows_of(i)] = kr[rows_of(i)].T
        return 0

    lax.fori_loop(0, subs, turn, 0)
    for s in range(4):
        hop(s, 2, 2).wait_recv()

    def bias_row(s, _):
        fcb[s] = flat_pr[s, :, 128:256].astype(f32).T[64:65]
        return 0

    lax.fori_loop(0, 4, bias_row, 0)

    inward = (d, jnp.where(m < 2, 1, 2))
    across = (d, 3 - m)
    outward = (d, jnp.where(m < 2, 0, 3))

    def hop_a(i):
        return remote(part.at[i], edge.at[i], ar_s.at[0, i], ar_r.at[0, i], inward)

    def hop_b(i):
        return remote(part.at[i], far.at[i], ar_s.at[1, i], ar_r.at[1, i], across)

    def hop_c(i):
        return remote(edge.at[i], far.at[i], ar_s.at[2, i], ar_r.at[2, i], outward)

    def stage_two(i):
        @pl.when(inner)
        def _():
            hop_a(i).wait_recv()
            part[i] = (part[i].astype(f32) + edge[i].astype(f32)).astype(bf16)
            hop_b(i).start()

    def stage_three(i):
        @pl.when(inner)
        def _():
            hop_b(i).wait_recv()
            edge[i] = (part[i].astype(f32) + far[i].astype(f32)).astype(bf16)
            hop_c(i).start()

    def gt_out(i):
        return pltpu.make_async_copy(
            hid.at[rows_of(i, RB)], grad_tokens.at[rows_of(i, RB)], g_s.at[8 + i]
        )

    def stage_four(i):
        @pl.when(end)
        def _():
            hop_c(i).wait_recv()
            edge[i] = far[i]

        there = rows_of(i, RB)
        grad = edge[i].astype(f32)
        unit, inverse = norm(tokens[there].astype(f32))
        back = norm_back(grad, par[0:1], unit, inverse)
        hid[there] = (hid[there].astype(f32) + back).astype(bf16)
        gt_out(i).start()

    def out_copy(b, slot):
        return pltpu.make_async_copy(gbuf.at[slot], output.at[rows_of(b, TB)], loc.at[2])

    def out_half(i):
        return pltpu.make_async_copy(
            gbuf.at[(blocks - 1) % 2, rows_of(i)], output.at[rows_of(i)], loc.at[5 + i]
        )

    groups = ((0, 1), (2,), (3,))
    spans = (768, 768, 768, 256)
    wants = [(y, 1 - x, x_dev), (1 - y, x, y_dev), (1 - y, 1 - x, diag)]

    def take(c, dest):
        some = pl.ds(pl.multiple_of(dest * 96, 96), 96)
        return dw[c, some] if c < 3 else dwp[some]

    def span_of(ref, g, *rest):
        if g == 0:
            return ref.at[(slice(0, 2),) + rest]
        return ref.at[(g + 1,) + rest + ((slice(None), slice(0, 256)) if g == 2 else ())]

    def twin_sum(g):
        every = (slice(None), slice(None))
        return remote(
            span_of(w_out, g, *every, 1 - k), span_of(w_fc, g, *every, 0), d_s.at[g], d_r.at[g], twin
        )

    def to_owner(g, i):
        yy, xx, device = wants[i]
        n = 3 + 3 * i + g
        return remote(
            span_of(w_out, g, yy, xx, k),
            span_of(w_fc, g, i // 2, i % 2, 1),
            d_s.at[n],
            d_r.at[n],
            device,
        )

    def give_twin(g):
        for yy in range(2):
            for xx in range(2):
                for c in groups[g]:
                    w_out[c, yy, xx, 1 - k, :, : spans[c]] = take(
                        c, yy * 4 + xx * 2 + 1 - k
                    ).astype(bf16)

    def give_owners(g):
        twin_sum(g).wait_recv()
        for i, (yy, xx, _) in enumerate(wants):
            for c in groups[g]:
                w_out[c, yy, xx, k, :, : spans[c]] = (
                    take(c, yy * 4 + xx * 2 + k) + w_fc[c, yy, xx, 0, :, : spans[c]].astype(f32)
                ).astype(bf16)
            to_owner(g, i).start()

    own_rows = pl.ds(pl.multiple_of(d * 96, 96), 96)
    fc_result = pltpu.make_async_copy(dw.at[0, own_rows], fc_grad, loc.at[7])

    def own_sum(g):
        for i in range(3):
            to_owner(g, i).wait_recv()
        for c in groups[g]:
            value = take(c, d) + w_fc[c, y, x, 0, :, : spans[c]].astype(f32)
            for i in range(3):
                value = value + w_fc[c, i // 2, i % 2, 1, :, : spans[c]].astype(f32)
            if c == 0:
                dw[0, own_rows] = value
                fc_result.start()
            elif c == 1:
                out_grad[...] = value
            elif c == 2:
                for n in range(3):
                    qkv_grad[n] = value[:, WIDE * n : WIDE * n + HPD * HD]
            else:
                pr_grad[...] = value.T[: HPD * HD]

    def make_block(size):
        big = size == TB
        all_rows = slice(0, size)

        def block(t, _):
            b = blocks - 1 - t if big else 0
            i_last = 2 * b + 1 if big else 1 - t
            row = b * TB if big else (1 - t) * QB
            off = 0 if big else (1 - t) * QB
            rows = pl.ds(pl.multiple_of(row, QB), size)
            slot = lax.rem(t, 2) if big else (blocks - 1) % 2
            g_rows = pl.ds(pl.multiple_of(off, QB), size)

            def part_of(r, step):
                return pl.ds(pl.multiple_of(off + r * step, step), step)

            @pl.when((t >= 0) if big else (t == 0))
            def _():
                pltpu.make_async_copy(
                    grads.at[rows_of(b, TB)], gbuf.at[slot], loc.at[slot]
                ).wait()

            if big:

                @pl.when(t >= 1)
                def _():
                    out_copy(b + 1, 1 - slot).wait()

                pltpu.make_async_copy(
                    grads.at[rows_of(b - 1, TB)], gbuf.at[1 - slot], loc.at[1 - slot]
                ).start()

            for s in range(4):

                @pl.when((end | (b == blocks - 1)) & (m != s) & ((t >= 0) if big else (t == 0)))
                def _():
                    a_wait(b, s)

            def head(s, _):
                third = rows_all[s, b, 2 * QB :].astype(f32)
                turned_third = pltpu.roll(third, 64, 1)
                if big:
                    third = jnp.concatenate([third, turned_third], axis=0)
                else:
                    third = jnp.where(t == 0, turned_third, third)
                lane = lax.broadcasted_iota(jnp.int32, third.shape, 1)
                third = jnp.where(lane < 64, third, 0.0).astype(bf16)
                left = jnp.concatenate([rows_all[s, b, g_rows], third], axis=1)
                oacc[all_rows] += mm(left, flat_pr[s], NT)
                return 0

            oacc[all_rows] = tokens[rows].astype(f32) + par[4:5]
            lax.fori_loop(0, 4, head, 0)

            def second(r, _):
                some = rows_of(r, RB)
                hidden = oacc[some]
                unit, inverse = norm(hidden)
                normed[some] = unit
                inv[some] = inverse
                act[some] = (unit * par[2:3] + par[3:4]).astype(bf16)
                oacc[some] = hidden + par[5:6]
                gacc[some] = jnp.zeros_like(hidden)
                return 0

            lax.fori_loop(0, size // RB, second, 0)

            def slab(s, _):
                if big:

                    @pl.when(t == 0)
                    def _():
                        for c in range(2):
                            hop(s, c, 2).wait_recv()

                def units(r, _):
                    some = rows_of(r)
                    pre = mm(act[some], flat_fc[s]) + fcb[s]
                    back = mm(gbuf[slot, part_of(r, QB)], flat_out[s])
                    square = pre * pre
                    tangent = jnp.tanh(pre * (GELU_C + (GELU_C * 0.044715) * square))
                    half = 0.5 * pre
                    fired[some] = (half + half * tangent).astype(bf16)
                    slope = (0.5 + 0.5 * tangent) + half * (1.0 - tangent * tangent) * (
                        GELU_C + (3.0 * GELU_C * 0.044715) * square
                    )
                    preg[some] = (back * slope).astype(bf16)
                    return 0

                lax.fori_loop(0, size // QB, units, 0)
                oacc[all_rows] += mm(fired[all_rows], flat_out[s], NT)
                gacc[all_rows] += mm(preg[all_rows], flat_fc[s], NT)

                @pl.when(s == m)
                def _():
                    def outer(r, _):
                        some = rows_of(r)
                        dw[0, some] += mm(act[all_rows, some], preg[all_rows], TN)
                        dw[1, some] += mm(gbuf[slot, g_rows, some], fired[all_rows], TN)
                        return 0

                    lax.fori_loop(0, 3, outer, 0)
                    pgrad[6:7] += jnp.sum(preg[all_rows].astype(f32), axis=0, keepdims=True)

                def at(when, do, *what):
                    @pl.when(when)
                    def _():
                        for item in what:
                            do(item)

                if big:

                    @pl.when((t == 0) & (s == 0))
                    def _():
                        advance(2, 2)

                    @pl.when((t == 0) & (s == jnp.where(m == 3, 1, 2)))
                    def _():
                        advance(3, 2)

                    @pl.when((t == 0) & (s == 2))
                    def _():
                        a_step(2, 1)
                        a_step(1, 1)

                    j = 4 * b + 4
                    at((t >= 1) & (s == 0), stage_two, j + 3, j + 2)
                    at((t >= 1) & (s == 2), stage_two, j + 1, j)
                    at((t >= 1) & (s == 3), stage_three, j + 3, j + 2)
                    at((t >= 2) & (s == 1), stage_four, j + 7, j + 6, j + 5, j + 4)
                else:
                    at((t == 0) & (s == 1), stage_two, 7, 6)
                    at((t == 0) & (s == 3), stage_two, 5)
                    at((t == 0) & (s == 2), stage_four, 11, 10, 9, 8)
                    at((t == 1) & (s == 1), stage_three, 5)
                    at((t == 1) & (s == 3), stage_three, 4)
                return 0

            lax.fori_loop(0, 4, slab, 0)
            if big:

                @pl.when(t == 0)
                def _():
                    a_step(2, 2)
                    a_step(0, 1)

            else:

                @pl.when(t == 1)
                def _():
                    for c in range(3):
                        for s in range(4):
                            passed_on(*z_args(c, s))
                            for stage in range(3):
                                hop(s, c, stage).wait_send()
                    for device in (x_dev, y_dev, diag, twin):
                        pl.semaphore_signal(free, inc=1, device_id=device, device_id_type=MESH)
                    give_twin(0)
                    pl.semaphore_wait(free, 4)
                    twin_sum(0).start()

            def rejoin(r, _):
                some = rows_of(r, RB)
                there = pl.ds(pl.multiple_of(row + r * RB, RB), RB)
                grad = gbuf[slot, part_of(r, RB)].astype(f32)
                through, unit = gacc[some], normed[some]
                pgrad[5:6] += jnp.sum(grad, axis=0, keepdims=True)
                pgrad[2:3] += jnp.sum(through * unit, axis=0, keepdims=True)
                pgrad[3:4] += jnp.sum(through, axis=0, keepdims=True)
                branch = (grad + norm_back(through, par[2:3], unit, inv[some])).astype(bf16)
                hid[there] = branch
                pgrad[4:5] += jnp.sum(branch.astype(f32), axis=0, keepdims=True)
                gbuf[slot, part_of(r, RB)] = oacc[some].astype(bf16)
                return 0

            lax.fori_loop(0, size // RB, rejoin, 0)
            if big:
                out_copy(b, slot).start()
            else:
                out_half(1 - t).start()
            dwp[...] += mm(hid[rows], orow[rows], TN)
            if not big:

                @pl.when(t == 1)
                def _():
                    give_twin(2)
                    twin_sum(2).start()
                    give_owners(0)

            rowg[all_rows] = mm(hid[rows], flat_pr[m]).astype(bf16)

            for n in range(size // QB):
                i = i_last - n
                some = slice(size - QB * (n + 1), size - QB * n)
                attend_block_back(
                    i, rowg[some], qr, kr, vr, turned, orow, starts, lse, dk, dv, qs, gs, dqt
                )
                stacked[some, :WIDE] = (dqt[...].T * SCALE).astype(bf16)
                stacked[some, WIDE : 2 * WIDE] = dk[rows_of(i)].astype(bf16)
                stacked[some, 2 * WIDE :] = dv[rows_of(i)].astype(bf16)
                whole = mm(stacked[some], flat_qkv[...], NT).astype(bf16)
                part[2 * i] = whole[:RB]
                part[2 * i + 1] = whole[RB:]

                @pl.when(end)
                def _():
                    hop_a(2 * i + 1).start()
                    hop_a(2 * i).start()

                if big and n == 0:

                    @pl.when(t >= 1)
                    def _():
                        stage_three(4 * b + 5)
                        stage_three(4 * b + 4)

                if not big:

                    @pl.when(t == 0)
                    def _():
                        stage_two(4)
                        stage_three(7)
                        stage_three(6)

                    @pl.when(t == 1)
                    def _():
                        stage_two(3)
                        stage_two(2)

            pgrad[7:8] += jnp.sum(stacked[all_rows].astype(f32), axis=0, keepdims=True)

            def again(r, _):
                unit, _ = norm(tokens[pl.ds(pl.multiple_of(row + r * RB, RB), RB)].astype(f32))
                act[rows_of(r, RB)] = (unit * par[0:1] + par[1:2]).astype(bf16)
                grad = part[row // RB + r].astype(f32)
                pgrad[0:1] += jnp.sum(grad * unit, axis=0, keepdims=True)
                pgrad[1:2] += jnp.sum(grad, axis=0, keepdims=True)
                return 0

            lax.fori_loop(0, size // RB, again, 0)

            def outer(r, _):
                some = rows_of(r)
                dw[2, some] += mm(act[all_rows, some], stacked[all_rows], TN)
                return 0

            lax.fori_loop(0, 3, outer, 0)
            if big:

                @pl.when(t == 0)
                def _():
                    a_step(1, 2)

                @pl.when(t == 1)
                def _():
                    a_step(0, 2)

            return 0

        return block

    lax.fori_loop(0, blocks - 1, make_block(TB), 0)
    lax.fori_loop(0, 2, make_block(QB), 0)

    zg_send = [
        remote(zgbuf.at[m], zgbuf.at[m], zg_s.at[o], zg_r.at[m], line[o]) for o in range(1, 4)
    ]
    zgbuf[m] = pgrad[...]
    for copy in zg_send:
        copy.start()
    give_twin(1)
    twin_sum(1).start()
    stage_three(3)
    stage_three(2)
    for s in range(4):

        @pl.when(m != s)
        def _():
            remote(zgbuf.at[s], zgbuf.at[s], zg_s.at[1], zg_r.at[s], line[1]).wait_recv()

    pgrad[0:2] = zgbuf[0, 0:2] + zgbuf[1, 0:2] + zgbuf[2, 0:2] + zgbuf[3, 0:2]
    g_send = [
        remote(pgrad, pgbuf.at[o], g_s.at[o], g_r.at[o], plane[o]) for o in range(1, 8)
    ]
    for copy in g_send:
        copy.start()
    give_owners(2)
    give_owners(1)
    for i in (7, 6, 5, 4):
        stage_four(i)
    stage_two(1)
    stage_two(0)
    total = pgrad[...]
    for copy in g_send:
        copy.wait_recv()
    for o in range(1, 8):
        total = total + pgbuf[o]
    pg_out[0:8] = pltpu.roll(total, lax.rem(768 - 96 * d, 768), 1)[:, :128]
    heads = pltpu.roll(total, lax.rem(768 - 24 * d, 768), 1)
    pg_out[8:16] = heads[:, :128]
    pg_out[16:24] = heads[:, 2 * WIDE : 2 * WIDE + 128]
    stage_three(1)
    stage_three(0)
    stage_four(3)
    stage_four(2)
    own_sum(0)
    own_sum(2)
    own_sum(1)
    stage_four(1)
    stage_four(0)

    fc_result.wait()
    for copy in g_send + zg_send + q_send + q_pass + p_send:
        copy.wait_send()
    for g in range(3):
        twin_sum(g).wait_send()
        for i in range(3):
            to_owner(g, i).wait_send()
    out_copy(1, (blocks - 2) % 2).wait()
    out_half(1).wait()
    out_half(0).wait()

    def leave(i, _):
        gt_out(i).wait()

        @pl.when(end)
        def _():
            hop_a(i).wait_send()

        @pl.when(inner)
        def _():
            hop_b(i).wait_send()
            hop_c(i).wait_send()

        return 0

    lax.fori_loop(0, count // RB, leave, 0)
    for o in range(1, 4):
        direct(blocks - 1, o).wait_send()
    for b in range(blocks - 1):
        for s in range(4):
            passed_on(*a_args(b, s))


def whole_block(tokens, out_grad, lengths, *shards):
    count = tokens.shape[0]
    blocks, subs = count // TB, count // QB
    any_space = pl.BlockSpec(memory_space=pl.ANY)
    dma = pltpu.SemaphoreType.DMA
    return pl.pallas_call(
        whole_kernel,
        out_shape=(
            jax.ShapeDtypeStruct((count, 768), bf16),
            jax.ShapeDtypeStruct((count, 768), bf16),
            jax.ShapeDtypeStruct((96, 768), f32),
            jax.ShapeDtypeStruct((96, 768), f32),
            jax.ShapeDtypeStruct((3, 96, HPD * HD), f32),
            jax.ShapeDtypeStruct((HPD * HD, 96), f32),
            jax.ShapeDtypeStruct((24, 128), f32),
        ),
        in_specs=[VMEM, any_space, pl.BlockSpec(memory_space=pltpu.SMEM)] + [VMEM] * len(shards),
        out_specs=(any_space, any_space, any_space, VMEM, VMEM, VMEM, VMEM),
        scratch_shapes=[
            pltpu.VMEM((4, 2, 2, 2, 96, 768), bf16),
            pltpu.VMEM((4, 2, 2, 2, 96, 768), bf16),
            pltpu.VMEM((4, 2, 2, 2, 96, 256), bf16),
            pltpu.VMEM((1, count), jnp.int32),
            pltpu.VMEM((16, 768), bf16),
            pltpu.VMEM((2, 2, 2, 96, 768), bf16),
            pltpu.VMEM((8, 16, 768), bf16),
            pltpu.VMEM((16, 768), f32),
            pltpu.VMEM((4, 1, 768), f32),
            pltpu.VMEM((count, WIDE), bf16),
            pltpu.VMEM((count, WIDE), bf16),
            pltpu.VMEM((count, WIDE), bf16),
            pltpu.VMEM((WIDE, count), bf16),
            pltpu.VMEM((count, WIDE), bf16),
            pltpu.VMEM((4, blocks, 3 * QB, 128), bf16),
            pltpu.VMEM((subs, 1, HPD * QB), f32),
            pltpu.VMEM((HPD * QB, WIDE), bf16),
            pltpu.VMEM((HPD * QB, WIDE), bf16),
            pltpu.VMEM((HD, HPD * QB), f32),
            pltpu.VMEM((WIDE, QB), f32),
            pltpu.VMEM((count, WIDE), f32),
            pltpu.VMEM((count, WIDE), f32),
            pltpu.VMEM((2, TB, 768), bf16),
            pltpu.VMEM((TB, 768), f32),
            pltpu.VMEM((TB, 1), f32),
            pltpu.VMEM((TB, 768), bf16),
            pltpu.VMEM((TB, 768), f32),
            pltpu.VMEM((TB, 768), f32),
            pltpu.VMEM((TB, 768), bf16),
            pltpu.VMEM((TB, 768), bf16),
            pltpu.VMEM((TB, WIDE), bf16),
            pltpu.VMEM((TB, 768), bf16),
            pltpu.VMEM((count, 768), bf16),
            pltpu.VMEM((3, 768, 768), f32),
            pltpu.VMEM((768, 256), f32),
            pltpu.VMEM((8, 768), f32),
            pltpu.VMEM((8, 8, 768), f32),
            pltpu.VMEM((4, 8, 768), f32),
            pltpu.VMEM((count // RB, RB, 768), bf16),
            pltpu.VMEM((count // RB, RB, 768), bf16),
            pltpu.VMEM((count // RB, RB, 768), bf16),
            dma((7,)),
            dma((7,)),
            dma((8,)),
            dma((8,)),
            dma((3, 4, 2)),
            dma((3, 4)),
            dma((3, 3, 4)),
            dma((3, 3, 4)),
            dma((4,)),
            dma((blocks, 4, 2)),
            dma((blocks, 4)),
            dma((3, count // RB)),
            dma((3, count // RB)),
            dma((12,)),
            dma((12,)),
            dma((4,)),
            dma((4,)),
            dma((8 + count // RB,)),
            dma((8,)),
            dma((11,)),
            pltpu.SemaphoreType.REGULAR,
        ],
        compiler_params=pltpu.CompilerParams(
            collective_id=0, has_side_effects=True, vmem_limit_bytes=63 * 2**20
        ),
    )(tokens, out_grad, lengths, *shards)


def per_device_whole(
    tokens,
    lengths,
    first_gain,
    first_shift,
    qkv_weight,
    qv_bias,
    proj_weight,
    proj_bias,
    second_gain,
    second_shift,
    fc_weight,
    fc_bias,
    out_weight,
    out_bias,
    out_grad,
):
    output, grad_tokens, fc_grad, out_w_grad, qkv_grad, proj_grad, pg = whole_block(
        tokens,
        out_grad,
        lengths,
        fc_weight,
        out_weight.T,
        proj_weight,
        fc_bias,
        qkv_weight,
        first_gain[None],
        first_shift[None],
        second_gain[None],
        second_shift[None],
        proj_bias[None],
        out_bias[None],
        qv_bias[:, 0],
    )
    vec = pg[:7, :96]
    qv = jnp.concatenate([pg[15:16, :24], pg[23:24, :24]])[:, None, :]
    return (
        output,
        grad_tokens,
        vec[0],
        vec[1],
        qkv_grad,
        qv,
        proj_grad,
        vec[4],
        vec[2],
        vec[3],
        fc_grad,
        vec[6][None],
        out_w_grad.T,
        vec[5],
    )


def solution(mesh):
    placed = (
        P("dp", None),
        P("dp", None),
        P("dp"),
        P("dp"),
        P(None, "dp", "mp"),
        P(None, "mp", "dp"),
        P("mp", "dp"),
        P("dp"),
        P("dp"),
        P("dp"),
        P("dp", "mp"),
        P("mp", "dp"),
        P("mp", "dp"),
        P("dp"),
        P("dp", None),
    )
    return jax.shard_map(
        per_device_whole if dict(mesh.shape) == {"dp": 8, "mp": 4} else per_device,
        mesh=mesh,
        in_specs=placed,
        out_specs=(
            P("dp", None),
            P("dp", None),
            P("dp"),
            P("dp"),
            P(None, "dp", "mp"),
            P(None, "mp", "dp"),
            P("mp", "dp"),
            P("dp"),
            P("dp"),
            P("dp"),
            P("dp", "mp"),
            P("mp", "dp"),
            P("mp", "dp"),
            P("dp"),
        ),
        check_vma=False,
    )
```

```python
import functools

import jax
import jax.numpy as jnp
from jax import lax
from jax.experimental import pallas as pl
from jax.experimental.pallas import tpu as pltpu
from jax.sharding import PartitionSpec as P

HD = 64
HPD = 3
WIDE = 256
MAXLEN = 1024
QB = 256
BAND = MAXLEN // QB


EPS = 1e-05
SCALE = 0.125
NEG = -1e30
GELU_C = 0.7978845608028654
NN = (((1,), (0,)), ((), ()))
NT = (((1,), (1,)), ((), ()))
TN = (((0,), (0,)), ((), ()))
f32 = jnp.float32
bf16 = jnp.bfloat16


def mm(left, right, dims=NN):
    return lax.dot_general(left, right, dims, preferred_element_type=f32)


def split_up(shard, dim, size):
    before, after = (shard.shape[:dim], shard.shape[dim + 1 :])
    return jnp.moveaxis(shard.reshape(*before, size, -1, *after), dim, 0)


def summed_on_arrival(shard, axis, dim):
    size = lax.axis_size(axis)
    pieces = lax.all_to_all(split_up(shard, dim, size), axis, 0, 0, tiled=True)
    return jnp.sum(pieces.astype(jnp.float32), axis=0)


def norm_parts(values):
    mean = jnp.mean(values, axis=-1, keepdims=True)
    centred = values - mean
    inverse = lax.rsqrt(jnp.mean(centred * centred, axis=-1, keepdims=True) + EPS)
    return (centred * inverse, inverse)


def norm_back(grad, gain, normed, inverse):
    scaled = grad * gain
    return inverse * (
        scaled
        - jnp.mean(scaled, axis=-1, keepdims=True)
        - normed * jnp.mean(scaled * normed, axis=-1, keepdims=True)
    )


def gelu_tanh(values):
    return 0.5 * values * (1.0 + jnp.tanh(GELU_C * (values + 0.044715 * values * values * values)))


def gelu_slope(values):
    inner = GELU_C * (values + 0.044715 * values * values * values)
    tangent = jnp.tanh(inner)
    return 0.5 * (1.0 + tangent) + 0.5 * values * (1.0 - tangent * tangent) * GELU_C * (
        1.0 + 3.0 * 0.044715 * values * values
    )


def segment_starts(lengths_row, count):
    ends = jnp.cumsum(lengths_row)
    places = jnp.arange(count, dtype=jnp.int32)
    return jnp.max(jnp.where(ends[None, :] <= places[:, None], ends[None, :], 0), axis=1)[None, :]


def rows_of(index, size=QB):
    return pl.ds(pl.multiple_of(index * size, size), size)


def tile_heads(x):
    return jnp.concatenate([x] * HPD, axis=1)


def allowed_keys(i, j, start_ref):
    start = start_ref[:, rows_of(i)]
    key = lax.broadcasted_iota(jnp.int32, (QB, QB), 0)
    query = lax.broadcasted_iota(jnp.int32, (QB, QB), 1)
    return (key >= start - j * QB) & (key <= query + (i - j) * QB)


def stack_heads(x):
    lane = lax.broadcasted_iota(jnp.int32, x.shape, 1)
    return jnp.concatenate(
        [
            jnp.where((lane >= HD * h) & (lane < HD * h + HD), x, jnp.zeros_like(x))
            for h in range(HPD)
        ],
        axis=0,
    )


def attend_block(i, q_ref, k_ref, vt_ref, start_ref, lse_ref, o_ref, qs, acc):
    rows = rows_of(i)
    qs[...] = stack_heads(q_ref[rows])
    acc[...] = jnp.zeros_like(acc)

    def step(jj, carry):
        biggest, total = carry
        j = i - jj
        keys = rows_of(j)
        s = mm(k_ref[keys], qs[...], NT)
        s = jnp.where(tile_heads(allowed_keys(i, j, start_ref)), s, NEG)
        new = jnp.maximum(biggest, jnp.max(s, axis=0, keepdims=True))
        p = jnp.exp(s - new)
        shrink = jnp.exp(biggest - new)
        total = total * shrink + jnp.sum(p, axis=0, keepdims=True)
        p = p.astype(bf16)
        for h in range(HPD):
            cols = slice(QB * h, QB * h + QB)
            acc[:, cols] = acc[:, cols] * shrink[:, cols] + mm(
                vt_ref[HD * h : HD * h + HD, keys], p[:, cols]
            )
        return new, total

    biggest, total = lax.fori_loop(
        0,
        jnp.minimum(i, BAND) + 1,
        step,
        (jnp.full((1, HPD * QB), NEG, f32), jnp.zeros((1, HPD * QB), f32)),
    )
    lse_ref[i] = biggest + jnp.log(total)
    inverse = 1.0 / total
    out = jnp.concatenate(
        [acc[:, QB * h : QB * h + QB] * inverse[:, QB * h : QB * h + QB] for h in range(HPD)]
        + [jnp.zeros((WIDE - HPD * HD, QB), f32)],
        axis=0,
    )
    o_ref[rows] = out.T.astype(bf16)


def attend_block_back(i, grad, q_ref, k_ref, v_ref, kt_ref, o_ref, start_ref, lse_ref, dk, dv, qs, gs, dqt):
    rows = rows_of(i)
    qs[...] = stack_heads(q_ref[rows])
    gs[...] = stack_heads(grad)
    both = (grad.astype(f32) * o_ref[rows].astype(f32)).T
    delta = jnp.concatenate(
        [jnp.sum(both[HD * h : HD * h + HD], axis=0, keepdims=True) for h in range(HPD)], axis=1
    )
    lse = lse_ref[i]
    dqt[...] = jnp.zeros_like(dqt)

    def step(jj, _):
        j = i - jj
        keys = rows_of(j)
        s = mm(k_ref[keys], qs[...], NT)
        s = jnp.where(tile_heads(allowed_keys(i, j, start_ref)), s, NEG)
        p = jnp.exp(s - lse)
        dp = mm(v_ref[keys], gs[...], NT)
        ds = (p * (dp - delta)).astype(bf16)
        p = p.astype(bf16)
        dv[keys] += mm(p, gs[...])
        dk[keys] += mm(ds, qs[...])
        for h in range(HPD):
            dqt[HD * h : HD * h + HD] += mm(
                kt_ref[HD * h : HD * h + HD, keys], ds[:, QB * h : QB * h + QB]
            )
        return 0

    lax.fori_loop(0, jnp.minimum(i, BAND) + 1, step, 0)


def forward_kernel(q_ref, k_ref, v_ref, start_ref, o_ref, lse_ref, vt, qs, acc):
    blocks = q_ref.shape[0] // QB

    def turn(i, _):
        vt[:, rows_of(i)] = v_ref[rows_of(i)].T
        return 0

    lax.fori_loop(0, blocks, turn, 0)

    def block(i, _):
        attend_block(i, q_ref, k_ref, vt, start_ref, lse_ref, o_ref, qs, acc)
        return 0

    lax.fori_loop(0, blocks, block, 0)


def backward_kernel(
    q_ref, k_ref, v_ref, o_ref, g_ref, start_ref, lse_ref, d_ref, kt, qs, gs, dqt, dk, dv
):
    blocks = q_ref.shape[0] // QB

    def turn(i, _):
        kt[:, rows_of(i)] = k_ref[rows_of(i)].T
        return 0

    lax.fori_loop(0, blocks, turn, 0)
    dk[...] = jnp.zeros_like(dk)
    dv[...] = jnp.zeros_like(dv)

    def block(turn_of, _):
        i = blocks - 1 - turn_of
        rows = rows_of(i)
        attend_block_back(
            i, g_ref[rows], q_ref, k_ref, v_ref, kt, o_ref, start_ref, lse_ref, dk, dv, qs, gs, dqt
        )
        d_ref[0, rows] = (dqt[...].T * SCALE).astype(bf16)
        d_ref[1, rows] = dk[rows].astype(bf16)
        d_ref[2, rows] = dv[rows].astype(bf16)
        return 0

    lax.fori_loop(0, blocks, block, 0)


VMEM = pl.BlockSpec(memory_space=pltpu.VMEM)
LIMIT = pltpu.CompilerParams(vmem_limit_bytes=40 * 2**20)


def attend_forward(query, keys, values, starts):
    count = query.shape[0]
    return pl.pallas_call(
        forward_kernel,
        out_shape=(
            jax.ShapeDtypeStruct((count, WIDE), bf16),
            jax.ShapeDtypeStruct((count // QB, 1, HPD * QB), f32),
        ),
        in_specs=[VMEM] * 4,
        out_specs=(VMEM, VMEM),
        scratch_shapes=[
            pltpu.VMEM((WIDE, count), bf16),
            pltpu.VMEM((HPD * QB, WIDE), bf16),
            pltpu.VMEM((HD, HPD * QB), f32),
        ],
        compiler_params=LIMIT,
    )(query, keys, values, starts)


def attend_backward(query, keys, values, rows, grad, starts, lse):
    count = query.shape[0]
    return pl.pallas_call(
        backward_kernel,
        out_shape=jax.ShapeDtypeStruct((3, count, WIDE), bf16),
        in_specs=[VMEM] * 7,
        out_specs=VMEM,
        scratch_shapes=[
            pltpu.VMEM((WIDE, count), bf16),
            pltpu.VMEM((HPD * QB, WIDE), bf16),
            pltpu.VMEM((HPD * QB, WIDE), bf16),
            pltpu.VMEM((WIDE, QB), f32),
            pltpu.VMEM((count, WIDE), f32),
            pltpu.VMEM((count, WIDE), f32),
        ],
        compiler_params=LIMIT,
    )(query, keys, values, rows, grad, starts, lse)


def per_device(
    tokens,
    lengths,
    first_gain,
    first_shift,
    qkv_weight,
    qv_bias,
    proj_weight,
    proj_bias,
    second_gain,
    second_shift,
    fc_weight,
    fc_bias,
    out_weight,
    out_bias,
    out_grad,
):
    count = tokens.shape[0]
    starts = segment_starts(lengths[0], count)
    gain_one, shift_one, qkv_all, qv_all, proj_all, proj_bias_all = (
        lax.all_gather(first_gain, "dp", axis=0, tiled=True),
        lax.all_gather(first_shift, "dp", axis=0, tiled=True),
        lax.all_gather(qkv_weight, "dp", axis=1, tiled=True),
        lax.all_gather(qv_bias, "dp", axis=2, tiled=True),
        lax.all_gather(proj_weight, "dp", axis=1, tiled=True),
        lax.all_gather(proj_bias, "dp", axis=0, tiled=True),
    )
    gain_one_f = gain_one.astype(jnp.float32)
    xin = tokens.astype(jnp.float32)
    normed_one, inverse_one = norm_parts(xin)
    act_one = (normed_one * gain_one_f + shift_one.astype(jnp.float32)).astype(jnp.bfloat16)
    projected = jnp.einsum("td,cde->cte", act_one, qkv_all, preferred_element_type=jnp.float32)
    width = qkv_all.shape[2]
    wide = ((0, 0), (0, WIDE - width))
    query = jnp.pad(
        (projected[0] + qv_all[0, 0].astype(f32)).astype(bf16) * jnp.asarray(SCALE, bf16), wide
    )
    keys = jnp.pad(projected[1].astype(bf16), wide)
    values = jnp.pad((projected[2] + qv_all[1, 0].astype(f32)).astype(bf16), wide)
    wide_rows, lse = attend_forward(query, keys, values, starts)
    flat_rows = wide_rows[:, :width]
    gain_two, shift_two, fc_all, fc_bias_all, out_all, out_bias_all = (
        lax.all_gather(second_gain, "dp", axis=0, tiled=True),
        lax.all_gather(second_shift, "dp", axis=0, tiled=True),
        lax.all_gather(fc_weight, "dp", axis=0, tiled=True),
        lax.all_gather(fc_bias, "dp", axis=1, tiled=True),
        lax.all_gather(out_weight, "dp", axis=1, tiled=True),
        lax.all_gather(out_bias, "dp", axis=0, tiled=True),
    )
    gain_two_f = gain_two.astype(jnp.float32)
    shift_two_f = shift_two.astype(jnp.float32)
    branch_one = lax.psum(
        jnp.dot(flat_rows, proj_all, preferred_element_type=jnp.float32).astype(jnp.bfloat16), "mp"
    ).astype(jnp.float32)
    hidden_one = xin + branch_one + proj_bias_all.astype(jnp.float32)
    normed_two, inverse_two = norm_parts(hidden_one)
    act_two = (normed_two * gain_two_f + shift_two_f).astype(jnp.bfloat16)
    pre = jnp.dot(act_two, fc_all, preferred_element_type=jnp.float32) + fc_bias_all[0].astype(
        jnp.float32
    )
    fired = gelu_tanh(pre).astype(jnp.bfloat16)
    branch_two = lax.psum(
        jnp.dot(fired, out_all, preferred_element_type=jnp.float32).astype(jnp.bfloat16), "mp"
    ).astype(jnp.float32)
    output = (hidden_one + branch_two + out_bias_all.astype(jnp.float32)).astype(jnp.bfloat16)
    grad_out = out_grad.astype(jnp.float32)
    out_bias_grad = jnp.sum(out_grad, axis=0, dtype=jnp.float32)
    out_weight_grad = jnp.einsum("tf,td->fd", fired, out_grad, preferred_element_type=jnp.float32)
    fired_grad = jnp.einsum("td,fd->tf", out_grad, out_all, preferred_element_type=jnp.float32)
    pre_grad = (fired_grad * gelu_slope(pre)).astype(jnp.bfloat16)
    fc_bias_grad = jnp.sum(pre_grad, axis=0, dtype=jnp.float32)
    fc_weight_grad = jnp.einsum("td,tf->df", act_two, pre_grad, preferred_element_type=jnp.float32)
    act_two_grad = lax.psum(
        jnp.einsum("tf,df->td", pre_grad, fc_all, preferred_element_type=jnp.float32).astype(
            jnp.bfloat16
        ),
        "mp",
    ).astype(jnp.float32)
    gain_two_grad = jnp.sum(act_two_grad * normed_two, axis=0)
    shift_two_grad = jnp.sum(act_two_grad, axis=0)
    hidden_grad = grad_out + norm_back(act_two_grad, gain_two_f, normed_two, inverse_two)
    branch_grad = hidden_grad.astype(jnp.bfloat16)
    proj_bias_grad = jnp.sum(branch_grad, axis=0, dtype=jnp.float32)
    proj_weight_grad = jnp.einsum(
        "te,td->ed", flat_rows, branch_grad, preferred_element_type=jnp.float32
    )
    rows_grad = jnp.einsum(
        "td,ed->te", branch_grad, proj_all, preferred_element_type=jnp.float32
    ).astype(jnp.bfloat16)
    stacked = attend_backward(
        query, keys, values, wide_rows, jnp.pad(rows_grad, wide), starts, lse
    )[:, :, :width]
    qkv_grad = jnp.einsum("td,cte->cde", act_one, stacked, preferred_element_type=jnp.float32)
    bias_sums = jnp.sum(stacked, axis=1, dtype=jnp.float32)
    qv_grad = jnp.stack([bias_sums[0], bias_sums[2]])[:, None, :]
    act_one_grad = lax.psum(
        jnp.einsum("cte,cde->td", stacked, qkv_all, preferred_element_type=jnp.float32).astype(
            jnp.bfloat16
        ),
        "mp",
    ).astype(jnp.float32)
    gain_one_grad = jnp.sum(act_one_grad * normed_one, axis=0)
    shift_one_grad = jnp.sum(act_one_grad, axis=0)
    input_grad = (
        hidden_grad + norm_back(act_one_grad, gain_one_f, normed_one, inverse_one)
    ).astype(jnp.bfloat16)
    mlp_grads = (
        lax.psum_scatter(gain_two_grad, "dp", scatter_dimension=0, tiled=True),
        lax.psum_scatter(shift_two_grad, "dp", scatter_dimension=0, tiled=True),
        lax.psum_scatter(fc_weight_grad, "dp", scatter_dimension=0, tiled=True),
        lax.psum_scatter(fc_bias_grad[None], "dp", scatter_dimension=1, tiled=True),
        lax.psum_scatter(out_weight_grad, "dp", scatter_dimension=1, tiled=True),
        lax.psum_scatter(out_bias_grad, "dp", scatter_dimension=0, tiled=True),
    )
    attn_grads = (
        summed_on_arrival(gain_one_grad.astype(jnp.bfloat16), "dp", 0),
        summed_on_arrival(shift_one_grad.astype(jnp.bfloat16), "dp", 0),
        summed_on_arrival(qkv_grad.astype(jnp.bfloat16), "dp", 1),
        summed_on_arrival(qv_grad.astype(jnp.bfloat16), "dp", 2),
        summed_on_arrival(proj_weight_grad.astype(jnp.bfloat16), "dp", 1),
        summed_on_arrival(proj_bias_grad.astype(jnp.bfloat16), "dp", 0),
    )
    return (
        output,
        input_grad,
        attn_grads[0],
        attn_grads[1],
        attn_grads[2],
        attn_grads[3],
        attn_grads[4],
        attn_grads[5],
        mlp_grads[0],
        mlp_grads[1],
        mlp_grads[2],
        mlp_grads[3],
        mlp_grads[4],
        mlp_grads[5],
    )


MESH = pl.DeviceIdType.MESH
TB = 512
RB = 128


def norm(values):
    mean = jnp.mean(values, axis=-1, keepdims=True)
    centred = values - mean
    inverse = lax.rsqrt(jnp.mean(centred * centred, axis=-1, keepdims=True) + EPS)
    return centred * inverse, inverse


def remote(src, dst, send, recv, device):
    return pltpu.make_async_remote_copy(
        src_ref=src, dst_ref=dst, send_sem=send, recv_sem=recv, device_id=device, device_id_type=MESH
    )


def whole_kernel(
    tokens,
    grads,
    lengths,
    fc_own,
    out_own,
    pr_own,
    fb_own,
    qkv_own,
    gain_one,
    shift_one,
    gain_two,
    shift_two,
    proj_bias,
    out_bias,
    qv_own,
    output,
    grad_tokens,
    fc_grad,
    out_grad,
    qkv_grad,
    pr_grad,
    pg_out,
    w_fc,
    w_out,
    w_pr,
    starts,
    par_own,
    w_qkv,
    pars,
    par,
    fcb,
    qr,
    kr,
    vr,
    turned,
    orow,
    rows_all,
    lse,
    qs,
    gs,
    acc,
    dqt,
    dk,
    dv,
    gbuf,
    normed,
    inv,
    act,
    oacc,
    gacc,
    fired,
    preg,
    rowg,
    stacked,
    hid,
    dw,
    dwp,
    pgrad,
    pgbuf,
    zgbuf,
    part,
    edge,
    far,
    q_s,
    q_r,
    p_s,
    p_r,
    z_s,
    z_r,
    w_s,
    w_r,
    af_s,
    a_s,
    a_r,
    ar_s,
    ar_r,
    d_s,
    d_r,
    zg_s,
    zg_r,
    g_s,
    g_r,
    loc,
    free,
):
    d = lax.axis_index("dp")
    m = lax.axis_index("mp")
    y, x, k = d // 4, (d // 2) % 2, d % 2
    count = tokens.shape[0]
    blocks, subs = count // TB, count // QB

    def place(yy, xx, kk):
        return (yy * 4 + xx * 2 + kk, m)

    flat_fc = w_fc.reshape(4, 768, 768)
    flat_pr = w_pr.reshape(4, 768, 256)
    flat_out = w_out.reshape(4, 768, 768)
    flat_qkv = w_qkv.reshape(768, 3 * WIDE)
    x_dev, y_dev, diag, twin = (
        place(y, 1 - x, k),
        place(1 - y, x, k),
        place(1 - y, 1 - x, k),
        place(y, x, 1 - k),
    )
    plane = [(lax.rem(d + o, 8), m) for o in range(8)]
    line = [(d, lax.rem(m + o, 4)) for o in range(4)]
    above, below = (d, jnp.minimum(m + 1, 3)), (d, jnp.maximum(m - 1, 0))
    end = (m == 0) | (m == 3)
    inner = jnp.logical_not(end)
    order = [m] + [jnp.where(m <= o - 1, o, o - 1) for o in range(1, 4)]

    for c in range(3):
        w_qkv[y, x, k, :, WIDE * c : WIDE * c + WIDE] = jnp.concatenate(
            [qkv_own[c], jnp.zeros((96, WIDE - HPD * HD), bf16)], axis=1
        )
    par[...] = jnp.zeros_like(par)
    vectors = (gain_one, shift_one, gain_two, shift_two, proj_bias, out_bias, fb_own)
    for n, vector in enumerate(vectors):
        par[n : n + 1, 0:96] = vector[...].astype(f32)
    par[8:9, 0:24] = qv_own[0:1].astype(f32)
    par[8:9, 2 * WIDE : 2 * WIDE + 24] = qv_own[1:2].astype(f32)
    lined = pltpu.roll(par[0:8], 96 * d, 1)
    heads = pltpu.roll(par[8:16], 24 * d, 1)
    row = lax.broadcasted_iota(jnp.int32, (8, 768), 0)
    lined = jnp.where(row == 7, jnp.broadcast_to(heads[0:1], (8, 768)), lined)
    par_own[...] = jnp.concatenate([lined, jnp.zeros((8, 768), f32)], axis=0).astype(bf16)
    barrier = pltpu.get_barrier_semaphore()
    for device in plane[1:] + line[1:]:
        pl.semaphore_signal(barrier, inc=1, device_id=device, device_id_type=MESH)
    pl.semaphore_wait(barrier, 10)

    q_send = [
        remote(w_qkv.at[y, x, k], w_qkv.at[y, x, k], q_s.at[i], q_r.at[i], device)
        for i, device in enumerate((x_dev, y_dev, diag, twin))
    ]
    q_from = [(y, 1 - x, k), (1 - y, x, k), (1 - y, 1 - x, k)]
    q_pass = [
        remote(w_qkv.at[c], w_qkv.at[c], q_s.at[4 + i], q_r.at[4 + i], twin)
        for i, c in enumerate(q_from)
    ]
    for copy in q_send:
        copy.start()
    p_send = [remote(par_own, pars.at[o], p_s.at[o], p_r.at[o], plane[o]) for o in range(1, 8)]
    for copy in p_send:
        copy.start()
    w_fc[m, y, x, k] = fc_own[...]
    w_out[m, y, x, k] = out_own[...]
    tall = jnp.concatenate(
        [pr_own[...].astype(f32), fb_own[...].astype(f32), jnp.zeros((63, 96), f32)], axis=0
    )
    w_pr[m, y, x, k] = tall.T.astype(bf16)
    pars[0] = par_own[...]
    held = (w_fc, w_out, w_pr)

    def along(piece, send, recv, s):
        up = remote(piece, piece, send.at[0], recv, above)
        down = remote(piece, piece, send.at[1], recv, below)
        return ((s <= m) & (m < 3), up), ((s >= m) & (m > 0), down)

    def pass_on(piece, send, recv, s):
        for where, copy in along(piece, send, recv, s):
            pl.when(where)(copy.start)

    def passed_on(piece, send, recv, s):
        for where, copy in along(piece, send, recv, s):
            pl.when(where)(copy.wait_send)

    def z_args(c, s):
        return held[c].at[s, y, x, k], z_s.at[c, s], z_r.at[c, s], s

    def z_step(cs, far_by):
        for s, there in ((m - far_by, m >= far_by), (m + far_by, m + far_by <= 3)):

            @pl.when(there)
            def _():
                for c in cs:
                    piece, send, recv, _ = z_args(c, s)
                    remote(piece, piece, send.at[0], recv, above).wait_recv()
                    pass_on(*z_args(c, s))
                if 0 in cs:
                    spread(s, cs)

    for c in (2, 0, 1):
        pass_on(*z_args(c, m))

    def hop(s, c, stage):
        if stage == 0:
            part_of = held[c].at[s, y, x, k]
            device = y_dev if c == 1 else x_dev
        elif stage == 1:
            part_of = held[c].at[s, :, x, k] if c == 1 else held[c].at[s, y, :, k]
            device = x_dev if c == 1 else y_dev
        else:
            part_of = held[c].at[s, :, :, k]
            device = twin
        return remote(part_of, part_of, w_s.at[c, stage, s], w_r.at[c, stage, s], device)

    def spread(s, cs=(0, 1)):
        for c in cs:
            hop(s, c, 0).start()

    def advance(o, stage, cs=(0, 1)):
        for c in cs:
            hop(order[o], c, stage - 1).wait_recv()
            hop(order[o], c, stage).start()

    pltpu.make_async_copy(
        grads.at[rows_of(blocks - 1, TB)], gbuf.at[0], loc.at[0]
    ).start()

    for copy in p_send:
        copy.wait_recv()
    total = pars[0].astype(f32)
    for o in range(1, 8):
        total = total + pars[o].astype(f32)
    par[...] = total
    spot = lax.broadcasted_iota(jnp.int32, (1, count), 1)
    start = jnp.zeros((1, count), jnp.int32)
    finish = lengths[0, 0]
    for n in range(lengths.shape[1]):
        start = jnp.where(spot >= finish, finish, start)
        if n + 1 < lengths.shape[1]:
            finish = finish + lengths[0, n + 1]
    starts[...] = start
    dk[...] = jnp.zeros_like(dk)
    dv[...] = jnp.zeros_like(dv)
    dw[...] = jnp.zeros_like(dw)
    dwp[...] = jnp.zeros_like(dwp)
    pgrad[...] = jnp.zeros_like(pgrad)
    z_step((2,), 1)
    z_step((2,), 2)
    z_step((2,), 3)
    for i in range(3):
        q_send[i].wait_recv()
        q_pass[i].start()
    spread(m)
    for s in range(4):
        spread(s, (2,))
    z_step((0, 1), 1)
    q_send[3].wait_recv()
    for copy in q_pass:
        copy.wait_recv()

    def first_act(rows):
        unit, inverse = norm(tokens[rows].astype(f32))
        return (unit * par[0:1] + par[1:2]).astype(bf16)

    def project(b, _):
        rows = rows_of(b)
        r = mm(first_act(rows), flat_qkv[...]) + par[7:8]
        qr[rows] = r[:, :WIDE].astype(bf16) * jnp.asarray(SCALE, bf16)
        kr[rows] = r[:, WIDE : 2 * WIDE].astype(bf16)
        v = r[:, 2 * WIDE :].astype(bf16)
        vr[rows] = v
        turned[:, rows] = v.T

        @pl.when(b == 0)
        def _():
            advance(0, 1)

        @pl.when(b == 2)
        def _():
            for o in range(4):
                advance(o, 1, (2,))

        @pl.when(b == 4)
        def _():
            z_step((0, 1), 2)

        @pl.when(b == 6)
        def _():
            for o in range(4):
                advance(o, 2, (2,))

        return 0

    lax.fori_loop(0, subs, project, 0)

    def a_args(b, s):
        return rows_all.at[s, b], a_s.at[b, s], a_r.at[b, s], s

    def a_wait(b, s):
        piece, send, recv, _ = a_args(b, s)
        remote(piece, piece, send.at[0], recv, above).wait_recv()

    def a_step(b, far_by):
        for s, there in ((m - far_by, m >= far_by), (m + far_by, m + far_by <= 3)):

            @pl.when(there & inner)
            def _():
                a_wait(b, s)
                pass_on(*a_args(b, s))

    def direct(b, o):
        return remote(rows_all.at[m, b], rows_all.at[m, b], af_s.at[o], a_r.at[b, m], line[o])

    def attend(t, _):
        b = blocks - 1 - t
        attend_block(2 * b + 1, qr, kr, turned, starts, lse, orow, qs, acc)

        @pl.when(t == 0)
        def _():
            advance(0, 2)

        @pl.when(t == 1)
        def _():
            advance(1, 1)

        @pl.when(t == 2)
        def _():
            advance(3, 1)

        attend_block(2 * b, qr, kr, turned, starts, lse, orow, qs, acc)
        top, low = rows_of(2 * b), rows_of(2 * b + 1)
        rows_all[m, b, :QB] = orow[top, :128]
        rows_all[m, b, QB : 2 * QB] = orow[low, :128]
        rows_all[m, b, 2 * QB :] = (
            orow[top, 128:].astype(f32) + pltpu.roll(orow[low, 128:].astype(f32), 64, 1)
        ).astype(bf16)

        @pl.when(t == 0)
        def _():
            z_step((0, 1), 3)
            for o in range(1, 4):
                direct(blocks - 1, o).start()

        @pl.when(t > 0)
        def _():
            pass_on(*a_args(b, m))

        @pl.when(t == 1)
        def _():
            advance(2, 1)

        return 0

    lax.fori_loop(0, blocks, attend, 0)
    advance(1, 2)

    def turn(i, _):
        turned[:, rows_of(i)] = kr[rows_of(i)].T
        return 0

    lax.fori_loop(0, subs, turn, 0)
    for s in range(4):
        hop(s, 2, 2).wait_recv()

    def bias_row(s, _):
        fcb[s] = flat_pr[s, :, 128:256].astype(f32).T[64:65]
        return 0

    lax.fori_loop(0, 4, bias_row, 0)

    inward = (d, jnp.where(m < 2, 1, 2))
    across = (d, 3 - m)
    outward = (d, jnp.where(m < 2, 0, 3))

    def hop_a(i):
        return remote(part.at[i], edge.at[i], ar_s.at[0, i], ar_r.at[0, i], inward)

    def hop_b(i):
        return remote(part.at[i], far.at[i], ar_s.at[1, i], ar_r.at[1, i], across)

    def hop_c(i):
        return remote(edge.at[i], far.at[i], ar_s.at[2, i], ar_r.at[2, i], outward)

    def stage_two(i):
        @pl.when(inner)
        def _():
            hop_a(i).wait_recv()
            part[i] = (part[i].astype(f32) + edge[i].astype(f32)).astype(bf16)
            hop_b(i).start()

    def stage_three(i):
        @pl.when(inner)
        def _():
            hop_b(i).wait_recv()
            edge[i] = (part[i].astype(f32) + far[i].astype(f32)).astype(bf16)
            hop_c(i).start()

    def gt_out(i):
        return pltpu.make_async_copy(
            hid.at[rows_of(i, RB)], grad_tokens.at[rows_of(i, RB)], g_s.at[8 + i]
        )

    def stage_four(i):
        @pl.when(end)
        def _():
            hop_c(i).wait_recv()
            edge[i] = far[i]

        there = rows_of(i, RB)
        grad = edge[i].astype(f32)
        unit, inverse = norm(tokens[there].astype(f32))
        back = norm_back(grad, par[0:1], unit, inverse)
        hid[there] = (hid[there].astype(f32) + back).astype(bf16)
        gt_out(i).start()

    def out_copy(b, slot):
        return pltpu.make_async_copy(gbuf.at[slot], output.at[rows_of(b, TB)], loc.at[2])

    def out_half(i):
        return pltpu.make_async_copy(
            gbuf.at[(blocks - 1) % 2, rows_of(i)], output.at[rows_of(i)], loc.at[5 + i]
        )

    groups = ((0, 1), (2,), (3,))
    spans = (768, 768, 768, 256)
    wants = [(y, 1 - x, x_dev), (1 - y, x, y_dev), (1 - y, 1 - x, diag)]

    def take(c, dest):
        some = pl.ds(pl.multiple_of(dest * 96, 96), 96)
        return dw[c, some] if c < 3 else dwp[some]

    def span_of(ref, g, *rest):
        if g == 0:
            return ref.at[(slice(0, 2),) + rest]
        return ref.at[(g + 1,) + rest + ((slice(None), slice(0, 256)) if g == 2 else ())]

    def twin_sum(g):
        every = (slice(None), slice(None))
        return remote(
            span_of(w_out, g, *every, 1 - k), span_of(w_fc, g, *every, 0), d_s.at[g], d_r.at[g], twin
        )

    def to_owner(g, i):
        yy, xx, device = wants[i]
        n = 3 + 3 * i + g
        return remote(
            span_of(w_out, g, yy, xx, k),
            span_of(w_fc, g, i // 2, i % 2, 1),
            d_s.at[n],
            d_r.at[n],
            device,
        )

    def give_twin(g):
        for yy in range(2):
            for xx in range(2):
                for c in groups[g]:
                    w_out[c, yy, xx, 1 - k, :, : spans[c]] = take(
                        c, yy * 4 + xx * 2 + 1 - k
                    ).astype(bf16)

    def give_owners(g):
        twin_sum(g).wait_recv()
        for i, (yy, xx, _) in enumerate(wants):
            for c in groups[g]:
                w_out[c, yy, xx, k, :, : spans[c]] = (
                    take(c, yy * 4 + xx * 2 + k) + w_fc[c, yy, xx, 0, :, : spans[c]].astype(f32)
                ).astype(bf16)
            to_owner(g, i).start()

    own_rows = pl.ds(pl.multiple_of(d * 96, 96), 96)
    fc_result = pltpu.make_async_copy(dw.at[0, own_rows], fc_grad, loc.at[7])

    def own_sum(g):
        for i in range(3):
            to_owner(g, i).wait_recv()
        for c in groups[g]:
            value = take(c, d) + w_fc[c, y, x, 0, :, : spans[c]].astype(f32)
            for i in range(3):
                value = value + w_fc[c, i // 2, i % 2, 1, :, : spans[c]].astype(f32)
            if c == 0:
                dw[0, own_rows] = value
                fc_result.start()
            elif c == 1:
                out_grad[...] = value
            elif c == 2:
                for n in range(3):
                    qkv_grad[n] = value[:, WIDE * n : WIDE * n + HPD * HD]
            else:
                pr_grad[...] = value.T[: HPD * HD]

    def make_block(size):
        big = size == TB
        all_rows = slice(0, size)

        def block(t, _):
            b = blocks - 1 - t if big else 0
            i_last = 2 * b + 1 if big else 1 - t
            row = b * TB if big else (1 - t) * QB
            off = 0 if big else (1 - t) * QB
            rows = pl.ds(pl.multiple_of(row, QB), size)
            slot = lax.rem(t, 2) if big else (blocks - 1) % 2
            g_rows = pl.ds(pl.multiple_of(off, QB), size)

            def part_of(r, step):
                return pl.ds(pl.multiple_of(off + r * step, step), step)

            @pl.when((t >= 0) if big else (t == 0))
            def _():
                pltpu.make_async_copy(
                    grads.at[rows_of(b, TB)], gbuf.at[slot], loc.at[slot]
                ).wait()

            if big:

                @pl.when(t >= 1)
                def _():
                    out_copy(b + 1, 1 - slot).wait()

                pltpu.make_async_copy(
                    grads.at[rows_of(b - 1, TB)], gbuf.at[1 - slot], loc.at[1 - slot]
                ).start()

            for s in range(4):

                @pl.when((end | (b == blocks - 1)) & (m != s) & ((t >= 0) if big else (t == 0)))
                def _():
                    a_wait(b, s)

            def head(s):
                third = rows_all[s, b, 2 * QB :].astype(f32)
                turned_third = pltpu.roll(third, 64, 1)
                if big:
                    third = jnp.concatenate([third, turned_third], axis=0)
                else:
                    third = jnp.where(t == 0, turned_third, third)
                lane = lax.broadcasted_iota(jnp.int32, third.shape, 1)
                third = jnp.where(lane < 64, third, 0.0).astype(bf16)
                left = jnp.concatenate([rows_all[s, b, g_rows], third], axis=1)
                return mm(left, flat_pr[s], NT)

            oacc[all_rows] = (
                tokens[rows].astype(f32) + par[4:5] + (head(0) + head(1) + head(2) + head(3))
            )

            def second(r, _):
                some = rows_of(r, RB)
                hidden = oacc[some]
                unit, inverse = norm(hidden)
                normed[some] = unit
                inv[some] = inverse
                act[some] = (unit * par[2:3] + par[3:4]).astype(bf16)
                oacc[some] = hidden + par[5:6]
                gacc[some] = jnp.zeros_like(hidden)
                return 0

            lax.fori_loop(0, size // RB, second, 0)

            def slab(s, _):
                if big:

                    @pl.when(t == 0)
                    def _():
                        for c in range(2):
                            hop(s, c, 2).wait_recv()

                def units(r, _):
                    some = rows_of(r)
                    pre = mm(act[some], flat_fc[s]) + fcb[s]
                    back = mm(gbuf[slot, part_of(r, QB)], flat_out[s])
                    square = pre * pre
                    tangent = jnp.tanh(pre * (GELU_C + (GELU_C * 0.044715) * square))
                    half = 0.5 * pre
                    fired[some] = (half + half * tangent).astype(bf16)
                    slope = (0.5 + 0.5 * tangent) + half * (1.0 - tangent * tangent) * (
                        GELU_C + (3.0 * GELU_C * 0.044715) * square
                    )
                    preg[some] = (back * slope).astype(bf16)
                    return 0

                lax.fori_loop(0, size // QB, units, 0)
                oacc[all_rows] += mm(fired[all_rows], flat_out[s], NT)
                gacc[all_rows] += mm(preg[all_rows], flat_fc[s], NT)

                @pl.when(s == m)
                def _():
                    def outer(r, _):
                        some = rows_of(r)
                        dw[0, some] += mm(act[all_rows, some], preg[all_rows], TN)
                        dw[1, some] += mm(gbuf[slot, g_rows, some], fired[all_rows], TN)
                        return 0

                    lax.fori_loop(0, 3, outer, 0)
                    pgrad[6:7] += jnp.sum(preg[all_rows].astype(f32), axis=0, keepdims=True)

                def at(when, do, *what):
                    @pl.when(when)
                    def _():
                        for item in what:
                            do(item)

                if big:

                    @pl.when((t == 0) & (s == 0))
                    def _():
                        advance(2, 2)

                    @pl.when((t == 0) & (s == jnp.where(m == 3, 1, 2)))
                    def _():
                        advance(3, 2)

                    @pl.when((t == 0) & (s == 2))
                    def _():
                        a_step(2, 1)
                        a_step(1, 1)

                    j = 4 * b + 4
                    at((t >= 1) & (s == 0), stage_two, j + 3, j + 2)
                    at((t >= 1) & (s == 2), stage_two, j + 1, j)
                    at((t >= 1) & (s == 3), stage_three, j + 3, j + 2)
                    at((t >= 2) & (s == 1), stage_four, j + 7, j + 6, j + 5, j + 4)
                else:
                    at((t == 0) & (s == 1), stage_two, 7, 6)
                    at((t == 0) & (s == 3), stage_two, 5)
                    at((t == 0) & (s == 2), stage_four, 11, 10, 9, 8)
                    at((t == 1) & (s == 1), stage_three, 5)
                    at((t == 1) & (s == 3), stage_three, 4)
                return 0

            lax.fori_loop(0, 4, slab, 0)
            if big:

                @pl.when(t == 0)
                def _():
                    a_step(2, 2)
                    a_step(0, 1)

            else:

                @pl.when(t == 1)
                def _():
                    for c in range(3):
                        for s in range(4):
                            passed_on(*z_args(c, s))
                            for stage in range(3):
                                hop(s, c, stage).wait_send()
                    for device in (x_dev, y_dev, diag, twin):
                        pl.semaphore_signal(free, inc=1, device_id=device, device_id_type=MESH)
                    give_twin(0)
                    pl.semaphore_wait(free, 4)
                    twin_sum(0).start()

            def rejoin(r, _):
                some = rows_of(r, RB)
                there = pl.ds(pl.multiple_of(row + r * RB, RB), RB)
                grad = gbuf[slot, part_of(r, RB)].astype(f32)
                through, unit = gacc[some], normed[some]
                pgrad[5:6] += jnp.sum(grad, axis=0, keepdims=True)
                pgrad[2:3] += jnp.sum(through * unit, axis=0, keepdims=True)
                pgrad[3:4] += jnp.sum(through, axis=0, keepdims=True)
                branch = (grad + norm_back(through, par[2:3], unit, inv[some])).astype(bf16)
                hid[there] = branch
                pgrad[4:5] += jnp.sum(branch.astype(f32), axis=0, keepdims=True)
                gbuf[slot, part_of(r, RB)] = oacc[some].astype(bf16)
                return 0

            lax.fori_loop(0, size // RB, rejoin, 0)
            if big:
                out_copy(b, slot).start()
            else:
                out_half(1 - t).start()
            dwp[...] += mm(hid[rows], orow[rows], TN)
            if not big:

                @pl.when(t == 1)
                def _():
                    give_twin(2)
                    twin_sum(2).start()
                    give_owners(0)

            rowg[all_rows] = mm(hid[rows], flat_pr[m]).astype(bf16)

            for n in range(size // QB):
                i = i_last - n
                some = slice(size - QB * (n + 1), size - QB * n)
                attend_block_back(
                    i, rowg[some], qr, kr, vr, turned, orow, starts, lse, dk, dv, qs, gs, dqt
                )
                stacked[some, :WIDE] = (dqt[...].T * SCALE).astype(bf16)
                stacked[some, WIDE : 2 * WIDE] = dk[rows_of(i)].astype(bf16)
                stacked[some, 2 * WIDE :] = dv[rows_of(i)].astype(bf16)
                whole = mm(stacked[some], flat_qkv[...], NT).astype(bf16)
                part[2 * i] = whole[:RB]
                part[2 * i + 1] = whole[RB:]

                @pl.when(end)
                def _():
                    hop_a(2 * i + 1).start()
                    hop_a(2 * i).start()

                if big and n == 0:

                    @pl.when(t >= 1)
                    def _():
                        stage_three(4 * b + 5)
                        stage_three(4 * b + 4)

                if not big:

                    @pl.when(t == 0)
                    def _():
                        stage_two(4)
                        stage_three(7)
                        stage_three(6)

                    @pl.when(t == 1)
                    def _():
                        stage_two(3)
                        stage_two(2)

            pgrad[7:8] += jnp.sum(stacked[all_rows].astype(f32), axis=0, keepdims=True)

            def again(r, _):
                unit, _ = norm(tokens[pl.ds(pl.multiple_of(row + r * RB, RB), RB)].astype(f32))
                act[rows_of(r, RB)] = (unit * par[0:1] + par[1:2]).astype(bf16)
                grad = part[row // RB + r].astype(f32)
                pgrad[0:1] += jnp.sum(grad * unit, axis=0, keepdims=True)
                pgrad[1:2] += jnp.sum(grad, axis=0, keepdims=True)
                return 0

            lax.fori_loop(0, size // RB, again, 0)

            def outer(r, _):
                some = rows_of(r)
                dw[2, some] += mm(act[all_rows, some], stacked[all_rows], TN)
                return 0

            lax.fori_loop(0, 3, outer, 0)
            if big:

                @pl.when(t == 0)
                def _():
                    a_step(1, 2)

                @pl.when(t == 1)
                def _():
                    a_step(0, 2)

            return 0

        return block

    lax.fori_loop(0, blocks - 1, make_block(TB), 0)
    lax.fori_loop(0, 2, make_block(QB), 0)

    zg_send = [
        remote(zgbuf.at[m], zgbuf.at[m], zg_s.at[o], zg_r.at[m], line[o]) for o in range(1, 4)
    ]
    zgbuf[m] = pgrad[...]
    for copy in zg_send:
        copy.start()
    give_twin(1)
    twin_sum(1).start()
    stage_three(3)
    stage_three(2)
    for s in range(4):

        @pl.when(m != s)
        def _():
            remote(zgbuf.at[s], zgbuf.at[s], zg_s.at[1], zg_r.at[s], line[1]).wait_recv()

    pgrad[0:2] = zgbuf[0, 0:2] + zgbuf[1, 0:2] + zgbuf[2, 0:2] + zgbuf[3, 0:2]
    g_send = [
        remote(pgrad, pgbuf.at[o], g_s.at[o], g_r.at[o], plane[o]) for o in range(1, 8)
    ]
    for copy in g_send:
        copy.start()
    give_owners(2)
    give_owners(1)
    for i in (7, 6, 5, 4):
        stage_four(i)
    stage_two(1)
    stage_two(0)
    total = pgrad[...]
    for copy in g_send:
        copy.wait_recv()
    for o in range(1, 8):
        total = total + pgbuf[o]
    pg_out[0:8] = pltpu.roll(total, lax.rem(768 - 96 * d, 768), 1)[:, :128]
    heads = pltpu.roll(total, lax.rem(768 - 24 * d, 768), 1)
    pg_out[8:16] = heads[:, :128]
    pg_out[16:24] = heads[:, 2 * WIDE : 2 * WIDE + 128]
    stage_three(1)
    stage_three(0)
    stage_four(3)
    stage_four(2)
    own_sum(0)
    own_sum(2)
    own_sum(1)
    stage_four(1)
    stage_four(0)

    fc_result.wait()
    for copy in g_send + zg_send + q_send + q_pass + p_send:
        copy.wait_send()
    for g in range(3):
        twin_sum(g).wait_send()
        for i in range(3):
            to_owner(g, i).wait_send()
    out_copy(1, (blocks - 2) % 2).wait()
    out_half(1).wait()
    out_half(0).wait()

    def leave(i, _):
        gt_out(i).wait()

        @pl.when(end)
        def _():
            hop_a(i).wait_send()

        @pl.when(inner)
        def _():
            hop_b(i).wait_send()
            hop_c(i).wait_send()

        return 0

    lax.fori_loop(0, count // RB, leave, 0)
    for o in range(1, 4):
        direct(blocks - 1, o).wait_send()
    for b in range(blocks - 1):
        for s in range(4):
            passed_on(*a_args(b, s))


def whole_block(tokens, out_grad, lengths, *shards):
    count = tokens.shape[0]
    blocks, subs = count // TB, count // QB
    any_space = pl.BlockSpec(memory_space=pl.ANY)
    dma = pltpu.SemaphoreType.DMA
    return pl.pallas_call(
        whole_kernel,
        out_shape=(
            jax.ShapeDtypeStruct((count, 768), bf16),
            jax.ShapeDtypeStruct((count, 768), bf16),
            jax.ShapeDtypeStruct((96, 768), f32),
            jax.ShapeDtypeStruct((96, 768), f32),
            jax.ShapeDtypeStruct((3, 96, HPD * HD), f32),
            jax.ShapeDtypeStruct((HPD * HD, 96), f32),
            jax.ShapeDtypeStruct((24, 128), f32),
        ),
        in_specs=[VMEM, any_space, pl.BlockSpec(memory_space=pltpu.SMEM)] + [VMEM] * len(shards),
        out_specs=(any_space, any_space, any_space, VMEM, VMEM, VMEM, VMEM),
        scratch_shapes=[
            pltpu.VMEM((4, 2, 2, 2, 96, 768), bf16),
            pltpu.VMEM((4, 2, 2, 2, 96, 768), bf16),
            pltpu.VMEM((4, 2, 2, 2, 96, 256), bf16),
            pltpu.VMEM((1, count), jnp.int32),
            pltpu.VMEM((16, 768), bf16),
            pltpu.VMEM((2, 2, 2, 96, 768), bf16),
            pltpu.VMEM((8, 16, 768), bf16),
            pltpu.VMEM((16, 768), f32),
            pltpu.VMEM((4, 1, 768), f32),
            pltpu.VMEM((count, WIDE), bf16),
            pltpu.VMEM((count, WIDE), bf16),
            pltpu.VMEM((count, WIDE), bf16),
            pltpu.VMEM((WIDE, count), bf16),
            pltpu.VMEM((count, WIDE), bf16),
            pltpu.VMEM((4, blocks, 3 * QB, 128), bf16),
            pltpu.VMEM((subs, 1, HPD * QB), f32),
            pltpu.VMEM((HPD * QB, WIDE), bf16),
            pltpu.VMEM((HPD * QB, WIDE), bf16),
            pltpu.VMEM((HD, HPD * QB), f32),
            pltpu.VMEM((WIDE, QB), f32),
            pltpu.VMEM((count, WIDE), f32),
            pltpu.VMEM((count, WIDE), f32),
            pltpu.VMEM((2, TB, 768), bf16),
            pltpu.VMEM((TB, 768), f32),
            pltpu.VMEM((TB, 1), f32),
            pltpu.VMEM((TB, 768), bf16),
            pltpu.VMEM((TB, 768), f32),
            pltpu.VMEM((TB, 768), f32),
            pltpu.VMEM((TB, 768), bf16),
            pltpu.VMEM((TB, 768), bf16),
            pltpu.VMEM((TB, WIDE), bf16),
            pltpu.VMEM((TB, 768), bf16),
            pltpu.VMEM((count, 768), bf16),
            pltpu.VMEM((3, 768, 768), f32),
            pltpu.VMEM((768, 256), f32),
            pltpu.VMEM((8, 768), f32),
            pltpu.VMEM((8, 8, 768), f32),
            pltpu.VMEM((4, 8, 768), f32),
            pltpu.VMEM((count // RB, RB, 768), bf16),
            pltpu.VMEM((count // RB, RB, 768), bf16),
            pltpu.VMEM((count // RB, RB, 768), bf16),
            dma((7,)),
            dma((7,)),
            dma((8,)),
            dma((8,)),
            dma((3, 4, 2)),
            dma((3, 4)),
            dma((3, 3, 4)),
            dma((3, 3, 4)),
            dma((4,)),
            dma((blocks, 4, 2)),
            dma((blocks, 4)),
            dma((3, count // RB)),
            dma((3, count // RB)),
            dma((12,)),
            dma((12,)),
            dma((4,)),
            dma((4,)),
            dma((8 + count // RB,)),
            dma((8,)),
            dma((11,)),
            pltpu.SemaphoreType.REGULAR,
        ],
        compiler_params=pltpu.CompilerParams(
            collective_id=0, has_side_effects=True, vmem_limit_bytes=63 * 2**20
        ),
    )(tokens, out_grad, lengths, *shards)


def per_device_whole(
    tokens,
    lengths,
    first_gain,
    first_shift,
    qkv_weight,
    qv_bias,
    proj_weight,
    proj_bias,
    second_gain,
    second_shift,
    fc_weight,
    fc_bias,
    out_weight,
    out_bias,
    out_grad,
):
    output, grad_tokens, fc_grad, out_w_grad, qkv_grad, proj_grad, pg = whole_block(
        tokens,
        out_grad,
        lengths,
        fc_weight,
        out_weight.T,
        proj_weight,
        fc_bias,
        qkv_weight,
        first_gain[None],
        first_shift[None],
        second_gain[None],
        second_shift[None],
        proj_bias[None],
        out_bias[None],
        qv_bias[:, 0],
    )
    vec = pg[:7, :96]
    qv = jnp.concatenate([pg[15:16, :24], pg[23:24, :24]])[:, None, :]
    return (
        output,
        grad_tokens,
        vec[0],
        vec[1],
        qkv_grad,
        qv,
        proj_grad,
        vec[4],
        vec[2],
        vec[3],
        fc_grad,
        vec[6][None],
        out_w_grad.T,
        vec[5],
    )


def solution(mesh):
    placed = (
        P("dp", None),
        P("dp", None),
        P("dp"),
        P("dp"),
        P(None, "dp", "mp"),
        P(None, "mp", "dp"),
        P("mp", "dp"),
        P("dp"),
        P("dp"),
        P("dp"),
        P("dp", "mp"),
        P("mp", "dp"),
        P("mp", "dp"),
        P("dp"),
        P("dp", None),
    )
    return jax.shard_map(
        per_device_whole if dict(mesh.shape) == {"dp": 8, "mp": 4} else per_device,
        mesh=mesh,
        in_specs=placed,
        out_specs=(
            P("dp", None),
            P("dp", None),
            P("dp"),
            P("dp"),
            P(None, "dp", "mp"),
            P(None, "mp", "dp"),
            P("mp", "dp"),
            P("dp"),
            P("dp"),
            P("dp"),
            P("dp", "mp"),
            P("mp", "dp"),
            P("mp", "dp"),
            P("dp"),
        ),
        check_vma=False,
    )
```

```python
import functools

import jax
import jax.numpy as jnp
from jax import lax
from jax.experimental import pallas as pl
from jax.experimental.pallas import tpu as pltpu
from jax.sharding import PartitionSpec as P

HD = 64
HPD = 3
WIDE = 256
MAXLEN = 1024
QB = 256
BAND = MAXLEN // QB


EPS = 1e-05
SCALE = 0.125
NEG = -1e30
GELU_C = 0.7978845608028654
NN = (((1,), (0,)), ((), ()))
NT = (((1,), (1,)), ((), ()))
TN = (((0,), (0,)), ((), ()))
f32 = jnp.float32
bf16 = jnp.bfloat16


def mm(left, right, dims=NN):
    return lax.dot_general(left, right, dims, preferred_element_type=f32)


def split_up(shard, dim, size):
    before, after = (shard.shape[:dim], shard.shape[dim + 1 :])
    return jnp.moveaxis(shard.reshape(*before, size, -1, *after), dim, 0)


def summed_on_arrival(shard, axis, dim):
    size = lax.axis_size(axis)
    pieces = lax.all_to_all(split_up(shard, dim, size), axis, 0, 0, tiled=True)
    return jnp.sum(pieces.astype(jnp.float32), axis=0)


def norm_parts(values):
    mean = jnp.mean(values, axis=-1, keepdims=True)
    centred = values - mean
    inverse = lax.rsqrt(jnp.mean(centred * centred, axis=-1, keepdims=True) + EPS)
    return (centred * inverse, inverse)


def norm_back(grad, gain, normed, inverse):
    scaled = grad * gain
    return inverse * (
        scaled
        - jnp.mean(scaled, axis=-1, keepdims=True)
        - normed * jnp.mean(scaled * normed, axis=-1, keepdims=True)
    )


def gelu_tanh(values):
    return 0.5 * values * (1.0 + jnp.tanh(GELU_C * (values + 0.044715 * values * values * values)))


def gelu_slope(values):
    inner = GELU_C * (values + 0.044715 * values * values * values)
    tangent = jnp.tanh(inner)
    return 0.5 * (1.0 + tangent) + 0.5 * values * (1.0 - tangent * tangent) * GELU_C * (
        1.0 + 3.0 * 0.044715 * values * values
    )


def segment_starts(lengths_row, count):
    ends = jnp.cumsum(lengths_row)
    places = jnp.arange(count, dtype=jnp.int32)
    return jnp.max(jnp.where(ends[None, :] <= places[:, None], ends[None, :], 0), axis=1)[None, :]


def rows_of(index, size=QB):
    return pl.ds(pl.multiple_of(index * size, size), size)


def tile_heads(x):
    return jnp.concatenate([x] * HPD, axis=1)


def allowed_keys(i, j, start_ref):
    start = start_ref[:, rows_of(i)]
    key = lax.broadcasted_iota(jnp.int32, (QB, QB), 0)
    query = lax.broadcasted_iota(jnp.int32, (QB, QB), 1)
    return (key >= start - j * QB) & (key <= query + (i - j) * QB)


def stack_heads(x):
    lane = lax.broadcasted_iota(jnp.int32, x.shape, 1)
    return jnp.concatenate(
        [
            jnp.where((lane >= HD * h) & (lane < HD * h + HD), x, jnp.zeros_like(x))
            for h in range(HPD)
        ],
        axis=0,
    )


def attend_block(i, q_ref, k_ref, vt_ref, start_ref, lse_ref, o_ref, qs, acc):
    rows = rows_of(i)
    qs[...] = stack_heads(q_ref[rows])
    acc[...] = jnp.zeros_like(acc)

    def step(jj, carry):
        biggest, total = carry
        j = i - jj
        keys = rows_of(j)
        s = mm(k_ref[keys], qs[...], NT)
        s = jnp.where(tile_heads(allowed_keys(i, j, start_ref)), s, NEG)
        new = jnp.maximum(biggest, jnp.max(s, axis=0, keepdims=True))
        p = jnp.exp(s - new)
        shrink = jnp.exp(biggest - new)
        total = total * shrink + jnp.sum(p, axis=0, keepdims=True)
        p = p.astype(bf16)
        for h in range(HPD):
            cols = slice(QB * h, QB * h + QB)
            acc[:, cols] = acc[:, cols] * shrink[:, cols] + mm(
                vt_ref[HD * h : HD * h + HD, keys], p[:, cols]
            )
        return new, total

    biggest, total = lax.fori_loop(
        0,
        jnp.minimum(i, BAND) + 1,
        step,
        (jnp.full((1, HPD * QB), NEG, f32), jnp.zeros((1, HPD * QB), f32)),
    )
    lse_ref[i] = biggest + jnp.log(total)
    inverse = 1.0 / total
    out = jnp.concatenate(
        [acc[:, QB * h : QB * h + QB] * inverse[:, QB * h : QB * h + QB] for h in range(HPD)]
        + [jnp.zeros((WIDE - HPD * HD, QB), f32)],
        axis=0,
    )
    o_ref[rows] = out.T.astype(bf16)


def attend_block_back(i, grad, q_ref, k_ref, v_ref, kt_ref, o_ref, start_ref, lse_ref, dk, dv, qs, gs, dqt):
    rows = rows_of(i)
    qs[...] = stack_heads(q_ref[rows])
    gs[...] = stack_heads(grad)
    both = (grad.astype(f32) * o_ref[rows].astype(f32)).T
    delta = jnp.concatenate(
        [jnp.sum(both[HD * h : HD * h + HD], axis=0, keepdims=True) for h in range(HPD)], axis=1
    )
    lse = lse_ref[i]
    dqt[...] = jnp.zeros_like(dqt)

    def step(jj, _):
        j = i - jj
        keys = rows_of(j)
        s = mm(k_ref[keys], qs[...], NT)
        s = jnp.where(tile_heads(allowed_keys(i, j, start_ref)), s, NEG)
        p = jnp.exp(s - lse)
        dp = mm(v_ref[keys], gs[...], NT)
        ds = (p * (dp - delta)).astype(bf16)
        p = p.astype(bf16)
        dv[keys] += mm(p, gs[...])
        dk[keys] += mm(ds, qs[...])
        for h in range(HPD):
            dqt[HD * h : HD * h + HD] += mm(
                kt_ref[HD * h : HD * h + HD, keys], ds[:, QB * h : QB * h + QB]
            )
        return 0

    lax.fori_loop(0, jnp.minimum(i, BAND) + 1, step, 0)


def forward_kernel(q_ref, k_ref, v_ref, start_ref, o_ref, lse_ref, vt, qs, acc):
    blocks = q_ref.shape[0] // QB

    def turn(i, _):
        vt[:, rows_of(i)] = v_ref[rows_of(i)].T
        return 0

    lax.fori_loop(0, blocks, turn, 0)

    def block(i, _):
        attend_block(i, q_ref, k_ref, vt, start_ref, lse_ref, o_ref, qs, acc)
        return 0

    lax.fori_loop(0, blocks, block, 0)


def backward_kernel(
    q_ref, k_ref, v_ref, o_ref, g_ref, start_ref, lse_ref, d_ref, kt, qs, gs, dqt, dk, dv
):
    blocks = q_ref.shape[0] // QB

    def turn(i, _):
        kt[:, rows_of(i)] = k_ref[rows_of(i)].T
        return 0

    lax.fori_loop(0, blocks, turn, 0)
    dk[...] = jnp.zeros_like(dk)
    dv[...] = jnp.zeros_like(dv)

    def block(turn_of, _):
        i = blocks - 1 - turn_of
        rows = rows_of(i)
        attend_block_back(
            i, g_ref[rows], q_ref, k_ref, v_ref, kt, o_ref, start_ref, lse_ref, dk, dv, qs, gs, dqt
        )
        d_ref[0, rows] = (dqt[...].T * SCALE).astype(bf16)
        d_ref[1, rows] = dk[rows].astype(bf16)
        d_ref[2, rows] = dv[rows].astype(bf16)
        return 0

    lax.fori_loop(0, blocks, block, 0)


VMEM = pl.BlockSpec(memory_space=pltpu.VMEM)
LIMIT = pltpu.CompilerParams(vmem_limit_bytes=40 * 2**20)


def attend_forward(query, keys, values, starts):
    count = query.shape[0]
    return pl.pallas_call(
        forward_kernel,
        out_shape=(
            jax.ShapeDtypeStruct((count, WIDE), bf16),
            jax.ShapeDtypeStruct((count // QB, 1, HPD * QB), f32),
        ),
        in_specs=[VMEM] * 4,
        out_specs=(VMEM, VMEM),
        scratch_shapes=[
            pltpu.VMEM((WIDE, count), bf16),
            pltpu.VMEM((HPD * QB, WIDE), bf16),
            pltpu.VMEM((HD, HPD * QB), f32),
        ],
        compiler_params=LIMIT,
    )(query, keys, values, starts)


def attend_backward(query, keys, values, rows, grad, starts, lse):
    count = query.shape[0]
    return pl.pallas_call(
        backward_kernel,
        out_shape=jax.ShapeDtypeStruct((3, count, WIDE), bf16),
        in_specs=[VMEM] * 7,
        out_specs=VMEM,
        scratch_shapes=[
            pltpu.VMEM((WIDE, count), bf16),
            pltpu.VMEM((HPD * QB, WIDE), bf16),
            pltpu.VMEM((HPD * QB, WIDE), bf16),
            pltpu.VMEM((WIDE, QB), f32),
            pltpu.VMEM((count, WIDE), f32),
            pltpu.VMEM((count, WIDE), f32),
        ],
        compiler_params=LIMIT,
    )(query, keys, values, rows, grad, starts, lse)


def per_device(
    tokens,
    lengths,
    first_gain,
    first_shift,
    qkv_weight,
    qv_bias,
    proj_weight,
    proj_bias,
    second_gain,
    second_shift,
    fc_weight,
    fc_bias,
    out_weight,
    out_bias,
    out_grad,
):
    count = tokens.shape[0]
    starts = segment_starts(lengths[0], count)
    gain_one, shift_one, qkv_all, qv_all, proj_all, proj_bias_all = (
        lax.all_gather(first_gain, "dp", axis=0, tiled=True),
        lax.all_gather(first_shift, "dp", axis=0, tiled=True),
        lax.all_gather(qkv_weight, "dp", axis=1, tiled=True),
        lax.all_gather(qv_bias, "dp", axis=2, tiled=True),
        lax.all_gather(proj_weight, "dp", axis=1, tiled=True),
        lax.all_gather(proj_bias, "dp", axis=0, tiled=True),
    )
    gain_one_f = gain_one.astype(jnp.float32)
    xin = tokens.astype(jnp.float32)
    normed_one, inverse_one = norm_parts(xin)
    act_one = (normed_one * gain_one_f + shift_one.astype(jnp.float32)).astype(jnp.bfloat16)
    projected = jnp.einsum("td,cde->cte", act_one, qkv_all, preferred_element_type=jnp.float32)
    width = qkv_all.shape[2]
    wide = ((0, 0), (0, WIDE - width))
    query = jnp.pad(
        (projected[0] + qv_all[0, 0].astype(f32)).astype(bf16) * jnp.asarray(SCALE, bf16), wide
    )
    keys = jnp.pad(projected[1].astype(bf16), wide)
    values = jnp.pad((projected[2] + qv_all[1, 0].astype(f32)).astype(bf16), wide)
    wide_rows, lse = attend_forward(query, keys, values, starts)
    flat_rows = wide_rows[:, :width]
    gain_two, shift_two, fc_all, fc_bias_all, out_all, out_bias_all = (
        lax.all_gather(second_gain, "dp", axis=0, tiled=True),
        lax.all_gather(second_shift, "dp", axis=0, tiled=True),
        lax.all_gather(fc_weight, "dp", axis=0, tiled=True),
        lax.all_gather(fc_bias, "dp", axis=1, tiled=True),
        lax.all_gather(out_weight, "dp", axis=1, tiled=True),
        lax.all_gather(out_bias, "dp", axis=0, tiled=True),
    )
    gain_two_f = gain_two.astype(jnp.float32)
    shift_two_f = shift_two.astype(jnp.float32)
    branch_one = lax.psum(
        jnp.dot(flat_rows, proj_all, preferred_element_type=jnp.float32).astype(jnp.bfloat16), "mp"
    ).astype(jnp.float32)
    hidden_one = xin + branch_one + proj_bias_all.astype(jnp.float32)
    normed_two, inverse_two = norm_parts(hidden_one)
    act_two = (normed_two * gain_two_f + shift_two_f).astype(jnp.bfloat16)
    pre = jnp.dot(act_two, fc_all, preferred_element_type=jnp.float32) + fc_bias_all[0].astype(
        jnp.float32
    )
    fired = gelu_tanh(pre).astype(jnp.bfloat16)
    branch_two = lax.psum(
        jnp.dot(fired, out_all, preferred_element_type=jnp.float32).astype(jnp.bfloat16), "mp"
    ).astype(jnp.float32)
    output = (hidden_one + branch_two + out_bias_all.astype(jnp.float32)).astype(jnp.bfloat16)
    grad_out = out_grad.astype(jnp.float32)
    out_bias_grad = jnp.sum(out_grad, axis=0, dtype=jnp.float32)
    out_weight_grad = jnp.einsum("tf,td->fd", fired, out_grad, preferred_element_type=jnp.float32)
    fired_grad = jnp.einsum("td,fd->tf", out_grad, out_all, preferred_element_type=jnp.float32)
    pre_grad = (fired_grad * gelu_slope(pre)).astype(jnp.bfloat16)
    fc_bias_grad = jnp.sum(pre_grad, axis=0, dtype=jnp.float32)
    fc_weight_grad = jnp.einsum("td,tf->df", act_two, pre_grad, preferred_element_type=jnp.float32)
    act_two_grad = lax.psum(
        jnp.einsum("tf,df->td", pre_grad, fc_all, preferred_element_type=jnp.float32).astype(
            jnp.bfloat16
        ),
        "mp",
    ).astype(jnp.float32)
    gain_two_grad = jnp.sum(act_two_grad * normed_two, axis=0)
    shift_two_grad = jnp.sum(act_two_grad, axis=0)
    hidden_grad = grad_out + norm_back(act_two_grad, gain_two_f, normed_two, inverse_two)
    branch_grad = hidden_grad.astype(jnp.bfloat16)
    proj_bias_grad = jnp.sum(branch_grad, axis=0, dtype=jnp.float32)
    proj_weight_grad = jnp.einsum(
        "te,td->ed", flat_rows, branch_grad, preferred_element_type=jnp.float32
    )
    rows_grad = jnp.einsum(
        "td,ed->te", branch_grad, proj_all, preferred_element_type=jnp.float32
    ).astype(jnp.bfloat16)
    stacked = attend_backward(
        query, keys, values, wide_rows, jnp.pad(rows_grad, wide), starts, lse
    )[:, :, :width]
    qkv_grad = jnp.einsum("td,cte->cde", act_one, stacked, preferred_element_type=jnp.float32)
    bias_sums = jnp.sum(stacked, axis=1, dtype=jnp.float32)
    qv_grad = jnp.stack([bias_sums[0], bias_sums[2]])[:, None, :]
    act_one_grad = lax.psum(
        jnp.einsum("cte,cde->td", stacked, qkv_all, preferred_element_type=jnp.float32).astype(
            jnp.bfloat16
        ),
        "mp",
    ).astype(jnp.float32)
    gain_one_grad = jnp.sum(act_one_grad * normed_one, axis=0)
    shift_one_grad = jnp.sum(act_one_grad, axis=0)
    input_grad = (
        hidden_grad + norm_back(act_one_grad, gain_one_f, normed_one, inverse_one)
    ).astype(jnp.bfloat16)
    mlp_grads = (
        lax.psum_scatter(gain_two_grad, "dp", scatter_dimension=0, tiled=True),
        lax.psum_scatter(shift_two_grad, "dp", scatter_dimension=0, tiled=True),
        lax.psum_scatter(fc_weight_grad, "dp", scatter_dimension=0, tiled=True),
        lax.psum_scatter(fc_bias_grad[None], "dp", scatter_dimension=1, tiled=True),
        lax.psum_scatter(out_weight_grad, "dp", scatter_dimension=1, tiled=True),
        lax.psum_scatter(out_bias_grad, "dp", scatter_dimension=0, tiled=True),
    )
    attn_grads = (
        summed_on_arrival(gain_one_grad.astype(jnp.bfloat16), "dp", 0),
        summed_on_arrival(shift_one_grad.astype(jnp.bfloat16), "dp", 0),
        summed_on_arrival(qkv_grad.astype(jnp.bfloat16), "dp", 1),
        summed_on_arrival(qv_grad.astype(jnp.bfloat16), "dp", 2),
        summed_on_arrival(proj_weight_grad.astype(jnp.bfloat16), "dp", 1),
        summed_on_arrival(proj_bias_grad.astype(jnp.bfloat16), "dp", 0),
    )
    return (
        output,
        input_grad,
        attn_grads[0],
        attn_grads[1],
        attn_grads[2],
        attn_grads[3],
        attn_grads[4],
        attn_grads[5],
        mlp_grads[0],
        mlp_grads[1],
        mlp_grads[2],
        mlp_grads[3],
        mlp_grads[4],
        mlp_grads[5],
    )


MESH = pl.DeviceIdType.MESH
TB = 512
RB = 128


def norm(values):
    mean = jnp.mean(values, axis=-1, keepdims=True)
    centred = values - mean
    inverse = lax.rsqrt(jnp.mean(centred * centred, axis=-1, keepdims=True) + EPS)
    return centred * inverse, inverse


def remote(src, dst, send, recv, device):
    return pltpu.make_async_remote_copy(
        src_ref=src, dst_ref=dst, send_sem=send, recv_sem=recv, device_id=device, device_id_type=MESH
    )


def whole_kernel(
    tokens,
    grads,
    lengths,
    fc_own,
    out_own,
    pr_own,
    fb_own,
    qkv_own,
    gain_one,
    shift_one,
    gain_two,
    shift_two,
    proj_bias,
    out_bias,
    qv_own,
    output,
    grad_tokens,
    fc_grad,
    out_grad,
    qkv_grad,
    pr_grad,
    pg_out,
    w_fc,
    w_out,
    w_pr,
    starts,
    par_own,
    w_qkv,
    pars,
    par,
    fcb,
    qr,
    kr,
    vr,
    turned,
    orow,
    rows_all,
    lse,
    qs,
    gs,
    acc,
    dqt,
    dk,
    dv,
    gbuf,
    normed,
    inv,
    act,
    oacc,
    gacc,
    fired,
    preg,
    stacked,
    hid,
    dw,
    dwp,
    pgrad,
    pgbuf,
    zgbuf,
    part,
    edge,
    far,
    q_s,
    q_r,
    p_s,
    p_r,
    z_s,
    z_r,
    w_s,
    w_r,
    af_s,
    a_s,
    a_r,
    ar_s,
    ar_r,
    d_s,
    d_r,
    zg_s,
    zg_r,
    g_s,
    g_r,
    loc,
    free,
):
    d = lax.axis_index("dp")
    m = lax.axis_index("mp")
    y, x, k = d // 4, (d // 2) % 2, d % 2
    count = tokens.shape[0]
    blocks, subs = count // TB, count // QB

    def place(yy, xx, kk):
        return (yy * 4 + xx * 2 + kk, m)

    flat_fc = w_fc.reshape(4, 768, 768)
    flat_pr = w_pr.reshape(4, 768, 256)
    flat_out = w_out.reshape(4, 768, 768)
    flat_qkv = w_qkv.reshape(768, 3 * WIDE)
    x_dev, y_dev, diag, twin = (
        place(y, 1 - x, k),
        place(1 - y, x, k),
        place(1 - y, 1 - x, k),
        place(y, x, 1 - k),
    )
    plane = [(lax.rem(d + o, 8), m) for o in range(8)]
    line = [(d, lax.rem(m + o, 4)) for o in range(4)]
    above, below = (d, jnp.minimum(m + 1, 3)), (d, jnp.maximum(m - 1, 0))
    end = (m == 0) | (m == 3)
    inner = jnp.logical_not(end)
    order = [m] + [jnp.where(m <= o - 1, o, o - 1) for o in range(1, 4)]

    for c in range(3):
        w_qkv[y, x, k, :, WIDE * c : WIDE * c + WIDE] = jnp.concatenate(
            [qkv_own[c], jnp.zeros((96, WIDE - HPD * HD), bf16)], axis=1
        )
    par[...] = jnp.zeros_like(par)
    vectors = (gain_one, shift_one, gain_two, shift_two, proj_bias, out_bias, fb_own)
    for n, vector in enumerate(vectors):
        par[n : n + 1, 0:96] = vector[...].astype(f32)
    par[8:9, 0:24] = qv_own[0:1].astype(f32)
    par[8:9, 2 * WIDE : 2 * WIDE + 24] = qv_own[1:2].astype(f32)
    lined = pltpu.roll(par[0:8], 96 * d, 1)
    heads = pltpu.roll(par[8:16], 24 * d, 1)
    row = lax.broadcasted_iota(jnp.int32, (8, 768), 0)
    lined = jnp.where(row == 7, jnp.broadcast_to(heads[0:1], (8, 768)), lined)
    par_own[...] = jnp.concatenate([lined, jnp.zeros((8, 768), f32)], axis=0).astype(bf16)
    barrier = pltpu.get_barrier_semaphore()
    for device in plane[1:] + line[1:]:
        pl.semaphore_signal(barrier, inc=1, device_id=device, device_id_type=MESH)
    pl.semaphore_wait(barrier, 10)

    q_send = [
        remote(w_qkv.at[y, x, k], w_qkv.at[y, x, k], q_s.at[i], q_r.at[i], device)
        for i, device in enumerate((x_dev, y_dev, diag, twin))
    ]
    q_from = [(y, 1 - x, k), (1 - y, x, k), (1 - y, 1 - x, k)]
    q_pass = [
        remote(w_qkv.at[c], w_qkv.at[c], q_s.at[4 + i], q_r.at[4 + i], twin)
        for i, c in enumerate(q_from)
    ]
    for copy in q_send:
        copy.start()
    p_send = [remote(par_own, pars.at[o], p_s.at[o], p_r.at[o], plane[o]) for o in range(1, 8)]
    for copy in p_send:
        copy.start()
    w_fc[m, y, x, k] = fc_own[...]
    w_out[m, y, x, k] = out_own[...]
    tall = jnp.concatenate(
        [pr_own[...].astype(f32), fb_own[...].astype(f32), jnp.zeros((63, 96), f32)], axis=0
    )
    w_pr[m, y, x, k] = tall.T.astype(bf16)
    pars[0] = par_own[...]
    held = (w_fc, w_out, w_pr)

    def along(piece, send, recv, s):
        up = remote(piece, piece, send.at[0], recv, above)
        down = remote(piece, piece, send.at[1], recv, below)
        return ((s <= m) & (m < 3), up), ((s >= m) & (m > 0), down)

    def pass_on(piece, send, recv, s):
        for where, copy in along(piece, send, recv, s):
            pl.when(where)(copy.start)

    def passed_on(piece, send, recv, s):
        for where, copy in along(piece, send, recv, s):
            pl.when(where)(copy.wait_send)

    def z_args(c, s):
        return held[c].at[s, y, x, k], z_s.at[c, s], z_r.at[c, s], s

    def z_step(cs, far_by):
        for s, there in ((m - far_by, m >= far_by), (m + far_by, m + far_by <= 3)):

            @pl.when(there)
            def _():
                for c in cs:
                    piece, send, recv, _ = z_args(c, s)
                    remote(piece, piece, send.at[0], recv, above).wait_recv()
                    pass_on(*z_args(c, s))
                if 0 in cs:
                    spread(s, cs)

    for c in (2, 0, 1):
        pass_on(*z_args(c, m))

    def hop(s, c, stage):
        if stage == 0:
            part_of = held[c].at[s, y, x, k]
            device = y_dev if c == 1 else x_dev
        elif stage == 1:
            part_of = held[c].at[s, :, x, k] if c == 1 else held[c].at[s, y, :, k]
            device = x_dev if c == 1 else y_dev
        else:
            part_of = held[c].at[s, :, :, k]
            device = twin
        return remote(part_of, part_of, w_s.at[c, stage, s], w_r.at[c, stage, s], device)

    def spread(s, cs=(0, 1)):
        for c in cs:
            hop(s, c, 0).start()

    def advance(o, stage, cs=(0, 1)):
        for c in cs:
            hop(order[o], c, stage - 1).wait_recv()
            hop(order[o], c, stage).start()

    pltpu.make_async_copy(
        grads.at[rows_of(blocks - 1, TB)], gbuf.at[0], loc.at[0]
    ).start()

    for copy in p_send:
        copy.wait_recv()
    total = pars[0].astype(f32)
    for o in range(1, 8):
        total = total + pars[o].astype(f32)
    par[...] = total
    spot = lax.broadcasted_iota(jnp.int32, (1, count), 1)
    start = jnp.zeros((1, count), jnp.int32)
    finish = lengths[0, 0]
    for n in range(lengths.shape[1]):
        start = jnp.where(spot >= finish, finish, start)
        if n + 1 < lengths.shape[1]:
            finish = finish + lengths[0, n + 1]
    starts[...] = start
    dk[...] = jnp.zeros_like(dk)
    dv[...] = jnp.zeros_like(dv)
    dw[...] = jnp.zeros_like(dw)
    dwp[...] = jnp.zeros_like(dwp)
    pgrad[...] = jnp.zeros_like(pgrad)
    z_step((2,), 1)
    z_step((2,), 2)
    z_step((2,), 3)
    for i in range(3):
        q_send[i].wait_recv()
        q_pass[i].start()
    spread(m)
    for s in range(4):
        spread(s, (2,))
    z_step((0, 1), 1)
    q_send[3].wait_recv()
    for copy in q_pass:
        copy.wait_recv()

    def first_act(rows):
        unit, inverse = norm(tokens[rows].astype(f32))
        return (unit * par[0:1] + par[1:2]).astype(bf16)

    def project(b, _):
        rows = rows_of(b)
        r = mm(first_act(rows), flat_qkv[...]) + par[7:8]
        qr[rows] = r[:, :WIDE].astype(bf16) * jnp.asarray(SCALE, bf16)
        kr[rows] = r[:, WIDE : 2 * WIDE].astype(bf16)
        v = r[:, 2 * WIDE :].astype(bf16)
        vr[rows] = v
        turned[:, rows] = v.T

        @pl.when(b == 0)
        def _():
            advance(0, 1)

        @pl.when(b == 2)
        def _():
            for o in range(4):
                advance(o, 1, (2,))

        @pl.when(b == 4)
        def _():
            z_step((0, 1), 2)

        @pl.when(b == 6)
        def _():
            for o in range(4):
                advance(o, 2, (2,))

        return 0

    lax.fori_loop(0, subs, project, 0)

    def a_args(b, s):
        return rows_all.at[s, b], a_s.at[b, s], a_r.at[b, s], s

    def a_wait(b, s):
        piece, send, recv, _ = a_args(b, s)
        remote(piece, piece, send.at[0], recv, above).wait_recv()

    def a_step(b, far_by):
        for s, there in ((m - far_by, m >= far_by), (m + far_by, m + far_by <= 3)):

            @pl.when(there & inner)
            def _():
                a_wait(b, s)
                pass_on(*a_args(b, s))

    def direct(b, o):
        return remote(rows_all.at[m, b], rows_all.at[m, b], af_s.at[o], a_r.at[b, m], line[o])

    def attend(t, _):
        b = blocks - 1 - t
        attend_block(2 * b + 1, qr, kr, turned, starts, lse, orow, qs, acc)

        @pl.when(t == 0)
        def _():
            advance(0, 2)

        @pl.when(t == 1)
        def _():
            advance(1, 1)

        @pl.when(t == 2)
        def _():
            advance(3, 1)

        attend_block(2 * b, qr, kr, turned, starts, lse, orow, qs, acc)
        top, low = rows_of(2 * b), rows_of(2 * b + 1)
        rows_all[m, b, :QB] = orow[top, :128]
        rows_all[m, b, QB : 2 * QB] = orow[low, :128]
        rows_all[m, b, 2 * QB :] = (
            orow[top, 128:].astype(f32) + pltpu.roll(orow[low, 128:].astype(f32), 64, 1)
        ).astype(bf16)

        @pl.when(t == 0)
        def _():
            z_step((0, 1), 3)
            for o in range(1, 4):
                direct(blocks - 1, o).start()

        @pl.when(t > 0)
        def _():
            pass_on(*a_args(b, m))

        @pl.when(t == 1)
        def _():
            advance(2, 1)

        return 0

    lax.fori_loop(0, blocks, attend, 0)
    advance(1, 2)

    def turn(i, _):
        turned[:, rows_of(i)] = kr[rows_of(i)].T
        return 0

    lax.fori_loop(0, subs, turn, 0)
    for s in range(4):
        hop(s, 2, 2).wait_recv()

    def bias_row(s, _):
        fcb[s] = flat_pr[s, :, 128:256].astype(f32).T[64:65]
        return 0

    lax.fori_loop(0, 4, bias_row, 0)

    inward = (d, jnp.where(m < 2, 1, 2))
    across = (d, 3 - m)
    outward = (d, jnp.where(m < 2, 0, 3))

    def hop_a(i):
        return remote(part.at[i], edge.at[i], ar_s.at[0, i], ar_r.at[0, i], inward)

    def hop_b(i):
        return remote(part.at[i], far.at[i], ar_s.at[1, i], ar_r.at[1, i], across)

    def hop_c(i):
        return remote(edge.at[i], far.at[i], ar_s.at[2, i], ar_r.at[2, i], outward)

    def stage_two(i):
        @pl.when(inner)
        def _():
            hop_a(i).wait_recv()
            part[i] = (part[i].astype(f32) + edge[i].astype(f32)).astype(bf16)
            hop_b(i).start()

    def stage_three(i):
        @pl.when(inner)
        def _():
            hop_b(i).wait_recv()
            edge[i] = (part[i].astype(f32) + far[i].astype(f32)).astype(bf16)
            hop_c(i).start()

    def gt_out(i):
        return pltpu.make_async_copy(
            hid.at[rows_of(i, RB)], grad_tokens.at[rows_of(i, RB)], g_s.at[8 + i]
        )

    def stage_four(i):
        @pl.when(end)
        def _():
            hop_c(i).wait_recv()
            edge[i] = far[i]

        there = rows_of(i, RB)
        grad = edge[i].astype(f32)
        unit, inverse = norm(tokens[there].astype(f32))
        back = norm_back(grad, par[0:1], unit, inverse)
        hid[there] = (hid[there].astype(f32) + back).astype(bf16)
        gt_out(i).start()

    def out_copy(b, slot):
        return pltpu.make_async_copy(gbuf.at[slot], output.at[rows_of(b, TB)], loc.at[2])

    def out_half(i):
        return pltpu.make_async_copy(
            gbuf.at[(blocks - 1) % 2, rows_of(i)], output.at[rows_of(i)], loc.at[5 + i]
        )

    groups = ((0, 1), (2,), (3,))
    spans = (768, 768, 768, 256)
    wants = [(y, 1 - x, x_dev), (1 - y, x, y_dev), (1 - y, 1 - x, diag)]

    def take(c, dest):
        some = pl.ds(pl.multiple_of(dest * 96, 96), 96)
        return dw[c, some] if c < 3 else dwp[some]

    def span_of(ref, g, *rest):
        if g == 0:
            return ref.at[(slice(0, 2),) + rest]
        return ref.at[(g + 1,) + rest + ((slice(None), slice(0, 256)) if g == 2 else ())]

    def twin_sum(g):
        every = (slice(None), slice(None))
        return remote(
            span_of(w_out, g, *every, 1 - k), span_of(w_fc, g, *every, 0), d_s.at[g], d_r.at[g], twin
        )

    def to_owner(g, i):
        yy, xx, device = wants[i]
        n = 3 + 3 * i + g
        return remote(
            span_of(w_out, g, yy, xx, k),
            span_of(w_fc, g, i // 2, i % 2, 1),
            d_s.at[n],
            d_r.at[n],
            device,
        )

    def give_twin(g):
        for yy in range(2):
            for xx in range(2):
                for c in groups[g]:
                    w_out[c, yy, xx, 1 - k, :, : spans[c]] = take(
                        c, yy * 4 + xx * 2 + 1 - k
                    ).astype(bf16)

    def give_owners(g):
        twin_sum(g).wait_recv()
        for i, (yy, xx, _) in enumerate(wants):
            for c in groups[g]:
                w_out[c, yy, xx, k, :, : spans[c]] = (
                    take(c, yy * 4 + xx * 2 + k) + w_fc[c, yy, xx, 0, :, : spans[c]].astype(f32)
                ).astype(bf16)
            to_owner(g, i).start()

    own_rows = pl.ds(pl.multiple_of(d * 96, 96), 96)
    fc_result = pltpu.make_async_copy(dw.at[0, own_rows], fc_grad, loc.at[7])

    def own_sum(g):
        for i in range(3):
            to_owner(g, i).wait_recv()
        for c in groups[g]:
            value = take(c, d) + w_fc[c, y, x, 0, :, : spans[c]].astype(f32)
            for i in range(3):
                value = value + w_fc[c, i // 2, i % 2, 1, :, : spans[c]].astype(f32)
            if c == 0:
                dw[0, own_rows] = value
                fc_result.start()
            elif c == 1:
                out_grad[...] = value
            elif c == 2:
                for n in range(3):
                    qkv_grad[n] = value[:, WIDE * n : WIDE * n + HPD * HD]
            else:
                pr_grad[...] = value.T[: HPD * HD]

    def make_block(size):
        big = size == TB
        all_rows = slice(0, size)

        def block(t, _):
            b = blocks - 1 - t if big else 0
            i_last = 2 * b + 1 if big else 1 - t
            row = b * TB if big else (1 - t) * QB
            off = 0 if big else (1 - t) * QB
            rows = pl.ds(pl.multiple_of(row, QB), size)
            slot = lax.rem(t, 2) if big else (blocks - 1) % 2
            g_rows = pl.ds(pl.multiple_of(off, QB), size)

            def part_of(r, step):
                return pl.ds(pl.multiple_of(off + r * step, step), step)

            @pl.when((t >= 0) if big else (t == 0))
            def _():
                pltpu.make_async_copy(
                    grads.at[rows_of(b, TB)], gbuf.at[slot], loc.at[slot]
                ).wait()

            if big:

                @pl.when(t >= 1)
                def _():
                    out_copy(b + 1, 1 - slot).wait()

                pltpu.make_async_copy(
                    grads.at[rows_of(b - 1, TB)], gbuf.at[1 - slot], loc.at[1 - slot]
                ).start()

            for s in range(4):

                @pl.when((end | (b == blocks - 1)) & (m != s) & ((t >= 0) if big else (t == 0)))
                def _():
                    a_wait(b, s)

            def head(s):
                third = rows_all[s, b, 2 * QB :].astype(f32)
                turned_third = pltpu.roll(third, 64, 1)
                if big:
                    third = jnp.concatenate([third, turned_third], axis=0)
                else:
                    third = jnp.where(t == 0, turned_third, third)
                lane = lax.broadcasted_iota(jnp.int32, third.shape, 1)
                third = jnp.where(lane < 64, third, 0.0).astype(bf16)
                left = jnp.concatenate([rows_all[s, b, g_rows], third], axis=1)
                return mm(left, flat_pr[s], NT)

            oacc[all_rows] = (
                tokens[rows].astype(f32) + par[4:5] + (head(0) + head(1) + head(2) + head(3))
            )

            def second(r, _):
                some = rows_of(r, RB)
                hidden = oacc[some]
                unit, inverse = norm(hidden)
                normed[some] = unit
                inv[some] = inverse
                act[some] = (unit * par[2:3] + par[3:4]).astype(bf16)
                oacc[some] = hidden + par[5:6]
                gacc[some] = jnp.zeros_like(hidden)
                return 0

            lax.fori_loop(0, size // RB, second, 0)

            def slab(s, _):
                if big:

                    @pl.when(t == 0)
                    def _():
                        for c in range(2):
                            hop(s, c, 2).wait_recv()

                def units(r, _):
                    some = rows_of(r)
                    pre = mm(act[some], flat_fc[s]) + fcb[s]
                    back = mm(gbuf[slot, part_of(r, QB)], flat_out[s])
                    square = pre * pre
                    tangent = jnp.tanh(pre * (GELU_C + (GELU_C * 0.044715) * square))
                    half = 0.5 * pre
                    fired[some] = (half + half * tangent).astype(bf16)
                    slope = (0.5 + 0.5 * tangent) + half * (1.0 - tangent * tangent) * (
                        GELU_C + (3.0 * GELU_C * 0.044715) * square
                    )
                    preg[some] = (back * slope).astype(bf16)
                    return 0

                lax.fori_loop(0, size // QB, units, 0, unroll=True)
                oacc[all_rows] += mm(fired[all_rows], flat_out[s], NT)
                gacc[all_rows] += mm(preg[all_rows], flat_fc[s], NT)

                @pl.when(s == m)
                def _():
                    def outer(r, _):
                        some = rows_of(r)
                        dw[0, some] += mm(act[all_rows, some], preg[all_rows], TN)
                        dw[1, some] += mm(gbuf[slot, g_rows, some], fired[all_rows], TN)
                        return 0

                    lax.fori_loop(0, 3, outer, 0)
                    pgrad[6:7] += jnp.sum(preg[all_rows].astype(f32), axis=0, keepdims=True)

                def at(when, do, *what):
                    @pl.when(when)
                    def _():
                        for item in what:
                            do(item)

                if big:

                    @pl.when((t == 0) & (s == 0))
                    def _():
                        advance(2, 2)

                    @pl.when((t == 0) & (s == jnp.where(m == 3, 1, 2)))
                    def _():
                        advance(3, 2)

                    @pl.when((t == 0) & (s == 2))
                    def _():
                        a_step(2, 1)
                        a_step(1, 1)

                    j = 4 * b + 4
                    at((t >= 1) & (s == 0), stage_two, j + 3, j + 2)
                    at((t >= 1) & (s == 2), stage_two, j + 1, j)
                    at((t >= 1) & (s == 3), stage_three, j + 3, j + 2)
                    at((t >= 2) & (s == 1), stage_four, j + 7, j + 6, j + 5, j + 4)
                else:
                    at((t == 0) & (s == 1), stage_two, 7, 6)
                    at((t == 0) & (s == 3), stage_two, 5)
                    at((t == 0) & (s == 2), stage_four, 11, 10, 9, 8)
                    at((t == 1) & (s == 1), stage_three, 5)
                    at((t == 1) & (s == 3), stage_three, 4)
                return 0

            lax.fori_loop(0, 4, slab, 0)
            if big:

                @pl.when(t == 0)
                def _():
                    a_step(2, 2)
                    a_step(0, 1)

            else:

                @pl.when(t == 1)
                def _():
                    for c in range(3):
                        for s in range(4):
                            passed_on(*z_args(c, s))
                            for stage in range(3):
                                hop(s, c, stage).wait_send()
                    for device in (x_dev, y_dev, diag, twin):
                        pl.semaphore_signal(free, inc=1, device_id=device, device_id_type=MESH)
                    give_twin(0)
                    pl.semaphore_wait(free, 4)
                    twin_sum(0).start()

            def rejoin(r, _):
                some = rows_of(r, RB)
                there = pl.ds(pl.multiple_of(row + r * RB, RB), RB)
                grad = gbuf[slot, part_of(r, RB)].astype(f32)
                through, unit = gacc[some], normed[some]
                pgrad[5:6] += jnp.sum(grad, axis=0, keepdims=True)
                pgrad[2:3] += jnp.sum(through * unit, axis=0, keepdims=True)
                pgrad[3:4] += jnp.sum(through, axis=0, keepdims=True)
                branch = (grad + norm_back(through, par[2:3], unit, inv[some])).astype(bf16)
                hid[there] = branch
                pgrad[4:5] += jnp.sum(branch.astype(f32), axis=0, keepdims=True)
                gbuf[slot, part_of(r, RB)] = oacc[some].astype(bf16)
                return 0

            lax.fori_loop(0, size // RB, rejoin, 0)
            if big:
                out_copy(b, slot).start()
            else:
                out_half(1 - t).start()
            dwp[...] += mm(hid[rows], orow[rows], TN)
            if not big:

                @pl.when(t == 1)
                def _():
                    give_twin(2)
                    twin_sum(2).start()
                    give_owners(0)

            stacked[all_rows, :WIDE] = mm(hid[rows], flat_pr[m]).astype(bf16)

            for n in range(size // QB):
                i = i_last - n
                some = slice(size - QB * (n + 1), size - QB * n)
                attend_block_back(
                    i, stacked[some, :WIDE], qr, kr, vr, turned, orow, starts, lse, dk, dv, qs, gs, dqt
                )
                stacked[some, :WIDE] = (dqt[...].T * SCALE).astype(bf16)
                stacked[some, WIDE : 2 * WIDE] = dk[rows_of(i)].astype(bf16)
                stacked[some, 2 * WIDE :] = dv[rows_of(i)].astype(bf16)
                whole = mm(stacked[some], flat_qkv[...], NT).astype(bf16)
                part[2 * i] = whole[:RB]
                part[2 * i + 1] = whole[RB:]

                @pl.when(end)
                def _():
                    hop_a(2 * i + 1).start()
                    hop_a(2 * i).start()

                if big and n == 0:

                    @pl.when(t >= 1)
                    def _():
                        stage_three(4 * b + 5)
                        stage_three(4 * b + 4)

                if not big:

                    @pl.when(t == 0)
                    def _():
                        stage_two(4)
                        stage_three(7)
                        stage_three(6)

                    @pl.when(t == 1)
                    def _():
                        stage_two(3)
                        stage_two(2)

            pgrad[7:8] += jnp.sum(stacked[all_rows].astype(f32), axis=0, keepdims=True)

            def again(r, _):
                unit, _ = norm(tokens[pl.ds(pl.multiple_of(row + r * RB, RB), RB)].astype(f32))
                act[rows_of(r, RB)] = (unit * par[0:1] + par[1:2]).astype(bf16)
                grad = part[row // RB + r].astype(f32)
                pgrad[0:1] += jnp.sum(grad * unit, axis=0, keepdims=True)
                pgrad[1:2] += jnp.sum(grad, axis=0, keepdims=True)
                return 0

            lax.fori_loop(0, size // RB, again, 0)

            def outer(r, _):
                some = rows_of(r)
                dw[2, some] += mm(act[all_rows, some], stacked[all_rows], TN)
                return 0

            lax.fori_loop(0, 3, outer, 0)
            if big:

                @pl.when(t == 0)
                def _():
                    a_step(1, 2)

                @pl.when(t == 1)
                def _():
                    a_step(0, 2)

            return 0

        return block

    lax.fori_loop(0, blocks - 1, make_block(TB), 0)
    lax.fori_loop(0, 2, make_block(QB), 0)

    zg_send = [
        remote(zgbuf.at[m], zgbuf.at[m], zg_s.at[o], zg_r.at[m], line[o]) for o in range(1, 4)
    ]
    zgbuf[m] = pgrad[...]
    for copy in zg_send:
        copy.start()
    give_twin(1)
    twin_sum(1).start()
    stage_three(3)
    stage_three(2)
    for s in range(4):

        @pl.when(m != s)
        def _():
            remote(zgbuf.at[s], zgbuf.at[s], zg_s.at[1], zg_r.at[s], line[1]).wait_recv()

    pgrad[0:2] = zgbuf[0, 0:2] + zgbuf[1, 0:2] + zgbuf[2, 0:2] + zgbuf[3, 0:2]
    g_send = [
        remote(pgrad, pgbuf.at[o], g_s.at[o], g_r.at[o], plane[o]) for o in range(1, 8)
    ]
    for copy in g_send:
        copy.start()
    give_owners(2)
    give_owners(1)
    for i in (7, 6, 5, 4):
        stage_four(i)
    stage_two(1)
    stage_two(0)
    total = pgrad[...]
    for copy in g_send:
        copy.wait_recv()
    for o in range(1, 8):
        total = total + pgbuf[o]
    pg_out[0:8] = pltpu.roll(total, lax.rem(768 - 96 * d, 768), 1)[:, :128]
    heads = pltpu.roll(total, lax.rem(768 - 24 * d, 768), 1)
    pg_out[8:16] = heads[:, :128]
    pg_out[16:24] = heads[:, 2 * WIDE : 2 * WIDE + 128]
    stage_three(1)
    stage_three(0)
    stage_four(3)
    stage_four(2)
    own_sum(0)
    own_sum(2)
    own_sum(1)
    stage_four(1)
    stage_four(0)

    fc_result.wait()
    for copy in g_send + zg_send + q_send + q_pass + p_send:
        copy.wait_send()
    for g in range(3):
        twin_sum(g).wait_send()
        for i in range(3):
            to_owner(g, i).wait_send()
    out_copy(1, (blocks - 2) % 2).wait()
    out_half(1).wait()
    out_half(0).wait()

    def leave(i, _):
        gt_out(i).wait()

        @pl.when(end)
        def _():
            hop_a(i).wait_send()

        @pl.when(inner)
        def _():
            hop_b(i).wait_send()
            hop_c(i).wait_send()

        return 0

    lax.fori_loop(0, count // RB, leave, 0)
    for o in range(1, 4):
        direct(blocks - 1, o).wait_send()
    for b in range(blocks - 1):
        for s in range(4):
            passed_on(*a_args(b, s))


def whole_block(tokens, out_grad, lengths, *shards):
    count = tokens.shape[0]
    blocks, subs = count // TB, count // QB
    any_space = pl.BlockSpec(memory_space=pl.ANY)
    dma = pltpu.SemaphoreType.DMA
    return pl.pallas_call(
        whole_kernel,
        out_shape=(
            jax.ShapeDtypeStruct((count, 768), bf16),
            jax.ShapeDtypeStruct((count, 768), bf16),
            jax.ShapeDtypeStruct((96, 768), f32),
            jax.ShapeDtypeStruct((96, 768), f32),
            jax.ShapeDtypeStruct((3, 96, HPD * HD), f32),
            jax.ShapeDtypeStruct((HPD * HD, 96), f32),
            jax.ShapeDtypeStruct((24, 128), f32),
        ),
        in_specs=[VMEM, any_space, pl.BlockSpec(memory_space=pltpu.SMEM)] + [VMEM] * len(shards),
        out_specs=(any_space, any_space, any_space, VMEM, VMEM, VMEM, VMEM),
        scratch_shapes=[
            pltpu.VMEM((4, 2, 2, 2, 96, 768), bf16),
            pltpu.VMEM((4, 2, 2, 2, 96, 768), bf16),
            pltpu.VMEM((4, 2, 2, 2, 96, 256), bf16),
            pltpu.VMEM((1, count), jnp.int32),
            pltpu.VMEM((16, 768), bf16),
            pltpu.VMEM((2, 2, 2, 96, 768), bf16),
            pltpu.VMEM((8, 16, 768), bf16),
            pltpu.VMEM((16, 768), f32),
            pltpu.VMEM((4, 1, 768), f32),
            pltpu.VMEM((count, WIDE), bf16),
            pltpu.VMEM((count, WIDE), bf16),
            pltpu.VMEM((count, WIDE), bf16),
            pltpu.VMEM((WIDE, count), bf16),
            pltpu.VMEM((count, WIDE), bf16),
            pltpu.VMEM((4, blocks, 3 * QB, 128), bf16),
            pltpu.VMEM((subs, 1, HPD * QB), f32),
            pltpu.VMEM((HPD * QB, WIDE), bf16),
            pltpu.VMEM((HPD * QB, WIDE), bf16),
            pltpu.VMEM((HD, HPD * QB), f32),
            pltpu.VMEM((WIDE, QB), f32),
            pltpu.VMEM((count, WIDE), f32),
            pltpu.VMEM((count, WIDE), f32),
            pltpu.VMEM((2, TB, 768), bf16),
            pltpu.VMEM((TB, 768), f32),
            pltpu.VMEM((TB, 1), f32),
            pltpu.VMEM((TB, 768), bf16),
            pltpu.VMEM((TB, 768), f32),
            pltpu.VMEM((TB, 768), f32),
            pltpu.VMEM((TB, 768), bf16),
            pltpu.VMEM((TB, 768), bf16),
            pltpu.VMEM((TB, 768), bf16),
            pltpu.VMEM((count, 768), bf16),
            pltpu.VMEM((3, 768, 768), f32),
            pltpu.VMEM((768, 256), f32),
            pltpu.VMEM((8, 768), f32),
            pltpu.VMEM((8, 8, 768), f32),
            pltpu.VMEM((4, 8, 768), f32),
            pltpu.VMEM((count // RB, RB, 768), bf16),
            pltpu.VMEM((count // RB, RB, 768), bf16),
            pltpu.VMEM((count // RB, RB, 768), bf16),
            dma((7,)),
            dma((7,)),
            dma((8,)),
            dma((8,)),
            dma((3, 4, 2)),
            dma((3, 4)),
            dma((3, 3, 4)),
            dma((3, 3, 4)),
            dma((4,)),
            dma((blocks, 4, 2)),
            dma((blocks, 4)),
            dma((3, count // RB)),
            dma((3, count // RB)),
            dma((12,)),
            dma((12,)),
            dma((4,)),
            dma((4,)),
            dma((8 + count // RB,)),
            dma((8,)),
            dma((11,)),
            pltpu.SemaphoreType.REGULAR,
        ],
        compiler_params=pltpu.CompilerParams(
            collective_id=0, has_side_effects=True, vmem_limit_bytes=63 * 2**20 + 2**18
        ),
    )(tokens, out_grad, lengths, *shards)


def per_device_whole(
    tokens,
    lengths,
    first_gain,
    first_shift,
    qkv_weight,
    qv_bias,
    proj_weight,
    proj_bias,
    second_gain,
    second_shift,
    fc_weight,
    fc_bias,
    out_weight,
    out_bias,
    out_grad,
):
    output, grad_tokens, fc_grad, out_w_grad, qkv_grad, proj_grad, pg = whole_block(
        tokens,
        out_grad,
        lengths,
        fc_weight,
        out_weight.T,
        proj_weight,
        fc_bias,
        qkv_weight,
        first_gain[None],
        first_shift[None],
        second_gain[None],
        second_shift[None],
        proj_bias[None],
        out_bias[None],
        qv_bias[:, 0],
    )
    vec = pg[:7, :96]
    qv = jnp.concatenate([pg[15:16, :24], pg[23:24, :24]])[:, None, :]
    return (
        output,
        grad_tokens,
        vec[0],
        vec[1],
        qkv_grad,
        qv,
        proj_grad,
        vec[4],
        vec[2],
        vec[3],
        fc_grad,
        vec[6][None],
        out_w_grad.T,
        vec[5],
    )


def solution(mesh):
    placed = (
        P("dp", None),
        P("dp", None),
        P("dp"),
        P("dp"),
        P(None, "dp", "mp"),
        P(None, "mp", "dp"),
        P("mp", "dp"),
        P("dp"),
        P("dp"),
        P("dp"),
        P("dp", "mp"),
        P("mp", "dp"),
        P("mp", "dp"),
        P("dp"),
        P("dp", None),
    )
    return jax.shard_map(
        per_device_whole if dict(mesh.shape) == {"dp": 8, "mp": 4} else per_device,
        mesh=mesh,
        in_specs=placed,
        out_specs=(
            P("dp", None),
            P("dp", None),
            P("dp"),
            P("dp"),
            P(None, "dp", "mp"),
            P(None, "mp", "dp"),
            P("mp", "dp"),
            P("dp"),
            P("dp"),
            P("dp"),
            P("dp", "mp"),
            P("mp", "dp"),
            P("mp", "dp"),
            P("dp"),
        ),
        check_vma=False,
    )
```
